32 devices in a mesh: ctx: 8 (over z, x), ch: 4 (over y, core).
Axes of the slice: x: 2, y: 2, z: 4, core: 2. Of those that a mesh axis runs over, the one named last changes fastest.
Arguments:
- inputs: bfloat16 [1536, 16384], P('ch', 'ctx'), may hold values from -6 to 6
- conv_weight: bfloat16 [3, 1536, 96], replicated, may hold values from -0.375 to 0.375
- pw_weight: bfloat16 [1536, 1536], replicated, may hold values from -0.15625 to 0.15625
- cotangent: bfloat16 [1536, 16384], P(None, ('ctx', 'ch')), may hold values from -6 to 6
Outputs:
- mixed: bfloat16 [1536, 16384], P(None, ('ctx', 'ch'))
- grad_inputs: bfloat16 [1536, 16384], P('ch', 'ctx')
The draws below stay inside these ranges and needn't reach their ends.
All inputs are finite; a program needn't handle non-finite values.
Results may differ from the reference program's by a relative error of at most 0.012.
Values may be sent and summed in bfloat16 or wider, within the bound.
No kernel may reach another device: no remote copies, remote signals or barrier semaphores. Data moves between devices by JAX's collectives and lax.ppermute only.
A program may use at most 64 MiB of HBM per device.

```python
import jax
import jax.numpy as jnp
from jax import lax

CHANNELS = 1536
GROUP = 96
DILATION_STEP = 512
POSITIONS_EACH = 2048
SEQ = 16384
N_CTX = 8


def block_levels(rng, extent, shards, least, top_value):
    gain, own = 1.0, jax.random.fold_in(rng, 6)
    for axis_at, blocks in shards:
        heights = jnp.exp(jax.random.uniform(jax.random.fold_in(own, axis_at), (blocks,), jnp.float32, least / len(shards), top_value / len(shards)))
        gain = gain * jnp.repeat(heights, extent[axis_at] // blocks).reshape([-1 if axis == axis_at else 1 for axis in range(len(extent))])
    return gain


def normal_values(rng, shape, scale, bound, shards=(), held_as=jnp.bfloat16):
    values = jax.random.normal(rng, shape, jnp.float32) * scale
    if len(shards) > 0:
        values = block_levels(rng, shape, shards, -0.22, 0.18) * values
    return jnp.clip(values, min=-bound, max=bound).astype(held_as)


def setup_inputs(seed: int = 0) -> dict:
    seeds = jax.random.split(jax.random.key(seed), 5)
    inputs = normal_values(seeds[0], (CHANNELS, SEQ), 1.0, 6.0, ((0, 4), (1, 8)))
    conv_weight = normal_values(seeds[1], (3, CHANNELS, GROUP), (3 * GROUP) ** -0.5, 0.375)
    pw_weight = normal_values(seeds[2], (CHANNELS, CHANNELS), CHANNELS ** -0.5, 0.15625)
    cotangent = normal_values(seeds[3], (CHANNELS, SEQ), 1.0, 6.0, ((1, 32),))
    return {"inputs": inputs, "conv_weight": conv_weight, "pw_weight": pw_weight, "cotangent": cotangent}


def gelu_slope(values):
    return jax.vjp(jax.nn.gelu, values)[1](jnp.ones_like(values))[0]

def group_conv(kernel_taps, conv_weight):
    channels, length = kernel_taps[0].shape
    width = conv_weight.shape[2]
    groups = channels // width
    total = jnp.zeros((groups, width, length), jnp.float32)
    for position_offset in range(3):
        kernel = conv_weight[position_offset].reshape(groups, width, width).astype(jnp.float32)
        signal = kernel_taps[position_offset].reshape(groups, width, length).astype(jnp.float32)
        total = total + jnp.einsum('gji,gip->gjp', kernel, signal)
    return total.reshape(channels, length)

def group_conv_back(kernel_taps, conv_weight):
    channels, length = kernel_taps[0].shape
    width = conv_weight.shape[2]
    groups = channels // width
    total = jnp.zeros((groups, width, length), jnp.float32)
    for position_offset in range(3):
        kernel = conv_weight[position_offset].reshape(groups, width, width).astype(jnp.float32)
        signal = kernel_taps[position_offset].reshape(groups, width, length).astype(jnp.float32)
        total = total + jnp.einsum('gji,gjp->gip', kernel, signal)
    return total.reshape(channels, length)

def joined_edges(stack):
    return jnp.moveaxis(stack, 0, 1).reshape(stack.shape[1], stack.shape[0] * stack.shape[2])

def reference(inputs, conv_weight, pw_weight, cotangent):
    widened_input = jnp.pad(inputs, ((0, 0), (DILATION_STEP, DILATION_STEP)))
    blocks = jnp.arange(N_CTX, dtype=jnp.int32)

    def forward_block(block):
        first_position = (block * POSITIONS_EACH).astype(jnp.int32)
        sliding_window = lax.dynamic_slice_in_dim(widened_input, first_position, POSITIONS_EACH + 2 * DILATION_STEP, 1)
        kernel_taps = [sliding_window[:, position_offset * DILATION_STEP:position_offset * DILATION_STEP + POSITIONS_EACH] for position_offset in range(3)]
        conv_out = group_conv(kernel_taps, conv_weight)
        active = jax.nn.gelu(conv_out).astype(jnp.bfloat16)
        mixed = jnp.dot(pw_weight, active, preferred_element_type=jnp.float32).astype(jnp.bfloat16)
        upstream = lax.dynamic_slice_in_dim(cotangent, first_position, POSITIONS_EACH, 1)
        grad_active = lax.dot_general(pw_weight, upstream, (((0,), (0,)), ((), ())), preferred_element_type=jnp.float32).astype(jnp.bfloat16)
        convolved_gradient = (grad_active.astype(jnp.float32) * gelu_slope(conv_out)).astype(jnp.bfloat16)
        return (mixed, convolved_gradient)
    mixed, convolved_gradient = lax.map(forward_block, blocks)
    mixed = joined_edges(mixed)
    gradient_widened = jnp.pad(joined_edges(convolved_gradient), ((0, 0), (DILATION_STEP, DILATION_STEP)))

    def backward_block(block):
        first_position = (block * POSITIONS_EACH).astype(jnp.int32)
        sliding_window = lax.dynamic_slice_in_dim(gradient_widened, first_position, POSITIONS_EACH + 2 * DILATION_STEP, 1)
        kernel_taps = [sliding_window[:, (2 - position_offset) * DILATION_STEP:(2 - position_offset) * DILATION_STEP + POSITIONS_EACH] for position_offset in range(3)]
        return group_conv_back(kernel_taps, conv_weight).astype(jnp.bfloat16)
    grad_inputs = joined_edges(lax.map(backward_block, blocks))
    return (mixed, grad_inputs)
```

```python
import functools

import jax
import jax.numpy as jnp
from jax import lax
from jax.experimental import pallas as pl
from jax.experimental.pallas import tpu as pltpu
from jax.sharding import PartitionSpec as P

DILATION_STEP = 512
VMEM = pltpu.VMEM
MIB = 1 << 20


def params(mib):
    return pltpu.CompilerParams(vmem_limit_bytes=mib * MIB)


def gelu_and_slope(v):
    square = v * v
    inner = v * (0.7978845608 + (0.7978845608 * 0.044715) * square)
    th = jnp.tanh(inner)
    half = 0.5 + 0.5 * th
    active = v * half
    inner_slope = 0.7978845608 + (3.0 * 0.7978845608 * 0.044715) * square
    slope = half + (0.5 * v) * (1.0 - th * th) * inner_slope
    return active, slope


def full(shape):
    return pl.BlockSpec(memory_space=VMEM)


def upstream_kernel(order, ch_ref, pw_ref, cot_ref, *piece_refs):
    step = pl.program_id(0)
    result = lax.dot_general(
        pw_ref[...], cot_ref[...], (((0,), (0,)), ((), ())), preferred_element_type=jnp.float32
    ).astype(jnp.bfloat16)
    for place in range(len(order)):
        @pl.when(step == place)
        def _(place=place):
            piece_refs[place][...] = result


def upstream(ch, pw_weight, cotangent, chunk, width, channels, order):
    total = pw_weight.shape[0]
    if channels % 128 != 0 or width % 128 != 0:
        whole = lax.dot_general(
            pw_weight, cotangent[:, chunk * width:(chunk + 1) * width], (((0,), (0,)), ((), ())),
            preferred_element_type=jnp.float32,
        ).astype(jnp.bfloat16)
        return [lax.dynamic_slice_in_dim(whole, (ch[0] ^ k) * channels, channels, 0) for k in order]

    def pw_index(step, ch_ref):
        k = order[0]
        for place in range(1, len(order)):
            k = jnp.where(step == place, order[place], k)
        return 0, ch_ref[0] ^ k

    return pl.pallas_call(
        functools.partial(upstream_kernel, order),
        grid_spec=pltpu.PrefetchScalarGridSpec(
            num_scalar_prefetch=1,
            grid=(len(order),),
            in_specs=[
                pl.BlockSpec((total, channels), pw_index),
                pl.BlockSpec((total, width), lambda step, ch_ref: (0, chunk)),
            ],
            out_specs=[pl.BlockSpec((channels, width), lambda step, ch_ref: (0, 0))] * len(order),
        ),
        out_shape=[jax.ShapeDtypeStruct((channels, width), jnp.bfloat16)] * len(order),
        compiler_params=params(24),
        name="upstream",
    )(ch, pw_weight, cotangent)


def forward_kernel(chunk, n, halo, group, ch_ref, x_ref, left_ref, right_ref, w_ref, *rest):
    active_refs, slope_ref, wide = rest[:n], rest[n], rest[n + 1]
    channels, width = active_refs[0].shape
    block = x_ref.shape[1] // n
    wide[:, :halo * width] = left_ref[...]
    for b in range(n):
        start = b * block + chunk * width
        wide[:, (halo + b) * width:(halo + b + 1) * width] = x_ref[:, start:start + width]
    wide[:, (halo + n) * width:] = right_ref[...]
    for k in range(n):
        b = ch_ref[0] ^ k
        for g in range(channels // group):
            rows = slice(g * group, (g + 1) * group)
            taps = [
                wide[rows, pl.ds(pl.multiple_of((b + t * halo) * width, width), width)]
                for t in range(3)
            ]
            conv_out = jnp.dot(
                w_ref[rows, :], jnp.concatenate(taps, axis=0), preferred_element_type=jnp.float32
            )
            active, slope = gelu_and_slope(conv_out)
            active_refs[k][rows, :] = active.astype(jnp.bfloat16)
            slope_ref[k, rows, :] = slope


def forward(ch, inputs, left, right, weight, chunk, n, halo, width, group):
    channels = inputs.shape[0]
    outs = pl.pallas_call(
        functools.partial(forward_kernel, chunk, n, halo, group),
        in_specs=[pl.BlockSpec(memory_space=pltpu.SMEM)] + [pl.BlockSpec(memory_space=VMEM)] * 4,
        out_specs=[pl.BlockSpec(memory_space=VMEM)] * (n + 1),
        out_shape=[jax.ShapeDtypeStruct((channels, width), jnp.bfloat16)] * n
        + [jax.ShapeDtypeStruct((n, channels, width), jnp.float32)],
        scratch_shapes=[VMEM((channels, (n + 2 * halo) * width), jnp.bfloat16)],
        compiler_params=params(24),
        name="forward",
    )(ch, inputs, left, right, weight)
    return outs[:n], outs[n]


def slope_kernel(n, halo, ch_ref, slope_ref, *rest):
    piece_refs, (grad_ref, first_ref, last_ref) = rest[:n], rest[n:]
    width = piece_refs[0].shape[1]
    for k in range(n):
        b = ch_ref[0] ^ k
        product = (piece_refs[k][...].astype(jnp.float32) * slope_ref[k]).astype(jnp.bfloat16)
        grad_ref[:, pl.ds(pl.multiple_of(b * width, width), width)] = product
    first_ref[...] = grad_ref[:, :halo * width]
    last_ref[...] = grad_ref[:, (n - halo) * width:]


def grad_conv(ch, slope, pieces, halo):
    n, (channels, width) = len(pieces), pieces[0].shape
    shapes = [(channels, n * width), (channels, halo * width), (channels, halo * width)]
    return pl.pallas_call(
        functools.partial(slope_kernel, n, halo),
        in_specs=[pl.BlockSpec(memory_space=pltpu.SMEM)] + [pl.BlockSpec(memory_space=VMEM)] * (n + 1),
        out_specs=[pl.BlockSpec(memory_space=VMEM)] * 3,
        out_shape=[jax.ShapeDtypeStruct(s, jnp.bfloat16) for s in shapes],
        compiler_params=params(24),
        name="grad_conv",
    )(ch, slope, *pieces)


def back_kernel(n, halo, group, grad_ref, left_ref, right_ref, w_ref, *rest):
    out_ref, wide = rest[-2:]
    channels, width = out_ref.shape
    step = pl.program_id(0)

    @pl.when(step == 0)
    def _():
        wide[:, :halo * width] = left_ref[...]
        wide[:, halo * width:(halo + n) * width] = grad_ref[...]
        wide[:, (halo + n) * width:] = right_ref[...]

    for g in range(channels // group):
        rows = slice(g * group, (g + 1) * group)
        taps = [
            wide[rows, pl.ds(pl.multiple_of((step + t * halo) * width, width), width)]
            for t in range(3)
        ]
        out_ref[rows, :] = jnp.dot(
            w_ref[rows, :], jnp.concatenate(taps, axis=0), preferred_element_type=jnp.float32
        ).astype(jnp.bfloat16)


def backward(grad, left, right, weight, before, chunk, chunks, n, halo, group):
    channels, length = grad.shape
    width = length // n
    operands = [grad, left, right, weight]
    specs = [pl.BlockSpec(o.shape, lambda b: (0, 0)) for o in operands]
    aliases = {}
    if before is not None:
        operands.append(before)
        specs.append(pl.BlockSpec(memory_space=pl.ANY))
        aliases = {4: 0}
    return pl.pallas_call(
        functools.partial(back_kernel, n, halo, group),
        grid=(n,),
        in_specs=specs,
        out_specs=pl.BlockSpec((channels, width), lambda b: (0, b * chunks + chunk)),
        out_shape=jax.ShapeDtypeStruct((channels, length * chunks), jnp.bfloat16),
        scratch_shapes=[VMEM((channels, (n + 2 * halo) * width), jnp.bfloat16)],
        input_output_aliases=aliases,
        compiler_params=params(24),
        name="backward",
    )(*operands)


def mix_kernel(n, ch_ref, pw_ref, *rest):
    piece_refs, (out_ref, gathered) = rest[:n], rest[-2:]
    channels = piece_refs[0].shape[0]

    @pl.when(pl.program_id(0) == 0)
    def _():
        for k in range(n):
            b = ch_ref[0] ^ k
            gathered[pl.ds(pl.multiple_of(b * channels, channels), channels), :] = piece_refs[k][...]

    out_ref[...] = jnp.dot(
        pw_ref[...], gathered[...], preferred_element_type=jnp.float32
    ).astype(jnp.bfloat16)


def mix(ch, pw_weight, pieces, before, chunk, chunks):
    n, (channels, width) = len(pieces), pieces[0].shape
    total = pw_weight.shape[0]
    rows = 256
    operands = [ch, pw_weight, *pieces]
    specs = [pl.BlockSpec(memory_space=pltpu.SMEM), pl.BlockSpec((rows, total), lambda m: (m, 0))]
    specs += [pl.BlockSpec(p.shape, lambda m: (0, 0)) for p in pieces]
    aliases = {}
    if before is not None:
        operands.append(before)
        specs.append(pl.BlockSpec(memory_space=pl.ANY))
        aliases = {n + 2: 0}
    return pl.pallas_call(
        functools.partial(mix_kernel, n),
        grid=(total // rows,),
        in_specs=specs,
        out_specs=pl.BlockSpec((rows, width), lambda m: (m, chunk)),
        out_shape=jax.ShapeDtypeStruct((total, width * chunks), jnp.bfloat16),
        scratch_shapes=[VMEM((total, width), jnp.bfloat16)],
        input_output_aliases=aliases,
        compiler_params=params(24),
        name="mix",
    )(*operands)


def exchange(piece, k, n):
    return piece if k == 0 else lax.ppermute(piece, "ch", [(i, i ^ k) for i in range(n)])


def along(values, step):
    size = lax.axis_size("ctx")
    return lax.ppermute(
        values, "ctx", [(i, i + step) for i in range(size) if 0 <= i + step < size]
    )


def body(inputs, conv_weight, pw_weight, cotangent):
    n = lax.axis_size("ch")
    ch = lax.axis_index("ch").astype(jnp.int32)[None]
    channels, length = inputs.shape
    group = conv_weight.shape[2]
    block = cotangent.shape[1]
    halo = DILATION_STEP // block
    chunks = 2 if block % 256 == 0 else 1
    width = block // chunks

    own = lax.dynamic_slice_in_dim(conv_weight, ch[0] * channels, channels, 1)
    weight = jnp.moveaxis(own, 0, 1).reshape(channels, 3 * group)
    turned = own[::-1].reshape(3, channels // group, group, group).transpose(1, 3, 0, 2)
    turned = turned.reshape(channels, 3 * group)

    def edge(first, chunk):
        parts = [
            inputs[:, (first + i) * block + chunk * width:(first + i) * block + (chunk + 1) * width]
            for i in range(halo)
        ]
        return parts[0] if halo == 1 else jnp.concatenate(parts, axis=1)

    halos = [
        (along(edge(n - halo, c), 1), along(edge(0, c), -1)) for c in range(chunks)
    ]
    order = [k for k in range(n - 1, -1, -1)]
    upstreams = []
    for c in range(chunks):
        pieces = dict(zip(order, upstream(ch, pw_weight, cotangent, c, width, channels, order)))
        upstreams.append([exchange(pieces[k], k, n) for k in range(n)])
    mixed = grad_inputs = None
    forwards, grads = [], []
    for c in range(chunks):
        active, slope = forward(ch, inputs, *halos[c], weight, c, n, halo, width, group)
        grad, first, last = grad_conv(ch, slope, upstreams[c], halo)
        grads.append((grad, along(last, 1), along(first, -1)))
        forwards.append([exchange(active[k], k, n) for k in range(n)])
    for c in range(chunks):
        mixed = mix(ch, pw_weight, forwards[c], mixed, c, chunks)
        grad_inputs = backward(*grads[c], turned, grad_inputs, c, chunks, n, halo, group)
    return mixed, grad_inputs


def solution(mesh):
    placed = (P("ch", "ctx"), P(), P(), P(None, ("ctx", "ch")))
    return jax.shard_map(
        body,
        mesh=mesh,
        in_specs=placed,
        out_specs=(P(None, ("ctx", "ch")), P("ch", "ctx")),
        check_vma=False,
    )
```

```python
import functools

import jax
import jax.numpy as jnp
from jax import lax
from jax.experimental import pallas as pl
from jax.experimental.pallas import tpu as pltpu
from jax.sharding import PartitionSpec as P

DILATION_STEP = 512
GRANT = 56 << 20
PARAMS = pltpu.CompilerParams(vmem_limit_bytes=GRANT)
BF16 = jnp.bfloat16


def gelu_and_slope(v):
    square = v * v
    inner = v * (0.7978845608 + (0.7978845608 * 0.044715) * square)
    th = jnp.tanh(inner)
    half = 0.5 + 0.5 * th
    active = v * half
    inner_slope = 0.7978845608 + (3.0 * 0.7978845608 * 0.044715) * square
    slope = half + (0.5 * v) * (1.0 - th * th) * inner_slope
    return active, slope


def lanes(start, size):
    return pl.ds(pl.multiple_of(start, 128), size)


def upstream_kernel(order, where_ref, pw_ref, cot_ref, *piece_refs):
    step = pl.program_id(0)
    result = lax.dot_general(
        pw_ref[...], cot_ref[...], (((0,), (0,)), ((), ())), preferred_element_type=jnp.float32
    ).astype(BF16)
    for place in range(len(order)):
        @pl.when(step == place)
        def _(place=place):
            piece_refs[place][...] = result


def upstream(where, pw_weight, cotangent, channels, order):
    total, width = cotangent.shape
    if channels % 128 != 0:
        whole = lax.dot_general(
            pw_weight, cotangent, (((0,), (0,)), ((), ())), preferred_element_type=jnp.float32
        ).astype(BF16)
        return [lax.dynamic_slice_in_dim(whole, (where[0] ^ k) * channels, channels, 0) for k in order]

    def pw_index(step, where_ref):
        k = order[0]
        for place in range(1, len(order)):
            k = jnp.where(step == place, order[place], k)
        return 0, where_ref[0] ^ k

    return pl.pallas_call(
        functools.partial(upstream_kernel, order),
        grid_spec=pltpu.PrefetchScalarGridSpec(
            num_scalar_prefetch=1,
            grid=(len(order),),
            in_specs=[
                pl.BlockSpec((total, channels), pw_index),
                pl.BlockSpec((total, width), lambda step, where_ref: (0, 0)),
            ],
            out_specs=[pl.BlockSpec((channels, width), lambda step, where_ref: (0, 0))] * len(order),
        ),
        out_shape=[jax.ShapeDtypeStruct((channels, width), BF16)] * len(order),
        compiler_params=PARAMS,
        name="upstream",
    )(where, pw_weight, cotangent)


def place_halos(wide, middle, near_ref, far_ref, odd):
    halo, length = near_ref.shape[1], middle.shape[1]
    wide[:, lanes((1 - odd) * (halo + length), halo)] = near_ref[...]
    wide[:, lanes(odd * (halo + length), halo)] = far_ref[...]
    wide[:, halo:halo + length] = middle[...]


def forward_kernel(n, where_ref, x_ref, near_ref, far_ref, w_ref, *rest):
    up_refs, active_refs = rest[:n], rest[n:2 * n]
    grad_ref, near_out, far_out, wide = rest[2 * n:]
    ch, odd = where_ref[0], where_ref[1]
    halo, length = near_ref.shape[1], x_ref.shape[1]
    place_halos(wide, x_ref, near_ref, far_ref, odd)
    block = length // n
    unit = min(block, 256)
    for k in range(n):
        for s in range(block // unit):
            start = (ch ^ k) * block + s * unit
            here = slice(s * unit, (s + 1) * unit)
            conv_out = sum(
                jnp.dot(
                    w_ref[t], wide[:, lanes(start + t * halo, unit)], preferred_element_type=jnp.float32
                )
                for t in range(3)
            )
            active, slope = gelu_and_slope(conv_out)
            active_refs[k][:, here] = active.astype(BF16)
            grad_ref[:, lanes(start, unit)] = (
                up_refs[k][:, here].astype(jnp.float32) * slope
            ).astype(BF16)
    near_out[...] = grad_ref[:, lanes((1 - odd) * (length - halo), halo)]
    far_out[...] = grad_ref[:, lanes(odd * (length - halo), halo)]


def rows_of(array, group):
    return pl.BlockSpec((group, array.shape[1]), lambda g, where_ref: (g, 0))


def forward(where, inputs, near, far, weight, ups):
    n = len(ups)
    channels, length = inputs.shape
    group = weight.shape[2]
    groups = channels // group
    w_spec = pl.BlockSpec((3, group, group), lambda g, where_ref: (0, where_ref[0] * groups + g, 0))
    outs = [ups[0]] * n + [inputs, near, far]
    results = pl.pallas_call(
        functools.partial(forward_kernel, n),
        grid_spec=pltpu.PrefetchScalarGridSpec(
            num_scalar_prefetch=1,
            grid=(groups,),
            in_specs=[rows_of(inputs, group), rows_of(near, group), rows_of(far, group), w_spec]
            + [rows_of(u, group) for u in ups],
            out_specs=[rows_of(o, group) for o in outs],
            scratch_shapes=[pltpu.VMEM((group, length + 2 * near.shape[1]), BF16)],
        ),
        out_shape=[jax.ShapeDtypeStruct(o.shape, BF16) for o in outs],
        compiler_params=PARAMS,
        name="forward",
    )(where, inputs, near, far, weight, *ups)
    return results[:n], *results[n:]


def back_kernel(where_ref, grad_ref, near_ref, far_ref, w_ref, out_ref, wide):
    halo, length = near_ref.shape[1], grad_ref.shape[1]
    place_halos(wide, grad_ref, near_ref, far_ref, where_ref[1])
    unit = 256
    turned = [w_ref[t].T for t in range(3)]
    for s in range(length // unit):
        out_ref[:, s * unit:(s + 1) * unit] = sum(
            jnp.dot(
                turned[2 - t], wide[:, s * unit + t * halo:s * unit + t * halo + unit],
                preferred_element_type=jnp.float32,
            )
            for t in range(3)
        ).astype(BF16)


def backward(where, grad, near, far, weight):
    channels, length = grad.shape
    group = weight.shape[2]
    groups = channels // group
    w_spec = pl.BlockSpec((3, group, group), lambda g, where_ref: (0, where_ref[0] * groups + g, 0))
    return pl.pallas_call(
        back_kernel,
        grid_spec=pltpu.PrefetchScalarGridSpec(
            num_scalar_prefetch=1,
            grid=(groups,),
            in_specs=[rows_of(grad, group), rows_of(near, group), rows_of(far, group), w_spec],
            out_specs=rows_of(grad, group),
            scratch_shapes=[pltpu.VMEM((group, length + 2 * near.shape[1]), BF16)],
        ),
        out_shape=jax.ShapeDtypeStruct(grad.shape, BF16),
        compiler_params=PARAMS,
        name="backward",
    )(where, grad, near, far, weight)


def mix_kernel(n, where_ref, pw_ref, *rest):
    piece_refs, (out_ref, gathered) = rest[:n], rest[n:]
    channels = piece_refs[0].shape[0]

    @pl.when(pl.program_id(0) == 0)
    def _():
        for k in range(n):
            start = (where_ref[0] ^ k) * channels
            gathered[pl.ds(pl.multiple_of(start, 16), channels), :] = piece_refs[k][...]

    out_ref[...] = jnp.dot(
        pw_ref[...], gathered[...], preferred_element_type=jnp.float32
    ).astype(BF16)


def mix(where, pw_weight, pieces):
    n, width = len(pieces), pieces[0].shape[1]
    total = pw_weight.shape[0]
    rows = 256
    return pl.pallas_call(
        functools.partial(mix_kernel, n),
        grid_spec=pltpu.PrefetchScalarGridSpec(
            num_scalar_prefetch=1,
            grid=(total // rows,),
            in_specs=[pl.BlockSpec((rows, total), lambda m, where_ref: (m, 0))]
            + [pl.BlockSpec(p.shape, lambda m, where_ref: (0, 0)) for p in pieces],
            out_specs=pl.BlockSpec((rows, width), lambda m, where_ref: (m, 0)),
            scratch_shapes=[pltpu.VMEM((total, width), BF16)],
        ),
        out_shape=jax.ShapeDtypeStruct((total, width), BF16),
        compiler_params=PARAMS,
        name="mix",
    )(where, pw_weight, *pieces)


def exchange(piece, k):
    if k == 0:
        return piece
    return lax.ppermute(piece, "ch", [(i, i ^ k) for i in range(lax.axis_size("ch"))])


def swap(values, first):
    size = lax.axis_size("ctx")
    pairs = [(i, i + 1) for i in range(first, size - 1, 2)]
    return lax.ppermute(values, "ctx", pairs + [(b, a) for a, b in pairs])


def body(inputs, conv_weight, pw_weight, cotangent):
    n = lax.axis_size("ch")
    odd = lax.axis_index("ctx") % 2
    where = jnp.stack([lax.axis_index("ch"), odd]).astype(jnp.int32)
    channels, length = inputs.shape

    def edge(at_end):
        return lax.dynamic_slice_in_dim(inputs, at_end * (length - DILATION_STEP), DILATION_STEP, 1)

    near, far = swap(edge(1 - odd), 0), swap(edge(odd), 1)
    order = list(range(n - 1, -1, -1))
    ups = {}
    for part in (order[:n // 2], order[n // 2:]):
        pieces = upstream(where, pw_weight, cotangent, channels, part)
        for k, piece in zip(part, pieces):
            ups[k] = exchange(piece, k)
    active, grad, near_grad, far_grad = forward(
        where, inputs, near, far, conv_weight, [ups[k] for k in range(n)]
    )
    near_grad, far_grad = swap(near_grad, 0), swap(far_grad, 1)
    active = {k: exchange(active[k], k) for k in order}
    mixed = mix(where, pw_weight, [active[k] for k in range(n)])
    return mixed, backward(where, grad, near_grad, far_grad, conv_weight)


def solution(mesh):
    placed = (P("ch", "ctx"), P(), P(), P(None, ("ctx", "ch")))
    return jax.shard_map(
        body,
        mesh=mesh,
        in_specs=placed,
        out_specs=(P(None, ("ctx", "ch")), P("ch", "ctx")),
        check_vma=False,
    )
```

```python
import functools

import jax
import jax.numpy as jnp
from jax import lax
from jax.experimental import pallas as pl
from jax.experimental.pallas import tpu as pltpu
from jax.sharding import PartitionSpec as P

DILATION_STEP = 512
BF16, F32 = jnp.bfloat16, jnp.float32
ANY = pl.BlockSpec(memory_space=pl.ANY)
INSIDE = pl.BlockSpec(memory_space=pltpu.VMEM)
DMA = pltpu.SemaphoreType.DMA


def kernel_call(name, kernel, operands, outs, scratch=(), aliases=None):
    return pl.pallas_call(
        kernel,
        in_specs=[INSIDE if held else ANY for _, held in operands],
        out_specs=[INSIDE if held else ANY for _, _, held in outs],
        out_shape=[
            pltpu.VMEM(shape, kind) if held else jax.ShapeDtypeStruct(shape, kind)
            for shape, kind, held in outs
        ],
        scratch_shapes=list(scratch),
        input_output_aliases=aliases or {},
        compiler_params=pltpu.CompilerParams(vmem_limit_bytes=16 << 20),
        name=name,
    )(*[
        pltpu.with_memory_space_constraint(array, pltpu.VMEM) if held else array
        for array, held in operands
    ])


def gelu_and_slope(v):
    square = v * v
    inner = v * (0.7978845608 + (0.7978845608 * 0.044715) * square)
    th = jnp.tanh(inner)
    half = 0.5 + 0.5 * th
    active = v * half
    inner_slope = 0.7978845608 + (3.0 * 0.7978845608 * 0.044715) * square
    slope = half + (0.5 * v) * (1.0 - th * th) * inner_slope
    return active, slope


def lanes(start, size):
    return pl.ds(pl.multiple_of(start, 128), size)


def dot(a, b):
    return jnp.dot(a, b, preferred_element_type=F32)


def turned_dot(a, b):
    return lax.dot_general(a, b, (((0,), (0,)), ((), ())), preferred_element_type=F32)


def odd_place():
    return lax.axis_index("ctx") % 2


def upstream_kernel(order, channels, first, pw_ref, cot_ref, *rest):
    count = len(order)
    sems = rest[-1]
    if first:
        x_ref, piece_refs = rest[0], rest[1:1 + count]
        columns_ref, cot_in, near_ref, far_ref = rest[1 + count:-1]
    else:
        piece_refs, columns_ref, cot_in = rest[:count], rest[count], cot_ref
    ch, odd = lax.axis_index("ch"), odd_place()
    copies = []
    if first:
        copies.append(pltpu.make_async_copy(cot_ref, cot_in, sems.at[count]))
        copies[0].start()
    blocks = []
    if channels % 128 == 0:
        for place, k in enumerate(order):
            blocks.append(pltpu.make_async_copy(
                pw_ref.at[:, lanes((ch ^ k) * channels, channels)],
                columns_ref.at[:, place * channels:(place + 1) * channels], sems.at[place],
            ))
    else:
        blocks.append(pltpu.make_async_copy(pw_ref, columns_ref, sems.at[0]))
    for block in blocks:
        block.start()
    if first:
        length, halo = x_ref.shape[1], near_ref.shape[1]
        for place, (edge_ref, at_end) in enumerate(((near_ref, 1 - odd), (far_ref, odd))):
            copies.append(pltpu.make_async_copy(
                x_ref.at[:, lanes(at_end * (length - halo), halo)], edge_ref, sems.at[count + 1 + place]
            ))
            copies[-1].start()
        copies[0].wait()
    if len(blocks) == count:
        for place in range(count):
            blocks[place].wait()
            columns = slice(place * channels, (place + 1) * channels)
            piece_refs[place][...] = turned_dot(columns_ref[:, columns], cot_in[...]).astype(BF16)
    else:
        blocks[0].wait()
        result = turned_dot(columns_ref[...], cot_in[...]).astype(BF16)
        for place in range(count):
            piece_refs[place][...] = result[place * channels:(place + 1) * channels]
    for copy in copies[1:]:
        copy.wait()


def upstream(pw_weight, cotangent, inputs, channels, order):
    total, width = cotangent.shape
    first = inputs is not None
    if channels % 128 != 0:
        ch = lax.axis_index("ch")
        pw_weight = jnp.concatenate(
            [lax.dynamic_slice_in_dim(pw_weight, (ch ^ k) * channels, channels, 1) for k in order], axis=1
        )
    count = len(order)
    operands = [(pw_weight, False), (cotangent, not first)]
    outs = [((channels, width), BF16, True)] * count + [((total, count * channels), BF16, True)]
    if first:
        operands.append((inputs, False))
        outs += [(cotangent.shape, BF16, True)] + [((channels, DILATION_STEP), BF16, True)] * 2
    results = kernel_call(
        "upstream", functools.partial(upstream_kernel, order, channels, first), operands, outs,
        [DMA((count + 3,))],
    )
    return results[:count], *results[count:]


def convolve(w_ref, rows, wide, start, halo, unit):
    return sum(dot(w_ref[t, rows, :], wide[rows, lanes(start + t * halo, unit)]) for t in range(3))


def interior_kernel(n, x_ref, w_ref, *rest):
    active_refs, (slope_ref, wide, plain_ref, turned_ref, sem) = rest[:n], rest[n:]
    ch = lax.axis_index("ch")
    channels, length = x_ref.shape
    group = w_ref.shape[1]
    halo = DILATION_STEP
    block = length // n
    unit = min(block, 256)
    copy = pltpu.make_async_copy(x_ref, wide.at[:, halo:halo + length], sem)
    copy.start()
    groups = [slice(g, g + group) for g in range(0, channels, group)]
    for t in range(3):
        for rows in groups:
            square = w_ref[t, :, rows]
            turned_ref[2 - t, rows, :] = square
            plain_ref[t, rows, :] = square.T
    copy.wait()
    for k in range(n):
        base = (ch ^ k) * block

        @pl.when((base >= halo) & (base < length - halo))
        def _(k=k, base=base):
            for s in range(0, block, unit):
                for rows in groups:
                    active, slope = gelu_and_slope(convolve(plain_ref, rows, wide, base + s, halo, unit))
                    active_refs[k][rows, s:s + unit] = active.astype(BF16)
                    slope_ref[k, rows, s:s + unit] = slope


def interior(inputs, weight, n):
    channels, length = inputs.shape
    group = weight.shape[1]
    block = length // n
    outs = [((channels, block), BF16, True)] * n
    outs += [((n, channels, block), F32, True), ((channels, length + 2 * DILATION_STEP), BF16, True)]
    outs += [((3, channels, group), BF16, True)] * 2
    results = kernel_call(
        "interior", functools.partial(interior_kernel, n), [(inputs, False), (weight, True)], outs, [DMA],
    )
    return results[:n], *results[n:]


def edges_kernel(n, near_ref, far_ref, slope_ref, plain_ref, *rest):
    up_refs, rest = rest[:n], rest[n + n + 1:]
    active_refs, (wide, grad_ref, near_out, far_out) = rest[:n], rest[n:]
    ch, odd = lax.axis_index("ch"), odd_place()
    channels, length = grad_ref.shape
    group = plain_ref.shape[2]
    halo = near_ref.shape[1]
    block = length // n
    unit = min(block, 256)
    groups = [slice(g, g + group) for g in range(0, channels, group)]
    wide[:, lanes((1 - odd) * (halo + length), halo)] = near_ref[...]
    wide[:, lanes(odd * (halo + length), halo)] = far_ref[...]
    for k in range(n):
        base = (ch ^ k) * block
        inner = (base >= halo) & (base < length - halo)

        @pl.when(inner)
        def _(k=k, base=base):
            grad_ref[:, lanes(base, block)] = (
                up_refs[k][...].astype(F32) * slope_ref[k]
            ).astype(BF16)

        @pl.when(jnp.logical_not(inner))
        def _(k=k, base=base):
            for s in range(0, block, unit):
                for rows in groups:
                    active, slope = gelu_and_slope(convolve(plain_ref, rows, wide, base + s, halo, unit))
                    active_refs[k][rows, s:s + unit] = active.astype(BF16)
                    grad_ref[rows, lanes(base + s, unit)] = (
                        up_refs[k][rows, s:s + unit].astype(F32) * slope
                    ).astype(BF16)
    near_out[...] = grad_ref[:, lanes((1 - odd) * (length - halo), halo)]
    far_out[...] = grad_ref[:, lanes(odd * (length - halo), halo)]


def edges(near, far, slope, plain, ups, active, wide):
    n = len(ups)
    channels, halo = near.shape
    length = wide.shape[1] - 2 * halo
    operands = [(o, True) for o in (near, far, slope, plain, *ups, *active, wide)]
    outs = [(a.shape, BF16, True) for a in active] + [(wide.shape, BF16, True)]
    outs += [((channels, length), BF16, True)] + [((channels, halo), BF16, True)] * 2
    results = kernel_call(
        "edges", functools.partial(edges_kernel, n), operands, outs,
        aliases={4 + n + i: i for i in range(n + 1)},
    )
    return results[:n], *results[n + 1:]


def half_mix_kernel(columns_ref, *rest):
    piece_refs, sum_ref = rest[:-1], rest[-1]
    pieces = jnp.concatenate([p[...] for p in piece_refs], axis=0)
    rows = 512
    for m in range(0, sum_ref.shape[0], rows):
        sum_ref[m:m + rows, :] = dot(columns_ref[m:m + rows, :], pieces)


def last_mix_kernel(columns_ref, sum_ref, *rest):
    piece_refs, (out_ref, held, sems) = rest[:-3], rest[-3:]
    pieces = jnp.concatenate([p[...] for p in piece_refs], axis=0)
    rows = 512
    copies = []
    for step, m in enumerate(range(0, sum_ref.shape[0], rows)):
        held[m:m + rows, :] = (sum_ref[m:m + rows, :] + dot(columns_ref[m:m + rows, :], pieces)).astype(BF16)
        copies.append(pltpu.make_async_copy(held.at[m:m + rows, :], out_ref.at[m:m + rows, :], sems.at[step]))
        copies[-1].start()
    for copy in copies:
        copy.wait()


def back(turned_ref, rows, taps):
    return sum(dot(turned_ref[t, rows, :], tap) for t, tap in enumerate(taps)).astype(BF16)


def back_interior_kernel(grad_ref, turned_ref, out_ref, held, sem):
    channels, length = grad_ref.shape
    group, halo, unit = turned_ref.shape[2], DILATION_STEP, 256
    for g in range(0, channels, group):
        rows = slice(g, g + group)
        for s in range(0, length - 2 * halo, unit):
            held[rows, s:s + unit] = back(
                turned_ref, rows, [grad_ref[rows, s + t * halo:s + t * halo + unit] for t in range(3)]
            )
    copy = pltpu.make_async_copy(held, out_ref.at[:, halo:length - halo], sem)
    copy.start()
    copy.wait()


def back_ends_kernel(grad_ref, near_ref, far_ref, turned_ref, _, out_ref, halos, held, sems):
    channels, length = grad_ref.shape
    group, halo, unit = turned_ref.shape[2], DILATION_STEP, 256
    odd = odd_place()
    halos[:, lanes((1 - odd) * halo, halo)] = near_ref[...]
    halos[:, lanes(odd * halo, halo)] = far_ref[...]
    copies = []
    for end in range(2):
        for g in range(0, channels, group):
            rows = slice(g, g + group)
            for s in range(0, halo, unit):
                inner = (length - 2 * halo) * end + s
                taps = [
                    grad_ref[rows, inner:inner + unit],
                    grad_ref[rows, inner + halo:inner + halo + unit],
                ]
                outer = halos[rows, end * halo + s:end * halo + s + unit]
                taps = taps + [outer] if end else [outer] + taps
                held[rows, end * halo + s:end * halo + s + unit] = back(turned_ref, rows, taps)
        copies.append(pltpu.make_async_copy(
            held.at[:, end * halo:(end + 1) * halo],
            out_ref.at[:, end * (length - halo):end * (length - halo) + halo], sems.at[end],
        ))
        copies[-1].start()
    for copy in copies:
        copy.wait()


def exchange(piece, k):
    if k == 0:
        return piece
    return lax.ppermute(piece, "ch", [(i, i ^ k) for i in range(lax.axis_size("ch"))])


def swap(values, first):
    size = lax.axis_size("ctx")
    pairs = [(i, i + 1) for i in range(first, size - 1, 2)]
    return lax.ppermute(values, "ctx", pairs + [(b, a) for a, b in pairs])


def body(inputs, conv_weight, pw_weight, cotangent):
    n = lax.axis_size("ch")
    channels, length = inputs.shape
    total, width = cotangent.shape
    halo = DILATION_STEP
    order = list(range(n - 1, -1, -1))
    parts = order[:n // 2], order[n // 2:]

    ups, columns = {}, []
    pieces, held, cot_in, near, far = upstream(pw_weight, cotangent, inputs, channels, parts[0])
    columns.append(held)
    ups.update({k: exchange(p, k) for k, p in zip(parts[0], pieces)})
    near, far = swap(near, 0), swap(far, 1)
    pieces, held = upstream(pw_weight, cot_in, None, channels, parts[1])
    columns.append(held)
    ups.update({k: exchange(p, k) for k, p in zip(parts[1], pieces)})

    weight = lax.dynamic_slice_in_dim(
        jnp.swapaxes(conv_weight, 1, 2), lax.axis_index("ch") * channels, channels, 2
    )
    active, slope, wide, plain, turned = interior(inputs, weight, n)
    active, grad, near_grad, far_grad = edges(
        near, far, slope, plain, [ups[k] for k in range(n)], active, wide
    )
    active = {k: exchange(active[k], k) for k in order}
    near_grad, far_grad = swap(near_grad, 0), swap(far_grad, 1)

    grad_shape = ((channels, length), BF16, False)
    (grad_inputs,) = kernel_call(
        "back_interior", back_interior_kernel, [(grad, True), (turned, True)], [grad_shape],
        [pltpu.VMEM((channels, length - 2 * halo), BF16), DMA],
    )
    (partial,) = kernel_call(
        "half_mix", half_mix_kernel, [(o, True) for o in (columns[1], *[active[k] for k in parts[1]])],
        [((total, width), F32, True)],
    )
    (mixed,) = kernel_call(
        "last_mix", last_mix_kernel,
        [(o, True) for o in (columns[0], partial, *[active[k] for k in parts[0]])],
        [((total, width), BF16, False)], [pltpu.VMEM((total, width), BF16), DMA((total // 512,))],
    )
    (grad_inputs,) = kernel_call(
        "back_ends", back_ends_kernel,
        [(o, True) for o in (grad, near_grad, far_grad, turned)] + [(grad_inputs, False)], [grad_shape],
        [pltpu.VMEM((channels, 2 * halo), BF16)] * 2 + [DMA((2,))], {4: 0},
    )
    return mixed, grad_inputs


def solution(mesh):
    placed = (P("ch", "ctx"), P(), P(), P(None, ("ctx", "ch")))
    return jax.shard_map(
        body,
        mesh=mesh,
        in_specs=placed,
        out_specs=(P(None, ("ctx", "ch")), P("ch", "ctx")),
        check_vma=False,
    )
```

```python
import functools

import jax
import jax.numpy as jnp
from jax import lax
from jax.experimental import pallas as pl
from jax.experimental.pallas import tpu as pltpu
from jax.sharding import PartitionSpec as P

DILATION_STEP = 512
BF16, F32 = jnp.bfloat16, jnp.float32
ANY = pl.BlockSpec(memory_space=pl.ANY)
INSIDE = pl.BlockSpec(memory_space=pltpu.VMEM)
DMA = pltpu.SemaphoreType.DMA


def kernel_call(name, kernel, operands, outs, scratch=(), aliases=None):
    return pl.pallas_call(
        kernel,
        in_specs=[INSIDE if held else ANY for _, held in operands],
        out_specs=[INSIDE if held else ANY for _, _, held in outs],
        out_shape=[
            pltpu.VMEM(shape, kind) if held else jax.ShapeDtypeStruct(shape, kind)
            for shape, kind, held in outs
        ],
        scratch_shapes=list(scratch),
        input_output_aliases=aliases or {},
        compiler_params=pltpu.CompilerParams(vmem_limit_bytes=16 << 20),
        name=name,
    )(*[
        pltpu.with_memory_space_constraint(array, pltpu.VMEM if held else pltpu.HBM)
        for array, held in operands
    ])


def gelu_and_slope(v):
    square = v * v
    inner = v * (0.7978845608 + (0.7978845608 * 0.044715) * square)
    th = jnp.tanh(inner)
    half = 0.5 + 0.5 * th
    active = v * half
    inner_slope = 0.7978845608 + (3.0 * 0.7978845608 * 0.044715) * square
    slope = half + (0.5 * v) * (1.0 - th * th) * inner_slope
    return active, slope


def lanes(start, size):
    return pl.ds(pl.multiple_of(start, 128), size)


def dot(a, b):
    return jnp.dot(a, b, preferred_element_type=F32)


def turned_dot(a, b):
    return lax.dot_general(a, b, (((0,), (0,)), ((), ())), preferred_element_type=F32)


def odd_place():
    return lax.axis_index("ctx") % 2


def ends_kernel(x_ref, near_ref, far_ref, sems):
    odd = odd_place()
    length, halo = x_ref.shape[1], near_ref.shape[1]
    copies = [
        pltpu.make_async_copy(x_ref.at[:, lanes(at_end * (length - halo), halo)], end_ref, sems.at[place])
        for place, (end_ref, at_end) in enumerate(((near_ref, 1 - odd), (far_ref, odd)))
    ]
    for copy in copies:
        copy.start()
    for copy in copies:
        copy.wait()


def upstream_kernel(order, channels, pw_ref, cot_ref, *piece_refs):
    if channels % 128 == 0:
        for k, piece_ref in zip(order, piece_refs):
            columns = lanes((lax.axis_index("ch") ^ k) * channels, channels)
            piece_ref[...] = turned_dot(pw_ref[:, columns], cot_ref[...]).astype(BF16)
    else:
        result = turned_dot(pw_ref[...], cot_ref[...]).astype(BF16)
        for place, piece_ref in enumerate(piece_refs):
            piece_ref[...] = result[place * channels:(place + 1) * channels]


def columns_of(pw_weight, channels, order):
    if channels % 128 == 0:
        return pw_weight
    ch = lax.axis_index("ch")
    return jnp.concatenate(
        [lax.dynamic_slice_in_dim(pw_weight, (ch ^ k) * channels, channels, 1) for k in order], axis=1
    )


def upstream(pw_weight, cotangent, channels, order):
    return kernel_call(
        "upstream", functools.partial(upstream_kernel, order, channels),
        [(columns_of(pw_weight, channels, order), True), (cotangent, True)],
        [((channels, cotangent.shape[1]), BF16, True)] * len(order),
    )


def convolve(w_ref, rows, wide, start, halo, unit):
    return sum(dot(w_ref[t, rows, :], wide[rows, lanes(start + t * halo, unit)]) for t in range(3))


def interior_kernel(n, x_ref, w_ref, *rest):
    active_refs, (slope_ref, wide, plain_ref, turned_ref, sem) = rest[:n], rest[n:]
    ch = lax.axis_index("ch")
    channels, length = x_ref.shape
    group = w_ref.shape[1]
    halo = DILATION_STEP
    block = length // n
    unit = min(block, 256)
    copy = pltpu.make_async_copy(x_ref, wide.at[:, halo:halo + length], sem)
    copy.start()
    groups = [slice(g, g + group) for g in range(0, channels, group)]
    for t in range(3):
        for rows in groups:
            square = w_ref[t, :, rows]
            turned_ref[2 - t, rows, :] = square
            plain_ref[t, rows, :] = square.T
    copy.wait()
    for k in range(n):
        base = (ch ^ k) * block

        @pl.when((base >= halo) & (base < length - halo))
        def _(k=k, base=base):
            for s in range(0, block, unit):
                for rows in groups:
                    active, slope = gelu_and_slope(convolve(plain_ref, rows, wide, base + s, halo, unit))
                    active_refs[k][rows, s:s + unit] = active.astype(BF16)
                    slope_ref[rows, lanes(base + s, unit)] = slope


def interior(inputs, weight, n):
    channels, length = inputs.shape
    group = weight.shape[1]
    block = length // n
    outs = [((channels, block), BF16, True)] * n
    outs += [((channels, length), F32, True), ((channels, length + 2 * DILATION_STEP), BF16, True)]
    outs += [((3, channels, group), BF16, True)] * 2
    results = kernel_call(
        "interior", functools.partial(interior_kernel, n), [(inputs, False), (weight, True)], outs, [DMA],
    )
    return results[:n], *results[n:]


def near_kernel(n, near_ref, plain_ref, *rest):
    active_refs, (slope_ref, wide) = rest[n + 2:n + 2 + n], rest[n + 2 + n:]
    ch, odd = lax.axis_index("ch"), odd_place()
    channels, length = slope_ref.shape
    group = plain_ref.shape[2]
    halo = near_ref.shape[1]
    block = length // n
    unit = min(block, 256)
    groups = [slice(g, g + group) for g in range(0, channels, group)]
    wide[:, lanes((1 - odd) * (halo + length), halo)] = near_ref[...]
    first = (1 - odd) * (length - halo)
    for k in range(n):
        base = (ch ^ k) * block

        @pl.when((base >= first) & (base < first + halo))
        def _(k=k, base=base):
            for s in range(0, block, unit):
                for rows in groups:
                    active, slope = gelu_and_slope(convolve(plain_ref, rows, wide, base + s, halo, unit))
                    active_refs[k][rows, s:s + unit] = active.astype(BF16)
                    slope_ref[rows, lanes(base + s, unit)] = slope


def near_end(near, plain, active, slope, wide):
    n = len(active)
    operands = [(o, True) for o in (near, plain, *active, slope, wide)]
    outs = [(a.shape, a.dtype, True) for a in (*active, slope, wide)]
    results = kernel_call(
        "near_end", functools.partial(near_kernel, n), operands, outs,
        aliases={2 + i: i for i in range(n + 2)},
    )
    return results[:n], *results[n:]


def grad_kernel(n, slope_ref, *rest):
    up_refs, (grad_ref, near_out) = rest[:n], rest[n:]
    ch, odd = lax.axis_index("ch"), odd_place()
    length, halo = grad_ref.shape[1], near_out.shape[1]
    block = length // n
    first = odd * (length - halo)
    for k in range(n):
        base = (ch ^ k) * block

        @pl.when((base < first) | (base >= first + halo))
        def _(k=k, base=base):
            here = lanes(base, block)
            grad_ref[:, here] = (up_refs[k][...].astype(F32) * slope_ref[:, here]).astype(BF16)
    near_out[...] = grad_ref[:, lanes((1 - odd) * (length - halo), halo)]


def grad_conv(slope, ups):
    channels = slope.shape[0]
    return kernel_call(
        "grad_conv", functools.partial(grad_kernel, len(ups)), [(o, True) for o in (slope, *ups)],
        [(slope.shape, BF16, True), ((channels, DILATION_STEP), BF16, True)],
    )


def far_kernel(n, far_ref, plain_ref, *rest):
    up_refs, rest = rest[:n], rest[n + n + 2:]
    active_refs, (wide, grad_ref, far_out) = rest[:n], rest[n:]
    ch, odd = lax.axis_index("ch"), odd_place()
    channels, length = grad_ref.shape
    group = plain_ref.shape[2]
    halo = far_ref.shape[1]
    block = length // n
    unit = min(block, 256)
    groups = [slice(g, g + group) for g in range(0, channels, group)]
    wide[:, lanes(odd * (halo + length), halo)] = far_ref[...]
    first = odd * (length - halo)
    for k in range(n):
        base = (ch ^ k) * block

        @pl.when((base >= first) & (base < first + halo))
        def _(k=k, base=base):
            for s in range(0, block, unit):
                for rows in groups:
                    active, slope = gelu_and_slope(convolve(plain_ref, rows, wide, base + s, halo, unit))
                    active_refs[k][rows, s:s + unit] = active.astype(BF16)
                    grad = (up_refs[k][rows, s:s + unit].astype(F32) * slope).astype(BF16)
                    grad_ref[rows, lanes(base + s, unit)] = grad
                    far_out[rows, lanes(base + s - first, unit)] = grad


def far_end(far, plain, ups, active, wide, grad):
    n = len(active)
    operands = [(o, True) for o in (far, plain, *ups, *active, wide, grad)]
    outs = [(a.shape, BF16, True) for a in (*active, wide, grad, far)]
    results = kernel_call(
        "far_end", functools.partial(far_kernel, n), operands, outs,
        aliases={2 + n + i: i for i in range(n + 2)},
    )
    return results[:n], *results[n + 1:]


def columns_times(order, pw_ref, rows, pieces):
    channels = pieces.shape[0] // len(order)
    if channels % 128 != 0:
        return dot(pw_ref[rows, :], pieces)
    return sum(
        dot(
            pw_ref[rows, lanes((lax.axis_index("ch") ^ k) * channels, channels)],
            pieces[place * channels:(place + 1) * channels],
        )
        for place, k in enumerate(order)
    )


def half_mix_kernel(order, pw_ref, *rest):
    piece_refs, sum_ref = rest[:-1], rest[-1]
    pieces = jnp.concatenate([p[...] for p in piece_refs], axis=0)
    step = 512
    for m in range(0, sum_ref.shape[0], step):
        rows = slice(m, m + step)
        sum_ref[rows, :] = columns_times(order, pw_ref, rows, pieces)


def last_mix_kernel(order, pw_ref, sum_ref, *rest):
    piece_refs, (out_ref, done_ref, held, sems) = rest[:-4], rest[-4:]
    pieces = jnp.concatenate([p[...] for p in piece_refs], axis=0)
    step = 512
    copies = []
    for m in range(0, sum_ref.shape[0], step):
        rows = slice(m, m + step)
        held[rows, :] = (sum_ref[rows, :] + columns_times(order, pw_ref, rows, pieces)).astype(BF16)
        copies.append(pltpu.make_async_copy(held.at[rows, :], out_ref.at[rows, :], sems.at[len(copies)]))
        copies[-1].start()
    done_ref[...] = jnp.zeros_like(done_ref)
    for copy in copies:
        copy.wait()


def back(turned_ref, rows, taps):
    return sum(dot(turned_ref[t, rows, :], tap) for t, tap in enumerate(taps)).astype(BF16)


def back_interior_kernel(grad_ref, turned_ref, out_ref, held, sem):
    channels, length = grad_ref.shape
    group, halo, unit = turned_ref.shape[2], DILATION_STEP, 256
    for g in range(0, channels, group):
        rows = slice(g, g + group)
        for s in range(0, length - 2 * halo, unit):
            held[rows, s:s + unit] = back(
                turned_ref, rows, [grad_ref[rows, s + t * halo:s + t * halo + unit] for t in range(3)]
            )
    copy = pltpu.make_async_copy(held, out_ref.at[:, halo:length - halo], sem)
    copy.start()
    copy.wait()


def back_ends_kernel(grad_ref, near_ref, far_ref, turned_ref, _, __, out_ref, halos, held, sems):
    channels, length = grad_ref.shape
    group, halo, unit = turned_ref.shape[2], DILATION_STEP, 256
    odd = odd_place()
    halos[:, lanes((1 - odd) * halo, halo)] = near_ref[...]
    halos[:, lanes(odd * halo, halo)] = far_ref[...]
    copies = []
    for end in range(2):
        for g in range(0, channels, group):
            rows = slice(g, g + group)
            for s in range(0, halo, unit):
                inner = (length - 2 * halo) * end + s
                taps = [
                    grad_ref[rows, inner:inner + unit],
                    grad_ref[rows, inner + halo:inner + halo + unit],
                ]
                outer = halos[rows, end * halo + s:end * halo + s + unit]
                taps = taps + [outer] if end else [outer] + taps
                held[rows, end * halo + s:end * halo + s + unit] = back(turned_ref, rows, taps)
        copies.append(pltpu.make_async_copy(
            held.at[:, end * halo:(end + 1) * halo],
            out_ref.at[:, end * (length - halo):end * (length - halo) + halo], sems.at[end],
        ))
        copies[-1].start()
    for copy in copies:
        copy.wait()


def exchange(piece, k):
    if k == 0:
        return piece
    return lax.ppermute(piece, "ch", [(i, i ^ k) for i in range(lax.axis_size("ch"))])


def swap(values, first):
    size = lax.axis_size("ctx")
    pairs = [(i, i + 1) for i in range(first, size - 1, 2)]
    return lax.ppermute(values, "ctx", pairs + [(b, a) for a, b in pairs])


def body(inputs, conv_weight, pw_weight, cotangent):
    n = lax.axis_size("ch")
    channels, length = inputs.shape
    total, width = cotangent.shape
    halo = DILATION_STEP
    order = list(range(n - 1, -1, -1))
    parts = order[:n // 2], order[n // 2:]

    near, far = kernel_call(
        "ends", ends_kernel, [(inputs, False)], [((channels, halo), BF16, True)] * 2, [DMA((2,))]
    )
    near, far = swap(near, 0), swap(far, 1)
    ups = {}
    for part in parts:
        pieces = upstream(pw_weight, cotangent, channels, part)
        ups.update({k: exchange(p, k) for k, p in zip(part, pieces)})
    ups = [ups[k] for k in range(n)]

    weight = lax.dynamic_slice_in_dim(
        jnp.swapaxes(conv_weight, 1, 2), lax.axis_index("ch") * channels, channels, 2
    )
    active, slope, wide, plain, turned = interior(inputs, weight, n)
    active, slope, wide = near_end(near, plain, active, slope, wide)
    grad, near_grad = grad_conv(slope, ups)
    near_grad = swap(near_grad, 0)
    active, grad, far_grad = far_end(far, plain, ups, active, wide, grad)
    active = {k: exchange(active[k], k) for k in order}
    far_grad = swap(far_grad, 1)

    grad_shape = ((channels, length), BF16, False)
    (grad_inputs,) = kernel_call(
        "back_interior", back_interior_kernel, [(grad, True), (turned, True)], [grad_shape],
        [pltpu.VMEM((channels, length - 2 * halo), BF16), DMA],
    )
    (partial,) = kernel_call(
        "half_mix", functools.partial(half_mix_kernel, parts[1]),
        [(o, True) for o in (columns_of(pw_weight, channels, parts[1]), *[active[k] for k in parts[1]])],
        [((total, width), F32, True)],
    )
    mixed, done = kernel_call(
        "last_mix", functools.partial(last_mix_kernel, parts[0]),
        [(o, True) for o in (columns_of(pw_weight, channels, parts[0]), partial, *[active[k] for k in parts[0]])],
        [((total, width), BF16, False), ((8, 128), F32, True)],
        [pltpu.VMEM((total, width), BF16), DMA((total // 512,))],
    )
    (grad_inputs,) = kernel_call(
        "back_ends", back_ends_kernel,
        [(o, True) for o in (grad, near_grad, far_grad, turned, done)] + [(grad_inputs, False)], [grad_shape],
        [pltpu.VMEM((channels, 2 * halo), BF16)] * 2 + [DMA((2,))], {5: 0},
    )
    return mixed, grad_inputs


def solution(mesh):
    placed = (P("ch", "ctx"), P(), P(), P(None, ("ctx", "ch")))
    return jax.shard_map(
        body,
        mesh=mesh,
        in_specs=placed,
        out_specs=(P(None, ("ctx", "ch")), P("ch", "ctx")),
        check_vma=False,
    )
```

```python
import functools

import jax
import jax.numpy as jnp
from jax import lax
from jax.experimental import pallas as pl
from jax.experimental.pallas import tpu as pltpu
from jax.sharding import PartitionSpec as P

DILATION_STEP = 512
BF16, F32 = jnp.bfloat16, jnp.float32
ANY = pl.BlockSpec(memory_space=pl.ANY)
INSIDE = pl.BlockSpec(memory_space=pltpu.VMEM)
DMA = pltpu.SemaphoreType.DMA


def kernel_call(name, kernel, operands, outs, scratch=(), aliases=None):
    return pl.pallas_call(
        kernel,
        in_specs=[INSIDE if held else ANY for _, held in operands],
        out_specs=[INSIDE if held else ANY for _, _, held in outs],
        out_shape=[
            pltpu.VMEM(shape, kind) if held else jax.ShapeDtypeStruct(shape, kind)
            for shape, kind, held in outs
        ],
        scratch_shapes=list(scratch),
        input_output_aliases=aliases or {},
        compiler_params=pltpu.CompilerParams(vmem_limit_bytes=16 << 20),
        name=name,
    )(*[
        pltpu.with_memory_space_constraint(array, pltpu.VMEM if held else pltpu.HBM)
        for array, held in operands
    ])


def gelu_and_slope(v):
    square = v * v
    inner = v * (0.7978845608 + (0.7978845608 * 0.044715) * square)
    th = jnp.tanh(inner)
    half = 0.5 + 0.5 * th
    active = v * half
    inner_slope = 0.7978845608 + (3.0 * 0.7978845608 * 0.044715) * square
    slope = half + (0.5 * v) * (1.0 - th * th) * inner_slope
    return active, slope


def lanes(start, size):
    return pl.ds(pl.multiple_of(start, 128), size)


def dot(a, b):
    return jnp.dot(a, b, preferred_element_type=F32)


def turned_dot(a, b):
    return lax.dot_general(a, b, (((0,), (0,)), ((), ())), preferred_element_type=F32)


def odd_place():
    return lax.axis_index("ctx") % 2


def upstream_kernel(order, channels, near, pw_ref, cot_ref, x_ref, *rest):
    count = len(order)
    piece_refs, (end_ref, columns_ref, cot_in, sems) = rest[:count], rest[count:]
    ch, odd = lax.axis_index("ch"), odd_place()
    length, halo = x_ref.shape[1], end_ref.shape[1]
    whole = pltpu.make_async_copy(cot_ref, cot_in, sems.at[count])
    whole.start()
    blocks = []
    if channels % 128 == 0:
        for place, k in enumerate(order):
            blocks.append(pltpu.make_async_copy(
                pw_ref.at[:, lanes((ch ^ k) * channels, channels)],
                columns_ref.at[:, place * channels:(place + 1) * channels], sems.at[place],
            ))
    else:
        blocks.append(pltpu.make_async_copy(pw_ref, columns_ref, sems.at[0]))
    for block in blocks:
        block.start()
    at_end = 1 - odd if near else odd
    end = pltpu.make_async_copy(
        x_ref.at[:, lanes(at_end * (length - halo), halo)], end_ref, sems.at[count + 1]
    )
    end.start()
    whole.wait()
    if len(blocks) == count:
        for place in range(count):
            blocks[place].wait()
            columns = slice(place * channels, (place + 1) * channels)
            piece_refs[place][...] = turned_dot(columns_ref[:, columns], cot_in[...]).astype(BF16)
    else:
        blocks[0].wait()
        result = turned_dot(columns_ref[...], cot_in[...]).astype(BF16)
        for place in range(count):
            piece_refs[place][...] = result[place * channels:(place + 1) * channels]
    end.wait()


def columns_of(pw_weight, channels, order):
    if channels % 128 == 0:
        return pw_weight
    ch = lax.axis_index("ch")
    return jnp.concatenate(
        [lax.dynamic_slice_in_dim(pw_weight, (ch ^ k) * channels, channels, 1) for k in order], axis=1
    )


def upstream(pw_weight, cotangent, inputs, order, near):
    channels = inputs.shape[0]
    total, width = cotangent.shape
    count = len(order)
    results = kernel_call(
        "upstream", functools.partial(upstream_kernel, order, channels, near),
        [(columns_of(pw_weight, channels, order), False), (cotangent, False), (inputs, False)],
        [((channels, width), BF16, True)] * count + [((channels, DILATION_STEP), BF16, True)],
        [pltpu.VMEM((total, count * channels), BF16), pltpu.VMEM(cotangent.shape, BF16), DMA((count + 2,))],
    )
    return results[:count], results[count]


def convolve(w_ref, rows, wide, start, halo, unit):
    return sum(dot(w_ref[t, rows, :], wide[rows, lanes(start + t * halo, unit)]) for t in range(3))


def interior_kernel(n, x_ref, w_ref, *rest):
    active_refs, (slope_ref, wide, plain_ref, turned_ref, sem) = rest[:n], rest[n:]
    ch = lax.axis_index("ch")
    channels, length = x_ref.shape
    group = w_ref.shape[1]
    halo = DILATION_STEP
    block = length // n
    unit = min(block, 256)
    copy = pltpu.make_async_copy(x_ref, wide.at[:, halo:halo + length], sem)
    copy.start()
    groups = [slice(g, g + group) for g in range(0, channels, group)]
    for t in range(3):
        for rows in groups:
            square = w_ref[t, :, rows]
            turned_ref[2 - t, rows, :] = square
            plain_ref[t, rows, :] = square.T
    copy.wait()
    for k in range(n):
        base = (ch ^ k) * block

        @pl.when((base >= halo) & (base < length - halo))
        def _(k=k, base=base):
            for s in range(0, block, unit):
                for rows in groups:
                    active, slope = gelu_and_slope(convolve(plain_ref, rows, wide, base + s, halo, unit))
                    active_refs[k][rows, s:s + unit] = active.astype(BF16)
                    slope_ref[rows, lanes(base + s, unit)] = slope


def interior(inputs, weight, n):
    channels, length = inputs.shape
    group = weight.shape[1]
    block = length // n
    outs = [((channels, block), BF16, True)] * n
    outs += [((channels, length), F32, True), ((channels, length + 2 * DILATION_STEP), BF16, True)]
    outs += [((3, channels, group), BF16, True)] * 2
    results = kernel_call(
        "interior", functools.partial(interior_kernel, n), [(inputs, False), (weight, True)], outs, [DMA],
    )
    return results[:n], *results[n:]


def near_kernel(n, *refs):
    up_refs, near_ref, plain_ref, rest = refs[:n], refs[n], refs[n + 1], refs[n + 2 + n + 2:]
    active_refs, (slope_ref, wide, grad_ref, near_out) = rest[:n], rest[n:]
    ch, odd = lax.axis_index("ch"), odd_place()
    channels, length = slope_ref.shape
    group = plain_ref.shape[2]
    halo = near_ref.shape[1]
    block = length // n
    unit = min(block, 256)
    groups = [slice(g, g + group) for g in range(0, channels, group)]
    wide[:, lanes((1 - odd) * (halo + length), halo)] = near_ref[...]
    first, far = (1 - odd) * (length - halo), odd * (length - halo)
    for k in range(n):
        base = (ch ^ k) * block

        @pl.when((base >= first) & (base < first + halo))
        def _(k=k, base=base):
            for s in range(0, block, unit):
                for rows in groups:
                    active, slope = gelu_and_slope(convolve(plain_ref, rows, wide, base + s, halo, unit))
                    active_refs[k][rows, s:s + unit] = active.astype(BF16)
                    grad = (up_refs[k][rows, s:s + unit].astype(F32) * slope).astype(BF16)
                    grad_ref[rows, lanes(base + s, unit)] = grad
                    near_out[rows, lanes(base + s - first, unit)] = grad

        @pl.when((base >= halo) & (base < length - halo))
        def _(k=k, base=base):
            here = lanes(base, block)
            grad_ref[:, here] = (up_refs[k][...].astype(F32) * slope_ref[:, here]).astype(BF16)


def near_end(order, ups, near, plain, active, slope, wide):
    n = len(active)
    operands = [(o, True) for o in (*ups, near, plain, *active, slope, wide)]
    outs = [(a.shape, a.dtype, True) for a in (*active, slope, wide)]
    outs += [(slope.shape, BF16, True), (near.shape, BF16, True)]
    results = kernel_call(
        "near_end", functools.partial(near_kernel, n), operands, outs,
        aliases={n + 2 + i: i for i in range(n + 2)},
    )
    return results[:n], *results[n + 1:]


def far_kernel(n, far_ref, plain_ref, *rest):
    up_refs, rest = rest[:n], rest[n + n + 2:]
    active_refs, (wide, grad_ref, far_out) = rest[:n], rest[n:]
    ch, odd = lax.axis_index("ch"), odd_place()
    channels, length = grad_ref.shape
    group = plain_ref.shape[2]
    halo = far_ref.shape[1]
    block = length // n
    unit = min(block, 256)
    groups = [slice(g, g + group) for g in range(0, channels, group)]
    wide[:, lanes(odd * (halo + length), halo)] = far_ref[...]
    first = odd * (length - halo)
    for k in range(n):
        base = (ch ^ k) * block

        @pl.when((base >= first) & (base < first + halo))
        def _(k=k, base=base):
            for s in range(0, block, unit):
                for rows in groups:
                    active, slope = gelu_and_slope(convolve(plain_ref, rows, wide, base + s, halo, unit))
                    active_refs[k][rows, s:s + unit] = active.astype(BF16)
                    grad = (up_refs[k][rows, s:s + unit].astype(F32) * slope).astype(BF16)
                    grad_ref[rows, lanes(base + s, unit)] = grad
                    far_out[rows, lanes(base + s - first, unit)] = grad


def far_end(far, plain, ups, active, wide, grad):
    n = len(active)
    operands = [(o, True) for o in (far, plain, *ups, *active, wide, grad)]
    outs = [(a.shape, BF16, True) for a in (*active, wide, grad, far)]
    results = kernel_call(
        "far_end", functools.partial(far_kernel, n), operands, outs,
        aliases={2 + n + i: i for i in range(n + 2)},
    )
    return results[:n], *results[n + 1:]


def columns_times(order, pw_ref, rows, pieces):
    channels = pieces.shape[0] // len(order)
    if channels % 128 != 0:
        return dot(pw_ref[rows, :], pieces)
    return sum(
        dot(
            pw_ref[rows, lanes((lax.axis_index("ch") ^ k) * channels, channels)],
            pieces[place * channels:(place + 1) * channels],
        )
        for place, k in enumerate(order)
    )


def mix_kernel(order, pw_ref, *rest):
    piece_refs, before, sum_ref = rest[:len(order)], rest[len(order):-1], rest[-1]
    pieces = jnp.concatenate([p[...] for p in piece_refs], axis=0)
    step = 512
    for m in range(0, sum_ref.shape[0], step):
        rows = slice(m, m + step)
        part = columns_times(order, pw_ref, rows, pieces)
        sum_ref[rows, :] = part + before[0][rows, :] if before else part


def mix(name, pw_weight, order, active, before):
    channels, width = active[order[0]].shape
    operands = [columns_of(pw_weight, channels, order), *[active[k] for k in order], *before]
    return kernel_call(
        name, functools.partial(mix_kernel, order), [(o, True) for o in operands],
        [((pw_weight.shape[0], width), F32, True)],
        aliases={len(operands) - 1: 0} if before else {},
    )


def last_mix_kernel(order, pw_ref, sum_ref, *rest):
    piece_refs, (out_ref, done_ref, held, sems) = rest[:-4], rest[-4:]
    pieces = jnp.concatenate([p[...] for p in piece_refs], axis=0)
    step = 512
    copies = []
    for m in range(0, sum_ref.shape[0], step):
        rows = slice(m, m + step)
        held[rows, :] = (sum_ref[rows, :] + columns_times(order, pw_ref, rows, pieces)).astype(BF16)
        copies.append(pltpu.make_async_copy(held.at[rows, :], out_ref.at[rows, :], sems.at[len(copies)]))
        copies[-1].start()
    done_ref[...] = jnp.zeros_like(done_ref)
    for copy in copies:
        copy.wait()


def back(turned_ref, rows, taps):
    return sum(dot(turned_ref[t, rows, :], tap) for t, tap in enumerate(taps)).astype(BF16)


def back_interior_kernel(grad_ref, turned_ref, out_ref, held, sem):
    channels, length = grad_ref.shape
    group, halo, unit = turned_ref.shape[2], DILATION_STEP, 256
    for g in range(0, channels, group):
        rows = slice(g, g + group)
        for s in range(0, length - 2 * halo, unit):
            held[rows, s:s + unit] = back(
                turned_ref, rows, [grad_ref[rows, s + t * halo:s + t * halo + unit] for t in range(3)]
            )
    copy = pltpu.make_async_copy(held, out_ref.at[:, halo:length - halo], sem)
    copy.start()
    copy.wait()


def back_end_kernel(near, grad_ref, halo_ref, turned_ref, _, __, out_ref, held, sem):
    channels, length = grad_ref.shape
    group, halo, unit = turned_ref.shape[2], DILATION_STEP, 256
    odd = odd_place()
    for end in range(2):
        @pl.when(odd == (1 - end if near else end))
        def _(end=end):
            for g in range(0, channels, group):
                rows = slice(g, g + group)
                for s in range(0, halo, unit):
                    inner = (length - 2 * halo) * end + s
                    taps = [
                        grad_ref[rows, inner:inner + unit],
                        grad_ref[rows, inner + halo:inner + halo + unit],
                    ]
                    outer = halo_ref[rows, s:s + unit]
                    taps = taps + [outer] if end else [outer] + taps
                    held[rows, s:s + unit] = back(turned_ref, rows, taps)
    at_end = 1 - odd if near else odd
    copy = pltpu.make_async_copy(held, out_ref.at[:, lanes(at_end * (length - halo), halo)], sem)
    copy.start()
    copy.wait()


def back_end(name, near, grad, halo, turned, token, grad_inputs):
    operands = [(o, True) for o in (grad, halo, turned, token)] + [(grad_inputs, False)]
    return kernel_call(
        name, functools.partial(back_end_kernel, near), operands, [(grad_inputs.shape, BF16, False)],
        [pltpu.VMEM(halo.shape, BF16), DMA], {4: 0},
    )


def exchange(piece, k):
    if k == 0:
        return piece
    return lax.ppermute(piece, "ch", [(i, i ^ k) for i in range(lax.axis_size("ch"))])


def swap(values, first):
    size = lax.axis_size("ctx")
    pairs = [(i, i + 1) for i in range(first, size - 1, 2)]
    return lax.ppermute(values, "ctx", pairs + [(b, a) for a, b in pairs])


def body(inputs, conv_weight, pw_weight, cotangent):
    n = lax.axis_size("ch")
    channels, length = inputs.shape
    total, width = cotangent.shape
    halo = DILATION_STEP
    order = list(range(n - 1, -1, -1))
    parts = order[:n // 2], order[n // 2:]

    weight = lax.dynamic_slice_in_dim(
        jnp.swapaxes(conv_weight, 1, 2), lax.axis_index("ch") * channels, channels, 2
    )
    ups, halos = {}, []
    for place, part in enumerate(parts):
        pieces, end = upstream(pw_weight, cotangent, inputs, part, place == 0)
        ups.update({k: exchange(p, k) for k, p in zip(part, pieces)})
        halos.append(swap(end, place))
    ups = [ups[k] for k in range(n)]

    active, slope, wide, plain, turned = interior(inputs, weight, n)
    active, wide, grad, near_grad = near_end(order, ups, halos[0], plain, active, slope, wide)
    near_grad = swap(near_grad, 0)
    active, grad, far_grad = far_end(halos[1], plain, ups, active, wide, grad)
    active = {k: exchange(active[k], k) for k in order}
    far_grad = swap(far_grad, 1)

    (grad_inputs,) = kernel_call(
        "back_interior", back_interior_kernel, [(grad, True), (turned, True)],
        [((channels, length), BF16, False)], [pltpu.VMEM((channels, length - 2 * halo), BF16), DMA],
    )
    (grad_inputs,) = back_end("back_near", True, grad, near_grad, turned, turned, grad_inputs)
    early, late = parts[0][:n // 4], parts[0][n // 4:]
    partial = mix("half_mix", pw_weight, parts[1], active, [])
    partial = mix("more_mix", pw_weight, early, active, partial)
    mixed, done = kernel_call(
        "last_mix", functools.partial(last_mix_kernel, late),
        [(o, True) for o in (columns_of(pw_weight, channels, late), *partial, *[active[k] for k in late])],
        [((total, width), BF16, False), ((8, 128), F32, True)],
        [pltpu.VMEM((total, width), BF16), DMA((total // 512,))],
    )
    (grad_inputs,) = back_end("back_far", False, grad, far_grad, turned, done, grad_inputs)
    return mixed, grad_inputs


def solution(mesh):
    placed = (P("ch", "ctx"), P(), P(), P(None, ("ctx", "ch")))
    return jax.shard_map(
        body,
        mesh=mesh,
        in_specs=placed,
        out_specs=(P(None, ("ctx", "ch")), P("ch", "ctx")),
        check_vma=False,
    )
```

```python
import functools

import jax
import jax.numpy as jnp
from jax import lax
from jax.experimental import pallas as pl
from jax.experimental.pallas import tpu as pltpu
from jax.sharding import PartitionSpec as P

DILATION_STEP = 512
UPSTREAM_ROWS = 512
BF16, F32 = jnp.bfloat16, jnp.float32
ANY = pl.BlockSpec(memory_space=pl.ANY)
INSIDE = pl.BlockSpec(memory_space=pltpu.VMEM)
DMA = pltpu.SemaphoreType.DMA


def kernel_call(name, kernel, operands, outs, scratch=(), aliases=None):
    return pl.pallas_call(
        kernel,
        in_specs=[INSIDE if held else ANY for _, held in operands],
        out_specs=[INSIDE if held else ANY for _, _, held in outs],
        out_shape=[
            pltpu.VMEM(shape, kind) if held else jax.ShapeDtypeStruct(shape, kind)
            for shape, kind, held in outs
        ],
        scratch_shapes=list(scratch),
        input_output_aliases=aliases or {},
        compiler_params=pltpu.CompilerParams(vmem_limit_bytes=16 << 20),
        name=name,
    )(*[
        pltpu.with_memory_space_constraint(array, pltpu.VMEM if held else pltpu.HBM)
        for array, held in operands
    ])


def gelu_and_slope(v):
    square = v * v
    inner = v * (0.7978845608 + (0.7978845608 * 0.044715) * square)
    th = jnp.tanh(inner)
    half = 0.5 + 0.5 * th
    active = v * half
    inner_slope = 0.7978845608 + (3.0 * 0.7978845608 * 0.044715) * square
    slope = half + (0.5 * v) * (1.0 - th * th) * inner_slope
    return active, slope


def lanes(start, size):
    return pl.ds(pl.multiple_of(start, 128), size)


def dot(a, b):
    return jnp.dot(a, b, preferred_element_type=F32)


def turned_dot(a, b):
    return lax.dot_general(a, b, (((0,), (0,)), ((), ())), preferred_element_type=F32)


def odd_place():
    return lax.axis_index("ctx") % 2


def upstream_kernel(order, channels, near, pw_ref, cot_ref, x_ref, *rest):
    count = len(order)
    piece_refs, (end_ref, columns_ref, cot_in, total_ref, sems) = rest[:count], rest[count:]
    ch, odd = lax.axis_index("ch"), odd_place()
    length, halo = x_ref.shape[1], end_ref.shape[1]
    blocks = []
    for m in range(0, cot_in.shape[0], UPSTREAM_ROWS):
        rows = slice(m, m + UPSTREAM_ROWS)
        pairs = [(cot_ref.at[rows], cot_in.at[rows])]
        if channels % 128 == 0:
            for place, k in enumerate(order):
                columns = lanes((ch ^ k) * channels, channels)
                held = slice(place * channels, (place + 1) * channels)
                pairs.append((pw_ref.at[rows, columns], columns_ref.at[rows, held]))
        else:
            pairs.append((pw_ref.at[rows], columns_ref.at[rows]))
        copies = [
            pltpu.make_async_copy(source, place, sems.at[len(blocks), i])
            for i, (source, place) in enumerate(pairs)
        ]
        for copy in copies:
            copy.start()
        blocks.append((rows, copies))
    at_end = 1 - odd if near else odd
    end = pltpu.make_async_copy(
        x_ref.at[:, lanes(at_end * (length - halo), halo)], end_ref, sems.at[0, count + 1]
    )
    end.start()
    for step, (rows, copies) in enumerate(blocks):
        for copy in copies:
            copy.wait()
        for place in range(count):
            held = slice(place * channels, (place + 1) * channels)
            part = turned_dot(columns_ref[rows, held], cot_in[rows, :])
            if step > 0:
                part = part + total_ref[held, :]
            if step < len(blocks) - 1:
                total_ref[held, :] = part
            else:
                piece_refs[place][...] = part.astype(BF16)
    end.wait()


def columns_of(pw_weight, channels, order):
    if channels % 128 == 0:
        return pw_weight
    ch = lax.axis_index("ch")
    return jnp.concatenate(
        [lax.dynamic_slice_in_dim(pw_weight, (ch ^ k) * channels, channels, 1) for k in order], axis=1
    )


def upstream(pw_weight, cotangent, inputs, order, near):
    channels = inputs.shape[0]
    total, width = cotangent.shape
    count = len(order)
    results = kernel_call(
        "upstream", functools.partial(upstream_kernel, order, channels, near),
        [(columns_of(pw_weight, channels, order), False), (cotangent, False), (inputs, False)],
        [((channels, width), BF16, True)] * count + [((channels, DILATION_STEP), BF16, True)],
        [
            pltpu.VMEM((total, count * channels), BF16), pltpu.VMEM(cotangent.shape, BF16),
            pltpu.VMEM((count * channels, width), F32), DMA((total // UPSTREAM_ROWS, count + 2)),
        ],
    )
    return results[:count], results[count]


def convolve(w_ref, rows, wide, start, halo, unit):
    return sum(dot(w_ref[t, rows, :], wide[rows, lanes(start + t * halo, unit)]) for t in range(3))


def interior_kernel(n, x_ref, w_ref, *rest):
    active_refs, (slope_ref, wide, plain_ref, turned_ref, sem) = rest[:n], rest[n:]
    ch = lax.axis_index("ch")
    channels, length = x_ref.shape
    group = w_ref.shape[1]
    halo = DILATION_STEP
    block = length // n
    unit = min(block, 256)
    copy = pltpu.make_async_copy(x_ref, wide.at[:, halo:halo + length], sem)
    copy.start()
    groups = [slice(g, g + group) for g in range(0, channels, group)]
    for t in range(3):
        for rows in groups:
            square = w_ref[t, :, rows]
            turned_ref[2 - t, rows, :] = square
            plain_ref[t, rows, :] = square.T
    copy.wait()
    for k in range(n):
        base = (ch ^ k) * block

        @pl.when((base >= halo) & (base < length - halo))
        def _(k=k, base=base):
            for s in range(0, block, unit):
                for rows in groups:
                    active, slope = gelu_and_slope(convolve(plain_ref, rows, wide, base + s, halo, unit))
                    active_refs[k][rows, s:s + unit] = active.astype(BF16)
                    slope_ref[rows, lanes(base + s, unit)] = slope


def interior(inputs, weight, n):
    channels, length = inputs.shape
    group = weight.shape[1]
    block = length // n
    outs = [((channels, block), BF16, True)] * n
    outs += [((channels, length), F32, True), ((channels, length + 2 * DILATION_STEP), BF16, True)]
    outs += [((3, channels, group), BF16, True)] * 2
    results = kernel_call(
        "interior", functools.partial(interior_kernel, n), [(inputs, False), (weight, True)], outs, [DMA],
    )
    return results[:n], *results[n:]


def near_kernel(order, n, *refs):
    up_refs = {k: refs[i + (i > 0)] for i, k in enumerate(order)}
    near_ref, plain_ref, rest = refs[1], refs[n + 1], refs[n + 2 + n + 2:]
    active_refs, (slope_ref, wide, grad_ref) = rest[:n], rest[n:]
    ch, odd = lax.axis_index("ch"), odd_place()
    channels, length = slope_ref.shape
    group = plain_ref.shape[2]
    halo = near_ref.shape[1]
    block = length // n
    unit = min(block, 256)
    groups = [slice(g, g + group) for g in range(0, channels, group)]
    wide[:, lanes((1 - odd) * (halo + length), halo)] = near_ref[...]
    first, far = (1 - odd) * (length - halo), odd * (length - halo)
    for k in range(n):
        base = (ch ^ k) * block

        @pl.when((base >= first) & (base < first + halo))
        def _(k=k, base=base):
            for s in range(0, block, unit):
                for rows in groups:
                    active, slope = gelu_and_slope(convolve(plain_ref, rows, wide, base + s, halo, unit))
                    active_refs[k][rows, s:s + unit] = active.astype(BF16)
                    grad_ref[rows, lanes(base + s, unit)] = (
                        up_refs[k][rows, s:s + unit].astype(F32) * slope
                    ).astype(BF16)

        @pl.when((base >= halo) & (base < length - halo))
        def _(k=k, base=base):
            here = lanes(base, block)
            grad_ref[:, here] = (up_refs[k][...].astype(F32) * slope_ref[:, here]).astype(BF16)


def near_end(order, ups, near, plain, active, slope, wide):
    n = len(active)
    lead = [ups[k] for k in order]
    operands = [(o, True) for o in (lead[0], near, *lead[1:], plain, *active, slope, wide)]
    outs = [(a.shape, a.dtype, True) for a in (*active, slope, wide)] + [(slope.shape, BF16, True)]
    results = kernel_call(
        "near_end", functools.partial(near_kernel, order, n), operands, outs,
        aliases={n + 2 + i: i for i in range(n + 2)},
    )
    return results[:n], *results[n + 1:]


def far_kernel(n, far_ref, plain_ref, *rest):
    up_refs, rest = rest[:n], rest[n + n + 2:]
    active_refs, (wide, grad_ref, near_out, far_out) = rest[:n], rest[n:]
    ch, odd = lax.axis_index("ch"), odd_place()
    channels, length = grad_ref.shape
    group = plain_ref.shape[2]
    halo = far_ref.shape[1]
    block = length // n
    unit = min(block, 256)
    groups = [slice(g, g + group) for g in range(0, channels, group)]
    wide[:, lanes(odd * (halo + length), halo)] = far_ref[...]
    first = odd * (length - halo)
    for k in range(n):
        base = (ch ^ k) * block

        @pl.when((base >= first) & (base < first + halo))
        def _(k=k, base=base):
            for s in range(0, block, unit):
                for rows in groups:
                    active, slope = gelu_and_slope(convolve(plain_ref, rows, wide, base + s, halo, unit))
                    active_refs[k][rows, s:s + unit] = active.astype(BF16)
                    grad = (up_refs[k][rows, s:s + unit].astype(F32) * slope).astype(BF16)
                    grad_ref[rows, lanes(base + s, unit)] = grad
                    far_out[rows, lanes(base + s - first, unit)] = grad
    near_out[...] = grad_ref[:, lanes((1 - odd) * (length - halo), halo)]


def far_end(far, plain, ups, active, wide, grad):
    n = len(active)
    operands = [(o, True) for o in (far, plain, *ups, *active, wide, grad)]
    outs = [(a.shape, BF16, True) for a in (*active, wide, grad, far, far)]
    results = kernel_call(
        "far_end", functools.partial(far_kernel, n), operands, outs,
        aliases={2 + n + i: i for i in range(n + 2)},
    )
    return results[:n], *results[n + 1:]


def columns_times(order, pw_ref, rows, pieces):
    channels = pieces.shape[0] // len(order)
    if channels % 128 != 0:
        return dot(pw_ref[rows, :], pieces)
    return sum(
        dot(
            pw_ref[rows, lanes((lax.axis_index("ch") ^ k) * channels, channels)],
            pieces[place * channels:(place + 1) * channels],
        )
        for place, k in enumerate(order)
    )


def mix_kernel(order, pw_ref, *rest):
    piece_refs, before, sum_ref = rest[:len(order)], rest[len(order):-1], rest[-1]
    pieces = jnp.concatenate([p[...] for p in piece_refs], axis=0)
    step = 512
    for m in range(0, sum_ref.shape[0], step):
        rows = slice(m, m + step)
        part = columns_times(order, pw_ref, rows, pieces)
        sum_ref[rows, :] = part + before[0][rows, :] if before else part


def mix(name, pw_weight, order, active, before):
    channels, width = active[order[0]].shape
    operands = [columns_of(pw_weight, channels, order), *[active[k] for k in order], *before]
    return kernel_call(
        name, functools.partial(mix_kernel, order), [(o, True) for o in operands],
        [((pw_weight.shape[0], width), F32, True)],
        aliases={len(operands) - 1: 0} if before else {},
    )


def back(turned_ref, rows, taps):
    return sum(dot(turned_ref[t, rows, :], tap) for t, tap in enumerate(taps)).astype(BF16)


def back_interior_kernel(grad_ref, turned_ref, out_ref, held, sem):
    channels, length = grad_ref.shape
    group, halo, unit = turned_ref.shape[2], DILATION_STEP, 256
    for g in range(0, channels, group):
        rows = slice(g, g + group)
        for s in range(0, length - 2 * halo, unit):
            held[rows, s:s + unit] = back(
                turned_ref, rows, [grad_ref[rows, s + t * halo:s + t * halo + unit] for t in range(3)]
            )
    copy = pltpu.make_async_copy(held, out_ref.at[:, halo:length - halo], sem)
    copy.start()
    copy.wait()


def tail_kernel(order, pw_ref, sum_ref, *rest):
    piece_refs, rest = rest[:len(order)], rest[len(order):]
    grad_ref, near_ref, far_ref, turned_ref, _, mixed_ref, out_ref, held, ends, halos, sems = rest
    channels, length = grad_ref.shape
    group, halo, unit = turned_ref.shape[2], DILATION_STEP, 256
    pieces = jnp.concatenate([p[...] for p in piece_refs], axis=0)
    copies = []

    def send(source, place):
        copies.append(pltpu.make_async_copy(source, place, sems.at[len(copies)]))
        copies[-1].start()

    step = 512
    for m in range(0, sum_ref.shape[0], step):
        rows = slice(m, m + step)
        held[rows, :] = (sum_ref[rows, :] + columns_times(order, pw_ref, rows, pieces)).astype(BF16)
        send(held.at[rows, :], mixed_ref.at[rows, :])
    odd = odd_place()
    halos[:, lanes((1 - odd) * halo, halo)] = near_ref[...]
    halos[:, lanes(odd * halo, halo)] = far_ref[...]
    for end in range(2):
        for g in range(0, channels, group):
            rows = slice(g, g + group)
            for s in range(0, halo, unit):
                inner = (length - 2 * halo) * end + s
                taps = [
                    grad_ref[rows, inner:inner + unit],
                    grad_ref[rows, inner + halo:inner + halo + unit],
                ]
                outer = halos[rows, end * halo + s:end * halo + s + unit]
                taps = taps + [outer] if end else [outer] + taps
                ends[rows, end * halo + s:end * halo + s + unit] = back(turned_ref, rows, taps)
        send(
            ends.at[:, end * halo:(end + 1) * halo],
            out_ref.at[:, end * (length - halo):end * (length - halo) + halo],
        )
    for copy in copies:
        copy.wait()


def tail(pw_weight, order, partial, active, grad, near, far, turned, grad_inputs):
    channels, halo = near.shape
    operands = [columns_of(pw_weight, channels, order), partial, *[active[k] for k in order]]
    operands = [(o, True) for o in (*operands, grad, near, far, turned)] + [(grad_inputs, False)]
    return kernel_call(
        "tail", functools.partial(tail_kernel, order), operands,
        [(partial.shape, BF16, False), (grad_inputs.shape, BF16, False)],
        [pltpu.VMEM(partial.shape, BF16)] + [pltpu.VMEM((channels, 2 * halo), BF16)] * 2
        + [DMA((partial.shape[0] // 512 + 2,))],
        {len(operands) - 1: 1},
    )


def exchange(piece, k):
    if k == 0:
        return piece
    return lax.ppermute(piece, "ch", [(i, i ^ k) for i in range(lax.axis_size("ch"))])


def swap(values, first):
    size = lax.axis_size("ctx")
    pairs = [(i, i + 1) for i in range(first, size - 1, 2)]
    return lax.ppermute(values, "ctx", pairs + [(b, a) for a, b in pairs])


def body(inputs, conv_weight, pw_weight, cotangent):
    n = lax.axis_size("ch")
    channels, length = inputs.shape
    halo = DILATION_STEP
    order = list(range(n - 1, -1, -1))
    parts = order[:n // 2], order[n // 2:]

    weight = lax.dynamic_slice_in_dim(
        jnp.swapaxes(conv_weight, 1, 2), lax.axis_index("ch") * channels, channels, 2
    )
    ups, halos = {}, []
    for place, part in enumerate(parts):
        pieces, end = upstream(pw_weight, cotangent, inputs, part, place == 0)
        ups.update({k: exchange(p, k) for k, p in zip(part, pieces)})
        halos.append(swap(end, place))
    ups = [ups[k] for k in range(n)]

    active, slope, wide, plain, turned = interior(inputs, weight, n)
    active, wide, grad = near_end(order, ups, halos[0], plain, active, slope, wide)
    active, grad, near_grad, far_grad = far_end(halos[1], plain, ups, active, wide, grad)
    active = {k: exchange(active[k], k) for k in order}
    near_grad, far_grad = swap(near_grad, 0), swap(far_grad, 1)

    (grad_inputs,) = kernel_call(
        "back_interior", back_interior_kernel, [(grad, True), (turned, True)],
        [((channels, length), BF16, False)], [pltpu.VMEM((channels, length - 2 * halo), BF16), DMA],
    )
    early, late = parts[0][:n // 4], parts[0][n // 4:]
    partial = mix("early_mix", pw_weight, early, active, [])
    (partial,) = mix("half_mix", pw_weight, parts[1], active, partial)
    return tuple(tail(pw_weight, late, partial, active, grad, near_grad, far_grad, turned, grad_inputs))


def solution(mesh):
    placed = (P("ch", "ctx"), P(), P(), P(None, ("ctx", "ch")))
    return jax.shard_map(
        body,
        mesh=mesh,
        in_specs=placed,
        out_specs=(P(None, ("ctx", "ch")), P("ch", "ctx")),
        check_vma=False,
    )
```

```python
import functools

import jax
import jax.numpy as jnp
from jax import lax
from jax.experimental import pallas as pl
from jax.experimental.pallas import tpu as pltpu
from jax.sharding import PartitionSpec as P

DILATION_STEP = 512
UPSTREAM_ROWS = 512
BF16, F32 = jnp.bfloat16, jnp.float32
ANY = pl.BlockSpec(memory_space=pl.ANY)
INSIDE = pl.BlockSpec(memory_space=pltpu.VMEM)
DMA = pltpu.SemaphoreType.DMA


def kernel_call(name, kernel, operands, outs, scratch=(), aliases=None):
    return pl.pallas_call(
        kernel,
        in_specs=[INSIDE if held else ANY for _, held in operands],
        out_specs=[INSIDE if held else ANY for _, _, held in outs],
        out_shape=[
            pltpu.VMEM(shape, kind) if held else jax.ShapeDtypeStruct(shape, kind)
            for shape, kind, held in outs
        ],
        scratch_shapes=list(scratch),
        input_output_aliases=aliases or {},
        compiler_params=pltpu.CompilerParams(vmem_limit_bytes=16 << 20),
        name=name,
    )(*[
        pltpu.with_memory_space_constraint(array, pltpu.VMEM if held else pltpu.HBM)
        for array, held in operands
    ])


def gelu_and_slope(v):
    square = v * v
    inner = v * (0.7978845608 + (0.7978845608 * 0.044715) * square)
    th = jnp.tanh(inner)
    half = 0.5 + 0.5 * th
    active = v * half
    inner_slope = 0.7978845608 + (3.0 * 0.7978845608 * 0.044715) * square
    slope = half + (0.5 * v) * (1.0 - th * th) * inner_slope
    return active, slope


def lanes(start, size):
    return pl.ds(pl.multiple_of(start, 128), size)


def dot(a, b):
    return jnp.dot(a, b, preferred_element_type=F32)


def turned_dot(a, b):
    return lax.dot_general(a, b, (((0,), (0,)), ((), ())), preferred_element_type=F32)


def odd_place():
    return lax.axis_index("ctx") % 2


def upstream_kernel(order, channels, near, far, pw_ref, cot_ref, x_ref, *rest):
    count = len(order)
    piece_refs, rest = rest[:count], rest[count:]
    columns_ref, total_ref, sems = rest[-3:]
    cot_in = rest[0] if near else cot_ref
    ch, odd = lax.axis_index("ch"), odd_place()
    blocks = []
    for m in range(0, cot_in.shape[0], UPSTREAM_ROWS):
        rows = slice(m, m + UPSTREAM_ROWS)
        pairs = [(cot_ref.at[rows], cot_in.at[rows])] if near else []
        if channels % 128 == 0:
            for place, k in enumerate(order):
                columns = lanes((ch ^ k) * channels, channels)
                held = slice(place * channels, (place + 1) * channels)
                pairs.append((pw_ref.at[rows, columns], columns_ref.at[rows, held]))
        else:
            pairs.append((pw_ref.at[rows], columns_ref.at[rows]))
        copies = [
            pltpu.make_async_copy(source, place, sems.at[len(blocks), i])
            for i, (source, place) in enumerate(pairs)
        ]
        for copy in copies:
            copy.start()
        blocks.append((rows, copies))
    end = None
    if near or far:
        end_ref = rest[-4]
        length, halo = x_ref.shape[1], end_ref.shape[1]
        at_end = 1 - odd if near else odd
        end = pltpu.make_async_copy(
            x_ref.at[:, lanes(at_end * (length - halo), halo)], end_ref, sems.at[0, count + 1]
        )
        end.start()
    for step, (rows, copies) in enumerate(blocks):
        for copy in copies:
            copy.wait()
        for place in range(count):
            held = slice(place * channels, (place + 1) * channels)
            part = turned_dot(columns_ref[rows, held], cot_in[rows, :])
            if step > 0:
                part = part + total_ref[held, :]
            if step < len(blocks) - 1:
                total_ref[held, :] = part
            else:
                piece_refs[place][...] = part.astype(BF16)
    if end is not None:
        end.wait()


def columns_of(pw_weight, channels, order):
    if channels % 128 == 0:
        return pw_weight
    ch = lax.axis_index("ch")
    return jnp.concatenate(
        [lax.dynamic_slice_in_dim(pw_weight, (ch ^ k) * channels, channels, 1) for k in order], axis=1
    )


def upstream(pw_weight, cotangent, inputs, order, near, far):
    channels = inputs.shape[0]
    total, width = cotangent.shape
    count = len(order)
    outs = [((channels, width), BF16, True)] * count
    outs += [(cotangent.shape, BF16, True)] * near + [((channels, DILATION_STEP), BF16, True)] * (near or far)
    results = kernel_call(
        "upstream", functools.partial(upstream_kernel, order, channels, near, far),
        [(columns_of(pw_weight, channels, order), False), (cotangent, not near), (inputs, False)], outs,
        [
            pltpu.VMEM((total, count * channels), BF16), pltpu.VMEM((count * channels, width), F32),
            DMA((total // UPSTREAM_ROWS, count + 2)),
        ],
    )
    return results[:count], *results[count:]


def convolve(w_ref, rows, wide, start, halo, unit):
    return sum(dot(w_ref[t, rows, :], wide[rows, lanes(start + t * halo, unit)]) for t in range(3))


def interior_kernel(n, x_ref, w_ref, *rest):
    active_refs, (slope_ref, wide, plain_ref, turned_ref, sem) = rest[:n], rest[n:]
    ch = lax.axis_index("ch")
    channels, length = x_ref.shape
    group = w_ref.shape[1]
    halo = DILATION_STEP
    block = length // n
    unit = min(block, 256)
    copy = pltpu.make_async_copy(x_ref, wide.at[:, halo:halo + length], sem)
    copy.start()
    groups = [slice(g, g + group) for g in range(0, channels, group)]
    for t in range(3):
        for rows in groups:
            square = w_ref[t, :, rows]
            turned_ref[2 - t, rows, :] = square
            plain_ref[t, rows, :] = square.T
    copy.wait()
    for k in range(n):
        base = (ch ^ k) * block

        @pl.when((base >= halo) & (base < length - halo))
        def _(k=k, base=base):
            for s in range(0, block, unit):
                for rows in groups:
                    active, slope = gelu_and_slope(convolve(plain_ref, rows, wide, base + s, halo, unit))
                    active_refs[k][rows, s:s + unit] = active.astype(BF16)
                    slope_ref[rows, lanes(base + s, unit)] = slope


def interior(inputs, weight, n):
    channels, length = inputs.shape
    group = weight.shape[1]
    block = length // n
    outs = [((channels, block), BF16, True)] * n
    outs += [((channels, length), F32, True), ((channels, length + 2 * DILATION_STEP), BF16, True)]
    outs += [((3, channels, group), BF16, True)] * 2
    results = kernel_call(
        "interior", functools.partial(interior_kernel, n), [(inputs, False), (weight, True)], outs, [DMA],
    )
    return results[:n], *results[n:]


def ends_kernel(n, _, near_ref, __, far_ref, plain_ref, *rest):
    active_refs, (slope_ref, wide) = rest[n + 2:n + 2 + n], rest[n + 2 + n:]
    ch, odd = lax.axis_index("ch"), odd_place()
    channels, length = slope_ref.shape
    group = plain_ref.shape[2]
    halo = near_ref.shape[1]
    block = length // n
    unit = min(block, 256)
    groups = [slice(g, g + group) for g in range(0, channels, group)]
    wide[:, lanes((1 - odd) * (halo + length), halo)] = near_ref[...]
    wide[:, lanes(odd * (halo + length), halo)] = far_ref[...]
    for k in range(n):
        base = (ch ^ k) * block

        @pl.when((base < halo) | (base >= length - halo))
        def _(k=k, base=base):
            for s in range(0, block, unit):
                for rows in groups:
                    active, slope = gelu_and_slope(convolve(plain_ref, rows, wide, base + s, halo, unit))
                    active_refs[k][rows, s:s + unit] = active.astype(BF16)
                    slope_ref[rows, lanes(base + s, unit)] = slope


def both_ends(first, near, second, far, plain, active, slope, wide):
    n = len(active)
    operands = [(o, True) for o in (first, near, second, far, plain, *active, slope, wide)]
    results = kernel_call(
        "ends", functools.partial(ends_kernel, n), operands,
        [(a.shape, a.dtype, True) for a in (*active, slope, wide)],
        aliases={5 + i: i for i in range(n + 2)},
    )
    return results[:n], results[n]


def grad_kernel(order, slope_ref, *rest):
    up_refs, (grad_ref, near_out, far_out) = rest[:-3], rest[-3:]
    ch, odd = lax.axis_index("ch"), odd_place()
    length, halo = grad_ref.shape[1], near_out.shape[1]
    block = up_refs[0].shape[1]
    for k, up_ref in zip(order, up_refs):
        here = lanes((ch ^ k) * block, block)
        grad_ref[:, here] = (up_ref[...].astype(F32) * slope_ref[:, here]).astype(BF16)
    near_out[...] = grad_ref[:, lanes((1 - odd) * (length - halo), halo)]
    far_out[...] = grad_ref[:, lanes(odd * (length - halo), halo)]


def grad_conv(slope, order, ups):
    channels = slope.shape[0]
    return kernel_call(
        "grad_conv", functools.partial(grad_kernel, order),
        [(o, True) for o in (slope, *[ups[k] for k in order])],
        [(slope.shape, BF16, True)] + [((channels, DILATION_STEP), BF16, True)] * 2,
    )


def columns_times(order, pw_ref, rows, pieces):
    channels = pieces.shape[0] // len(order)
    if channels % 128 != 0:
        return dot(pw_ref[rows, :], pieces)
    return sum(
        dot(
            pw_ref[rows, lanes((lax.axis_index("ch") ^ k) * channels, channels)],
            pieces[place * channels:(place + 1) * channels],
        )
        for place, k in enumerate(order)
    )


def mix_kernel(order, pw_ref, *rest):
    piece_refs, before, sum_ref = rest[:len(order)], rest[len(order):-1], rest[-1]
    pieces = jnp.concatenate([p[...] for p in piece_refs], axis=0)
    step = 512
    for m in range(0, sum_ref.shape[0], step):
        rows = slice(m, m + step)
        part = columns_times(order, pw_ref, rows, pieces)
        sum_ref[rows, :] = part + before[0][rows, :] if before else part


def mix(name, pw_weight, order, active, before):
    channels, width = active[order[0]].shape
    operands = [columns_of(pw_weight, channels, order), *[active[k] for k in order], *before]
    return kernel_call(
        name, functools.partial(mix_kernel, order), [(o, True) for o in operands],
        [((pw_weight.shape[0], width), F32, True)],
        aliases={len(operands) - 1: 0} if before else {},
    )


def back(turned_ref, rows, taps):
    return sum(dot(turned_ref[t, rows, :], tap) for t, tap in enumerate(taps)).astype(BF16)


def back_interior_kernel(grad_ref, turned_ref, out_ref, held, sem):
    channels, length = grad_ref.shape
    group, halo, unit = turned_ref.shape[2], DILATION_STEP, 256
    for g in range(0, channels, group):
        rows = slice(g, g + group)
        for s in range(0, length - 2 * halo, unit):
            held[rows, s:s + unit] = back(
                turned_ref, rows, [grad_ref[rows, s + t * halo:s + t * halo + unit] for t in range(3)]
            )
    copy = pltpu.make_async_copy(held, out_ref.at[:, halo:length - halo], sem)
    copy.start()
    copy.wait()


def tail_kernel(order, pw_ref, sum_ref, near_ref, *rest):
    piece_refs, rest = rest[:len(order)], rest[len(order):]
    far_ref, grad_ref, turned_ref, _, mixed_ref, out_ref, held, ends, halos, sems = rest
    channels, length = grad_ref.shape
    group, halo, unit = turned_ref.shape[2], DILATION_STEP, 256
    pieces = jnp.concatenate([p[...] for p in piece_refs], axis=0)
    copies = []

    def send(source, place):
        copies.append(pltpu.make_async_copy(source, place, sems.at[len(copies)]))
        copies[-1].start()

    step = 512
    for m in range(0, sum_ref.shape[0], step):
        rows = slice(m, m + step)
        held[rows, :] = (sum_ref[rows, :] + columns_times(order, pw_ref, rows, pieces)).astype(BF16)
        send(held.at[rows, :], mixed_ref.at[rows, :])
    odd = odd_place()
    halos[:, lanes((1 - odd) * halo, halo)] = near_ref[...]
    halos[:, lanes(odd * halo, halo)] = far_ref[...]
    for end in range(2):
        for g in range(0, channels, group):
            rows = slice(g, g + group)
            for s in range(0, halo, unit):
                inner = (length - 2 * halo) * end + s
                taps = [
                    grad_ref[rows, inner:inner + unit],
                    grad_ref[rows, inner + halo:inner + halo + unit],
                ]
                outer = halos[rows, end * halo + s:end * halo + s + unit]
                taps = taps + [outer] if end else [outer] + taps
                ends[rows, end * halo + s:end * halo + s + unit] = back(turned_ref, rows, taps)
        send(
            ends.at[:, end * halo:(end + 1) * halo],
            out_ref.at[:, end * (length - halo):end * (length - halo) + halo],
        )
    for copy in copies:
        copy.wait()


def tail(pw_weight, order, partial, active, grad, near, far, turned, grad_inputs):
    channels, halo = near.shape
    operands = [columns_of(pw_weight, channels, order), partial, near, *[active[k] for k in order]]
    operands = [(o, True) for o in (*operands, far, grad, turned)] + [(grad_inputs, False)]
    return kernel_call(
        "tail", functools.partial(tail_kernel, order), operands,
        [(partial.shape, BF16, False), (grad_inputs.shape, BF16, False)],
        [pltpu.VMEM(partial.shape, BF16)] + [pltpu.VMEM((channels, 2 * halo), BF16)] * 2
        + [DMA((partial.shape[0] // 512 + 2,))],
        {len(operands) - 1: 1},
    )


def exchange(piece, k):
    if k == 0:
        return piece
    return lax.ppermute(piece, "ch", [(i, i ^ k) for i in range(lax.axis_size("ch"))])


def swap(values, first):
    size = lax.axis_size("ctx")
    pairs = [(i, i + 1) for i in range(first, size - 1, 2)]
    return lax.ppermute(values, "ctx", pairs + [(b, a) for a, b in pairs])


def body(inputs, conv_weight, pw_weight, cotangent):
    n = lax.axis_size("ch")
    channels, length = inputs.shape
    halo = DILATION_STEP
    order = list(range(n - 1, -1, -1))
    first, second, rest = order[:n // 4], order[n // 4:n // 2], order[n // 2:]

    weight = lax.dynamic_slice_in_dim(
        jnp.swapaxes(conv_weight, 1, 2), lax.axis_index("ch") * channels, channels, 2
    )
    pieces, cot_in, near = upstream(pw_weight, cotangent, inputs, first, True, False)
    ups = {k: exchange(p, k) for k, p in zip(first, pieces)}
    near = swap(near, 0)
    pieces, far = upstream(pw_weight, cot_in, inputs, second, False, True)
    ups.update({k: exchange(p, k) for k, p in zip(second, pieces)})
    far = swap(far, 1)
    (pieces,) = upstream(pw_weight, cot_in, inputs, rest, False, False)
    ups.update({k: exchange(p, k) for k, p in zip(rest, pieces)})

    active, slope, wide, plain, turned = interior(inputs, weight, n)
    active, slope = both_ends(ups[first[0]], near, ups[second[0]], far, plain, active, slope, wide)
    grad, near_grad, far_grad = grad_conv(slope, order, ups)
    active = {k: exchange(active[k], k) for k in order}
    near_grad, far_grad = swap(near_grad, 0), swap(far_grad, 1)

    (grad_inputs,) = kernel_call(
        "back_interior", back_interior_kernel, [(grad, True), (turned, True)],
        [((channels, length), BF16, False)], [pltpu.VMEM((channels, length - 2 * halo), BF16), DMA],
    )
    partial = mix("early_mix", pw_weight, first, active, [])
    (partial,) = mix("half_mix", pw_weight, rest, active, partial)
    return tuple(tail(pw_weight, second, partial, active, grad, near_grad, far_grad, turned, grad_inputs))


def solution(mesh):
    placed = (P("ch", "ctx"), P(), P(), P(None, ("ctx", "ch")))
    return jax.shard_map(
        body,
        mesh=mesh,
        in_specs=placed,
        out_specs=(P(None, ("ctx", "ch")), P("ch", "ctx")),
        check_vma=False,
    )
```

```python
import functools

import jax
import jax.numpy as jnp
from jax import lax
from jax.experimental import pallas as pl
from jax.experimental.pallas import tpu as pltpu
from jax.sharding import PartitionSpec as P

DILATION_STEP = 512
UPSTREAM_ROWS = 512
BF16, F32 = jnp.bfloat16, jnp.float32
ANY = pl.BlockSpec(memory_space=pl.ANY)
INSIDE = pl.BlockSpec(memory_space=pltpu.VMEM)
DMA = pltpu.SemaphoreType.DMA


def kernel_call(name, kernel, operands, outs, scratch=(), aliases=None):
    return pl.pallas_call(
        kernel,
        in_specs=[INSIDE if held else ANY for _, held in operands],
        out_specs=[INSIDE if held else ANY for _, _, held in outs],
        out_shape=[
            pltpu.VMEM(shape, kind) if held else jax.ShapeDtypeStruct(shape, kind)
            for shape, kind, held in outs
        ],
        scratch_shapes=list(scratch),
        input_output_aliases=aliases or {},
        compiler_params=pltpu.CompilerParams(vmem_limit_bytes=16 << 20),
        name=name,
    )(*[
        pltpu.with_memory_space_constraint(array, pltpu.VMEM if held else pltpu.HBM)
        for array, held in operands
    ])


def gelu_and_slope(v):
    square = v * v
    inner = v * (0.7978845608 + (0.7978845608 * 0.044715) * square)
    th = jnp.tanh(inner)
    half = 0.5 + 0.5 * th
    active = v * half
    inner_slope = 0.7978845608 + (3.0 * 0.7978845608 * 0.044715) * square
    slope = half + (0.5 * v) * (1.0 - th * th) * inner_slope
    return active, slope


def lanes(start, size):
    return pl.ds(pl.multiple_of(start, 128), size)


def dot(a, b):
    return jnp.dot(a, b, preferred_element_type=F32)


def turned_dot(a, b):
    return lax.dot_general(a, b, (((0,), (0,)), ((), ())), preferred_element_type=F32)


def odd_place():
    return lax.axis_index("ctx") % 2


def end_copy(x_ref, end_ref, which, sem):
    length, halo = x_ref.shape[1], end_ref.shape[1]
    return pltpu.make_async_copy(x_ref.at[:, lanes(which * (length - halo), halo)], end_ref, sem)


def near_source_kernel(x_ref, near_ref, sem):
    copy = end_copy(x_ref, near_ref, 1 - odd_place(), sem)
    copy.start()
    copy.wait()


def upstream_kernel(order, channels, first, with_far, pw_ref, cot_ref, x_ref, *rest):
    count = len(order)
    piece_refs, rest = rest[:count], rest[count:]
    columns_ref, total_ref, sems = rest[-3:]
    cot_in = rest[0] if first else cot_ref
    ch = lax.axis_index("ch")
    blocks = []
    for m in range(0, cot_in.shape[0], UPSTREAM_ROWS):
        rows = slice(m, m + UPSTREAM_ROWS)
        pairs = [(cot_ref.at[rows], cot_in.at[rows])] if first else []
        if channels % 128 == 0:
            for place, k in enumerate(order):
                columns = lanes((ch ^ k) * channels, channels)
                held = slice(place * channels, (place + 1) * channels)
                pairs.append((pw_ref.at[rows, columns], columns_ref.at[rows, held]))
        else:
            pairs.append((pw_ref.at[rows], columns_ref.at[rows]))
        copies = [
            pltpu.make_async_copy(source, place, sems.at[len(blocks), i])
            for i, (source, place) in enumerate(pairs)
        ]
        for copy in copies:
            copy.start()
        blocks.append((rows, copies))
    if with_far:
        far = end_copy(x_ref, rest[-4], odd_place(), sems.at[0, count + 1])
        far.start()
    for step, (rows, copies) in enumerate(blocks):
        for copy in copies:
            copy.wait()
        for place in range(count):
            held = slice(place * channels, (place + 1) * channels)
            part = turned_dot(columns_ref[rows, held], cot_in[rows, :])
            if step > 0:
                part = part + total_ref[held, :]
            if step < len(blocks) - 1:
                total_ref[held, :] = part
            else:
                piece_refs[place][...] = part.astype(BF16)
    if with_far:
        far.wait()


def columns_of(pw_weight, channels, order):
    if channels % 128 == 0:
        return pw_weight
    ch = lax.axis_index("ch")
    return jnp.concatenate(
        [lax.dynamic_slice_in_dim(pw_weight, (ch ^ k) * channels, channels, 1) for k in order], axis=1
    )


def upstream(pw_weight, cotangent, inputs, order, first, with_far):
    channels = inputs.shape[0]
    total, width = cotangent.shape
    count = len(order)
    outs = [((channels, width), BF16, True)] * count
    outs += [(cotangent.shape, BF16, True)] * first + [((channels, DILATION_STEP), BF16, True)] * with_far
    results = kernel_call(
        "upstream", functools.partial(upstream_kernel, order, channels, first, with_far),
        [(columns_of(pw_weight, channels, order), False), (cotangent, not first), (inputs, False)], outs,
        [
            pltpu.VMEM((total, count * channels), BF16), pltpu.VMEM((count * channels, width), F32),
            DMA((total // UPSTREAM_ROWS, count + 2)),
        ],
    )
    return results[:count], *results[count:]


def convolve(w_ref, rows, wide, start, halo, unit):
    return sum(dot(w_ref[t, rows, :], wide[rows, lanes(start + t * halo, unit)]) for t in range(3))


def interior_kernel(n, x_ref, w_ref, *rest):
    active_refs, (slope_ref, wide, plain_ref, turned_ref, own_ref, sem, own_sem) = rest[:n], rest[n:]
    ch = lax.axis_index("ch")
    channels, length = x_ref.shape
    group = w_ref.shape[1]
    own = w_ref.at[:, :, lanes(ch * channels, channels)] if w_ref.shape[2] > channels else w_ref
    own_copy = pltpu.make_async_copy(own, own_ref, own_sem)
    own_copy.start()
    halo = DILATION_STEP
    block = length // n
    unit = min(block, 256)
    copy = pltpu.make_async_copy(x_ref, wide.at[:, halo:halo + length], sem)
    copy.start()
    groups = [slice(g, g + group) for g in range(0, channels, group)]
    own_copy.wait()
    for t in range(3):
        for rows in groups:
            square = own_ref[t, :, rows]
            turned_ref[2 - t, rows, :] = square
            plain_ref[t, rows, :] = square.T
    copy.wait()
    for k in range(n):
        base = (ch ^ k) * block

        @pl.when((base >= halo) & (base < length - halo))
        def _(k=k, base=base):
            for s in range(0, block, unit):
                for rows in groups:
                    active, slope = gelu_and_slope(convolve(plain_ref, rows, wide, base + s, halo, unit))
                    active_refs[k][rows, s:s + unit] = active.astype(BF16)
                    slope_ref[rows, lanes(base + s, unit)] = slope


def interior(inputs, weight, n):
    channels, length = inputs.shape
    group = weight.shape[1]
    block = length // n
    outs = [((channels, block), BF16, True)] * n
    outs += [((channels, length), F32, True), ((channels, length + 2 * DILATION_STEP), BF16, True)]
    outs += [((3, channels, group), BF16, True)] * 2
    results = kernel_call(
        "interior", functools.partial(interior_kernel, n), [(inputs, False), (weight, False)], outs,
        [pltpu.VMEM((3, group, channels), BF16), DMA, DMA],
    )
    return results[:n], *results[n:]


def end_kernel(n, near, waits, *refs):
    halo_ref, plain_ref, rest = refs[waits], refs[waits + 1], refs[-(n + 2):]
    active_refs, (slope_ref, wide) = rest[:n], rest[n:]
    ch, odd = lax.axis_index("ch"), odd_place()
    channels, length = slope_ref.shape
    group = plain_ref.shape[2]
    halo = halo_ref.shape[1]
    block = length // n
    unit = min(block, 256)
    groups = [slice(g, g + group) for g in range(0, channels, group)]
    at_end = 1 - odd if near else odd
    wide[:, lanes(at_end * (halo + length), halo)] = halo_ref[...]
    first = at_end * (length - halo)
    for k in range(n):
        base = (ch ^ k) * block

        @pl.when((base >= first) & (base < first + halo))
        def _(k=k, base=base):
            for s in range(0, block, unit):
                for rows in groups:
                    active, slope = gelu_and_slope(convolve(plain_ref, rows, wide, base + s, halo, unit))
                    active_refs[k][rows, s:s + unit] = active.astype(BF16)
                    slope_ref[rows, lanes(base + s, unit)] = slope


def one_end(near, halo, plain, active, slope, wide, waited):
    n = len(active)
    operands = [(o, True) for o in (*waited, halo, plain, *active, slope, wide)]
    results = kernel_call(
        "near_end" if near else "far_end", functools.partial(end_kernel, n, near, len(waited)), operands,
        [(a.shape, a.dtype, True) for a in (*active, slope, wide)],
        aliases={len(waited) + 2 + i: i for i in range(n + 2)},
    )
    return results[:n], *results[n:]


def grad_kernel(order, slope_ref, *rest):
    up_refs, (grad_ref, near_out, far_out) = rest[:-3], rest[-3:]
    ch, odd = lax.axis_index("ch"), odd_place()
    length, halo = grad_ref.shape[1], near_out.shape[1]
    block = up_refs[0].shape[1]
    for k, up_ref in zip(order, up_refs):
        here = lanes((ch ^ k) * block, block)
        grad_ref[:, here] = (up_ref[...].astype(F32) * slope_ref[:, here]).astype(BF16)
    near_out[...] = grad_ref[:, lanes((1 - odd) * (length - halo), halo)]
    far_out[...] = grad_ref[:, lanes(odd * (length - halo), halo)]


def grad_conv(slope, order, ups):
    channels = slope.shape[0]
    return kernel_call(
        "grad_conv", functools.partial(grad_kernel, order),
        [(o, True) for o in (slope, *[ups[k] for k in order])],
        [(slope.shape, BF16, True)] + [((channels, DILATION_STEP), BF16, True)] * 2,
    )


def columns_times(order, pw_ref, rows, pieces):
    channels = pieces.shape[0] // len(order)
    if channels % 128 != 0:
        return dot(pw_ref[rows, :], pieces)
    return sum(
        dot(
            pw_ref[rows, lanes((lax.axis_index("ch") ^ k) * channels, channels)],
            pieces[place * channels:(place + 1) * channels],
        )
        for place, k in enumerate(order)
    )


def mix_kernel(order, pw_ref, *rest):
    piece_refs, before, sum_ref = rest[:len(order)], rest[len(order):-1], rest[-1]
    pieces = jnp.concatenate([p[...] for p in piece_refs], axis=0)
    step = 512
    for m in range(0, sum_ref.shape[0], step):
        rows = slice(m, m + step)
        part = columns_times(order, pw_ref, rows, pieces)
        sum_ref[rows, :] = part + before[0][rows, :] if before else part


def mix(name, pw_weight, order, active, before):
    channels, width = active[order[0]].shape
    operands = [columns_of(pw_weight, channels, order), *[active[k] for k in order], *before]
    return kernel_call(
        name, functools.partial(mix_kernel, order), [(o, True) for o in operands],
        [((pw_weight.shape[0], width), F32, True)],
        aliases={len(operands) - 1: 0} if before else {},
    )


def back(turned_ref, rows, taps):
    return sum(dot(turned_ref[t, rows, :], tap) for t, tap in enumerate(taps)).astype(BF16)


def back_interior_kernel(grad_ref, turned_ref, out_ref, held, sem):
    channels, length = grad_ref.shape
    group, halo, unit = turned_ref.shape[2], DILATION_STEP, 256
    for g in range(0, channels, group):
        rows = slice(g, g + group)
        for s in range(0, length - 2 * halo, unit):
            held[rows, s:s + unit] = back(
                turned_ref, rows, [grad_ref[rows, s + t * halo:s + t * halo + unit] for t in range(3)]
            )
    copy = pltpu.make_async_copy(held, out_ref.at[:, halo:length - halo], sem)
    copy.start()
    copy.wait()


def late_mix_kernel(order, pw_ref, sum_ref, *rest):
    piece_refs, (out_ref, done_ref, held, sems) = rest[:len(order)], rest[len(order):]
    pieces = jnp.concatenate([p[...] for p in piece_refs], axis=0)
    step = 512
    copies = []
    for m in range(0, sum_ref.shape[0], step):
        rows = slice(m, m + step)
        held[rows, :] = (sum_ref[rows, :] + columns_times(order, pw_ref, rows, pieces)).astype(BF16)
        copies.append(pltpu.make_async_copy(held.at[rows, :], out_ref.at[rows, :], sems.at[len(copies)]))
        copies[-1].start()
    done_ref[...] = jnp.zeros_like(done_ref)
    for copy in copies:
        copy.wait()


def late_mix(pw_weight, order, active, partial):
    operands = [columns_of(pw_weight, active[order[0]].shape[0], order), partial, *[active[k] for k in order]]
    return kernel_call(
        "late_mix", functools.partial(late_mix_kernel, order), [(o, True) for o in operands],
        [(partial.shape, BF16, False), ((8, 128), F32, True)],
        [pltpu.VMEM(partial.shape, BF16), DMA((partial.shape[0] // 512,))],
    )


def back_ends_kernel(near_ref, far_ref, grad_ref, turned_ref, _, __, out_ref, ends, halos, sems):
    channels, length = grad_ref.shape
    group, halo, unit = turned_ref.shape[2], DILATION_STEP, 256
    odd = odd_place()
    halos[:, lanes((1 - odd) * halo, halo)] = near_ref[...]
    halos[:, lanes(odd * halo, halo)] = far_ref[...]
    copies = []
    for end in range(2):
        for g in range(0, channels, group):
            rows = slice(g, g + group)
            for s in range(0, halo, unit):
                inner = (length - 2 * halo) * end + s
                taps = [
                    grad_ref[rows, inner:inner + unit],
                    grad_ref[rows, inner + halo:inner + halo + unit],
                ]
                outer = halos[rows, end * halo + s:end * halo + s + unit]
                taps = taps + [outer] if end else [outer] + taps
                ends[rows, end * halo + s:end * halo + s + unit] = back(turned_ref, rows, taps)
        copies.append(pltpu.make_async_copy(
            ends.at[:, end * halo:(end + 1) * halo],
            out_ref.at[:, end * (length - halo):end * (length - halo) + halo], sems.at[end],
        ))
        copies[-1].start()
    for copy in copies:
        copy.wait()


def back_ends(near, far, grad, turned, done, grad_inputs):
    channels, halo = near.shape
    operands = [(o, True) for o in (near, far, grad, turned, done)] + [(grad_inputs, False)]
    return kernel_call(
        "back_ends", back_ends_kernel, operands, [(grad_inputs.shape, BF16, False)],
        [pltpu.VMEM((channels, 2 * halo), BF16)] * 2 + [DMA((2,))], {5: 0},
    )


def exchange(piece, k):
    if k == 0:
        return piece
    return lax.ppermute(piece, "ch", [(i, i ^ k) for i in range(lax.axis_size("ch"))])


def swap(values, first):
    size = lax.axis_size("ctx")
    pairs = [(i, i + 1) for i in range(first, size - 1, 2)]
    return lax.ppermute(values, "ctx", pairs + [(b, a) for a, b in pairs])


def body(inputs, conv_weight, pw_weight, cotangent):
    n = lax.axis_size("ch")
    channels, length = inputs.shape
    halo = DILATION_STEP
    order = list(range(n - 1, -1, -1))
    first, second, rest = order[:n // 4], order[n // 4:n // 2], order[n // 2:]

    weight = jnp.swapaxes(conv_weight, 1, 2)
    if channels % 128 != 0:
        weight = lax.dynamic_slice_in_dim(weight, lax.axis_index("ch") * channels, channels, 2)
    (near,) = kernel_call(
        "near_source", near_source_kernel, [(inputs, False)], [((channels, halo), BF16, True)], [DMA]
    )
    near = swap(near, 0)
    pieces, cot_in = upstream(pw_weight, cotangent, inputs, first, True, False)
    ups = {k: exchange(p, k) for k, p in zip(first, pieces)}
    pieces, far = upstream(pw_weight, cot_in, inputs, second, False, True)
    ups.update({k: exchange(p, k) for k, p in zip(second, pieces)})
    far = swap(far, 1)
    (pieces,) = upstream(pw_weight, cot_in, inputs, rest, False, False)
    ups.update({k: exchange(p, k) for k, p in zip(rest, pieces)})

    active, slope, wide, plain, turned = interior(inputs, weight, n)
    active, slope, wide = one_end(True, near, plain, active, slope, wide, [])
    active, slope, wide = one_end(
        False, far, plain, active, slope, wide, [ups[first[0]], ups[second[0]]]
    )
    grad, near_grad, far_grad = grad_conv(slope, order, ups)
    active = {k: exchange(active[k], k) for k in order}
    near_grad, far_grad = swap(near_grad, 0), swap(far_grad, 1)

    (grad_inputs,) = kernel_call(
        "back_interior", back_interior_kernel, [(grad, True), (turned, True)],
        [((channels, length), BF16, False)], [pltpu.VMEM((channels, length - 2 * halo), BF16), DMA],
    )
    partial = mix("early_mix", pw_weight, first, active, [])
    (partial,) = mix("half_mix", pw_weight, rest, active, partial)
    mixed, done = late_mix(pw_weight, second, active, partial)
    (grad_inputs,) = back_ends(near_grad, far_grad, grad, turned, done, grad_inputs)
    return mixed, grad_inputs


def solution(mesh):
    placed = (P("ch", "ctx"), P(), P(), P(None, ("ctx", "ch")))
    return jax.shard_map(
        body,
        mesh=mesh,
        in_specs=placed,
        out_specs=(P(None, ("ctx", "ch")), P("ch", "ctx")),
        check_vma=False,
    )
```

```python
import functools

import jax
import jax.numpy as jnp
from jax import lax
from jax.experimental import pallas as pl
from jax.experimental.pallas import tpu as pltpu
from jax.sharding import PartitionSpec as P

DILATION_STEP = 512
UPSTREAM_ROWS = 512
BF16, F32 = jnp.bfloat16, jnp.float32
ANY = pl.BlockSpec(memory_space=pl.ANY)
INSIDE = pl.BlockSpec(memory_space=pltpu.VMEM)
DMA = pltpu.SemaphoreType.DMA


def kernel_call(name, kernel, operands, outs, scratch=(), aliases=None):
    return pl.pallas_call(
        kernel,
        in_specs=[INSIDE if held else ANY for _, held in operands],
        out_specs=[INSIDE if held else ANY for _, _, held in outs],
        out_shape=[
            pltpu.VMEM(shape, kind) if held else jax.ShapeDtypeStruct(shape, kind)
            for shape, kind, held in outs
        ],
        scratch_shapes=list(scratch),
        input_output_aliases=aliases or {},
        compiler_params=pltpu.CompilerParams(vmem_limit_bytes=16 << 20),
        name=name,
    )(*[
        pltpu.with_memory_space_constraint(array, pltpu.VMEM if held else pltpu.HBM)
        for array, held in operands
    ])


def gelu_and_slope(v):
    square = v * v
    inner = v * (0.7978845608 + (0.7978845608 * 0.044715) * square)
    th = jnp.tanh(inner)
    half = 0.5 + 0.5 * th
    active = v * half
    inner_slope = 0.7978845608 + (3.0 * 0.7978845608 * 0.044715) * square
    slope = half + (0.5 * v) * (1.0 - th * th) * inner_slope
    return active, slope


def lanes(start, size):
    return pl.ds(pl.multiple_of(start, 128), size)


def dot(a, b):
    return jnp.dot(a, b, preferred_element_type=F32)


def turned_dot(a, b):
    return lax.dot_general(a, b, (((0,), (0,)), ((), ())), preferred_element_type=F32)


def odd_place():
    return lax.axis_index("ctx") % 2


def upstream_kernel(order, channels, first, pw_ref, cot_ref, x_ref, *rest):
    count = len(order)
    piece_refs, rest = rest[:count], rest[count:]
    columns_ref, total_ref, sems = rest[-3:]
    cot_in = rest[0] if first else cot_ref
    ch = lax.axis_index("ch")
    blocks = []
    for m in range(0, cot_in.shape[0], UPSTREAM_ROWS):
        rows = slice(m, m + UPSTREAM_ROWS)
        pairs = [(cot_ref.at[rows], cot_in.at[rows])] if first else []
        if channels % 128 == 0:
            for place, k in enumerate(order):
                columns = lanes((ch ^ k) * channels, channels)
                held = slice(place * channels, (place + 1) * channels)
                pairs.append((pw_ref.at[rows, columns], columns_ref.at[rows, held]))
        else:
            pairs.append((pw_ref.at[rows], columns_ref.at[rows]))
        copies = [
            pltpu.make_async_copy(source, place, sems.at[len(blocks), i])
            for i, (source, place) in enumerate(pairs)
        ]
        for copy in copies:
            copy.start()
        blocks.append((rows, copies))
    which = 1 - odd_place() if first else odd_place()
    length, halo = x_ref.shape[1], rest[-4].shape[1]
    end = pltpu.make_async_copy(
        x_ref.at[:, lanes(which * (length - halo), halo)], rest[-4], sems.at[0, count + 1]
    )
    end.start()
    for step, (rows, copies) in enumerate(blocks):
        for copy in copies:
            copy.wait()
        for place in range(count):
            held = slice(place * channels, (place + 1) * channels)
            part = turned_dot(columns_ref[rows, held], cot_in[rows, :])
            if step > 0:
                part = part + total_ref[held, :]
            if step < len(blocks) - 1:
                total_ref[held, :] = part
            else:
                piece_refs[place][...] = part.astype(BF16)
    end.wait()


def columns_of(pw_weight, channels, order):
    if channels % 128 == 0:
        return pw_weight
    ch = lax.axis_index("ch")
    return jnp.concatenate(
        [lax.dynamic_slice_in_dim(pw_weight, (ch ^ k) * channels, channels, 1) for k in order], axis=1
    )


def upstream(pw_weight, cotangent, inputs, order, first):
    channels = inputs.shape[0]
    total, width = cotangent.shape
    count = len(order)
    outs = [((channels, width), BF16, True)] * count
    outs += [(cotangent.shape, BF16, True)] * first
    outs += [((channels, DILATION_STEP), BF16, True)]
    results = kernel_call(
        "upstream", functools.partial(upstream_kernel, order, channels, first),
        [(columns_of(pw_weight, channels, order), False), (cotangent, not first), (inputs, False)], outs,
        [
            pltpu.VMEM((total, count * channels), BF16), pltpu.VMEM((count * channels, width), F32),
            DMA((total // UPSTREAM_ROWS, count + 2)),
        ],
    )
    return results[:count], *results[count:]


def convolve(w_ref, rows, wide, start, halo, unit):
    return sum(dot(w_ref[t, rows, :], wide[rows, lanes(start + t * halo, unit)]) for t in range(3))


def interior_kernel(n, x_ref, w_ref, *rest):
    active_refs, (slope_ref, wide, plain_ref, turned_ref, own_ref, sem, own_sem) = rest[:n], rest[n:]
    ch = lax.axis_index("ch")
    channels, length = x_ref.shape
    group = w_ref.shape[1]
    own = w_ref.at[:, :, lanes(ch * channels, channels)] if w_ref.shape[2] > channels else w_ref
    own_copy = pltpu.make_async_copy(own, own_ref, own_sem)
    own_copy.start()
    halo = DILATION_STEP
    block = length // n
    unit = min(block, 256)
    copy = pltpu.make_async_copy(x_ref, wide.at[:, halo:halo + length], sem)
    copy.start()
    groups = [slice(g, g + group) for g in range(0, channels, group)]
    own_copy.wait()
    for t in range(3):
        for rows in groups:
            square = own_ref[t, :, rows]
            turned_ref[2 - t, rows, :] = square
            plain_ref[t, rows, :] = square.T
    copy.wait()
    for k in range(n):
        base = (ch ^ k) * block

        @pl.when((base >= halo) & (base < length - halo))
        def _(k=k, base=base):
            for s in range(0, block, unit):
                for rows in groups:
                    active, slope = gelu_and_slope(convolve(plain_ref, rows, wide, base + s, halo, unit))
                    active_refs[k][rows, s:s + unit] = active.astype(BF16)
                    slope_ref[rows, lanes(base + s, unit)] = slope


def interior(inputs, weight, n):
    channels, length = inputs.shape
    group = weight.shape[1]
    block = length // n
    outs = [((channels, block), BF16, True)] * n
    outs += [((channels, length), F32, True), ((channels, length + 2 * DILATION_STEP), BF16, True)]
    outs += [((3, channels, group), BF16, True)] * 2
    results = kernel_call(
        "interior", functools.partial(interior_kernel, n), [(inputs, False), (weight, False)], outs,
        [pltpu.VMEM((3, group, channels), BF16), DMA, DMA],
    )
    return results[:n], *results[n:]


def end_kernel(n, near, waits, *refs):
    halo_ref, plain_ref, rest = refs[waits], refs[waits + 1], refs[-(n + 2):]
    active_refs, (slope_ref, wide) = rest[:n], rest[n:]
    ch, odd = lax.axis_index("ch"), odd_place()
    channels, length = slope_ref.shape
    group = plain_ref.shape[2]
    halo = halo_ref.shape[1]
    block = length // n
    unit = min(block, 256)
    groups = [slice(g, g + group) for g in range(0, channels, group)]
    at_end = 1 - odd if near else odd
    wide[:, lanes(at_end * (halo + length), halo)] = halo_ref[...]
    first = at_end * (length - halo)
    for k in range(n):
        base = (ch ^ k) * block

        @pl.when((base >= first) & (base < first + halo))
        def _(k=k, base=base):
            for s in range(0, block, unit):
                for rows in groups:
                    active, slope = gelu_and_slope(convolve(plain_ref, rows, wide, base + s, halo, unit))
                    active_refs[k][rows, s:s + unit] = active.astype(BF16)
                    slope_ref[rows, lanes(base + s, unit)] = slope


def one_end(near, halo, plain, active, slope, wide, waited):
    n = len(active)
    operands = [(o, True) for o in (*waited, halo, plain, *active, slope, wide)]
    results = kernel_call(
        "near_end" if near else "far_end", functools.partial(end_kernel, n, near, len(waited)), operands,
        [(a.shape, a.dtype, True) for a in (*active, slope, wide)],
        aliases={len(waited) + 2 + i: i for i in range(n + 2)},
    )
    return results[:n], *results[n:]


def grad_kernel(order, slope_ref, *rest):
    up_refs, (grad_ref, near_out, far_out) = rest[:-3], rest[-3:]
    ch, odd = lax.axis_index("ch"), odd_place()
    length, halo = grad_ref.shape[1], near_out.shape[1]
    block = up_refs[0].shape[1]
    for k, up_ref in zip(order, up_refs):
        here = lanes((ch ^ k) * block, block)
        grad_ref[:, here] = (up_ref[...].astype(F32) * slope_ref[:, here]).astype(BF16)
    near_out[...] = grad_ref[:, lanes((1 - odd) * (length - halo), halo)]
    far_out[...] = grad_ref[:, lanes(odd * (length - halo), halo)]


def grad_conv(slope, order, ups):
    channels = slope.shape[0]
    return kernel_call(
        "grad_conv", functools.partial(grad_kernel, order),
        [(o, True) for o in (slope, *[ups[k] for k in order])],
        [(slope.shape, BF16, True)] + [((channels, DILATION_STEP), BF16, True)] * 2,
    )


def columns_times(order, pw_ref, rows, pieces):
    channels = pieces.shape[0] // len(order)
    if channels % 128 != 0:
        return dot(pw_ref[rows, :], pieces)
    return sum(
        dot(
            pw_ref[rows, lanes((lax.axis_index("ch") ^ k) * channels, channels)],
            pieces[place * channels:(place + 1) * channels],
        )
        for place, k in enumerate(order)
    )


def mix_kernel(order, pw_ref, *rest):
    piece_refs, before, sum_ref = rest[:len(order)], rest[len(order):-1], rest[-1]
    pieces = jnp.concatenate([p[...] for p in piece_refs], axis=0)
    step = 512
    for m in range(0, sum_ref.shape[0], step):
        rows = slice(m, m + step)
        part = columns_times(order, pw_ref, rows, pieces)
        sum_ref[rows, :] = part + before[0][rows, :] if before else part


def mix(name, pw_weight, order, active, before):
    channels, width = active[order[0]].shape
    operands = [columns_of(pw_weight, channels, order), *[active[k] for k in order], *before]
    return kernel_call(
        name, functools.partial(mix_kernel, order), [(o, True) for o in operands],
        [((pw_weight.shape[0], width), F32, True)],
        aliases={len(operands) - 1: 0} if before else {},
    )


def back(turned_ref, rows, taps):
    return sum(dot(turned_ref[t, rows, :], tap) for t, tap in enumerate(taps)).astype(BF16)


def back_interior_kernel(grad_ref, turned_ref, out_ref, held, sem):
    channels, length = grad_ref.shape
    group, halo, unit = turned_ref.shape[2], DILATION_STEP, 256
    for g in range(0, channels, group):
        rows = slice(g, g + group)
        for s in range(0, length - 2 * halo, unit):
            held[rows, s:s + unit] = back(
                turned_ref, rows, [grad_ref[rows, s + t * halo:s + t * halo + unit] for t in range(3)]
            )
    copy = pltpu.make_async_copy(held, out_ref.at[:, halo:length - halo], sem)
    copy.start()
    copy.wait()


def tail_kernel(order, pw_ref, sum_ref, *rest):
    piece_refs, rest = rest[:len(order)], rest[len(order):]
    near_ref, far_ref, grad_ref, turned_ref, _, mixed_ref, out_ref, held, ends, halos, sems = rest
    channels, length = grad_ref.shape
    group, halo, unit = turned_ref.shape[2], DILATION_STEP, 256
    pieces = jnp.concatenate([p[...] for p in piece_refs], axis=0)
    copies = []

    def send(source, place):
        copies.append(pltpu.make_async_copy(source, place, sems.at[len(copies)]))
        copies[-1].start()

    step = 512
    for m in range(0, sum_ref.shape[0], step):
        rows = slice(m, m + step)
        held[rows, :] = (sum_ref[rows, :] + columns_times(order, pw_ref, rows, pieces)).astype(BF16)
        send(held.at[rows, :], mixed_ref.at[rows, :])
    odd = odd_place()
    halos[:, lanes((1 - odd) * halo, halo)] = near_ref[...]
    halos[:, lanes(odd * halo, halo)] = far_ref[...]
    for end in range(2):
        for g in range(0, channels, group):
            rows = slice(g, g + group)
            for s in range(0, halo, unit):
                inner = (length - 2 * halo) * end + s
                taps = [
                    grad_ref[rows, inner:inner + unit],
                    grad_ref[rows, inner + halo:inner + halo + unit],
                ]
                outer = halos[rows, end * halo + s:end * halo + s + unit]
                taps = taps + [outer] if end else [outer] + taps
                ends[rows, end * halo + s:end * halo + s + unit] = back(turned_ref, rows, taps)
        send(
            ends.at[:, end * halo:(end + 1) * halo],
            out_ref.at[:, end * (length - halo):end * (length - halo) + halo],
        )
    for copy in copies:
        copy.wait()


def tail(pw_weight, order, partial, active, near, far, grad, turned, grad_inputs):
    channels, halo = near.shape
    operands = [columns_of(pw_weight, channels, order), partial, *[active[k] for k in order]]
    operands = [(o, True) for o in (*operands, near, far, grad, turned)] + [(grad_inputs, False)]
    return kernel_call(
        "tail", functools.partial(tail_kernel, order), operands,
        [(partial.shape, BF16, False), (grad_inputs.shape, BF16, False)],
        [pltpu.VMEM(partial.shape, BF16)] + [pltpu.VMEM((channels, 2 * halo), BF16)] * 2
        + [DMA((partial.shape[0] // 512 + 2,))],
        {len(operands) - 1: 1},
    )


def exchange(piece, k):
    if k == 0:
        return piece
    return lax.ppermute(piece, "ch", [(i, i ^ k) for i in range(lax.axis_size("ch"))])


def swap(values, first):
    size = lax.axis_size("ctx")
    pairs = [(i, i + 1) for i in range(first, size - 1, 2)]
    return lax.ppermute(values, "ctx", pairs + [(b, a) for a, b in pairs])


def body(inputs, conv_weight, pw_weight, cotangent):
    n = lax.axis_size("ch")
    channels, length = inputs.shape
    halo = DILATION_STEP
    order = list(range(n - 1, -1, -1))
    first, second, rest = order[:n // 4], order[n // 4:n // 2], order[n // 2:]

    weight = jnp.swapaxes(conv_weight, 1, 2)
    if channels % 128 != 0:
        weight = lax.dynamic_slice_in_dim(weight, lax.axis_index("ch") * channels, channels, 2)
    pieces, cot_in, near = upstream(pw_weight, cotangent, inputs, first, True)
    near = swap(near, 0)
    ups = {k: exchange(p, k) for k, p in zip(first, pieces)}
    pieces, far = upstream(pw_weight, cot_in, inputs, second + rest, False)
    ups.update({k: exchange(p, k) for k, p in zip(second + rest, pieces)})
    far = swap(far, 1)

    active, slope, wide, plain, turned = interior(inputs, weight, n)
    active, slope, wide = one_end(True, near, plain, active, slope, wide, [])
    active, slope, wide = one_end(
        False, far, plain, active, slope, wide, [ups[first[0]]]
    )
    grad, near_grad, far_grad = grad_conv(slope, order, ups)
    active = {k: exchange(active[k], k) for k in order}
    near_grad, far_grad = swap(near_grad, 0), swap(far_grad, 1)

    (grad_inputs,) = kernel_call(
        "back_interior", back_interior_kernel, [(grad, True), (turned, True)],
        [((channels, length), BF16, False)], [pltpu.VMEM((channels, length - 2 * halo), BF16), DMA],
    )
    partial = mix("early_mix", pw_weight, first, active, [])
    (partial,) = mix("half_mix", pw_weight, rest, active, partial)
    return tuple(tail(pw_weight, second, partial, active, near_grad, far_grad, grad, turned, grad_inputs))


def solution(mesh):
    placed = (P("ch", "ctx"), P(), P(), P(None, ("ctx", "ch")))
    return jax.shard_map(
        body,
        mesh=mesh,
        in_specs=placed,
        out_specs=(P(None, ("ctx", "ch")), P("ch", "ctx")),
        check_vma=False,
    )
```

```python
import functools

import jax
import jax.numpy as jnp
from jax import lax
from jax.experimental import pallas as pl
from jax.experimental.pallas import tpu as pltpu
from jax.sharding import PartitionSpec as P

DILATION_STEP = 512
UPSTREAM_ROWS = 512
BF16, F32 = jnp.bfloat16, jnp.float32
ANY = pl.BlockSpec(memory_space=pl.ANY)
INSIDE = pl.BlockSpec(memory_space=pltpu.VMEM)
DMA = pltpu.SemaphoreType.DMA


def kernel_call(name, kernel, operands, outs, scratch=(), aliases=None):
    return pl.pallas_call(
        kernel,
        in_specs=[INSIDE if held else ANY for _, held in operands],
        out_specs=[INSIDE if held else ANY for _, _, held in outs],
        out_shape=[
            pltpu.VMEM(shape, kind) if held else jax.ShapeDtypeStruct(shape, kind)
            for shape, kind, held in outs
        ],
        scratch_shapes=list(scratch),
        input_output_aliases=aliases or {},
        compiler_params=pltpu.CompilerParams(vmem_limit_bytes=16 << 20),
        name=name,
    )(*[
        pltpu.with_memory_space_constraint(array, pltpu.VMEM if held else pltpu.HBM)
        for array, held in operands
    ])


def gelu_and_slope(v):
    square = v * v
    inner = v * (0.7978845608 + (0.7978845608 * 0.044715) * square)
    th = jnp.tanh(inner)
    half = 0.5 + 0.5 * th
    active = v * half
    inner_slope = 0.7978845608 + (3.0 * 0.7978845608 * 0.044715) * square
    slope = half + (0.5 * v) * (1.0 - th * th) * inner_slope
    return active, slope


def lanes(start, size):
    return pl.ds(pl.multiple_of(start, 128), size)


def dot(a, b):
    return jnp.dot(a, b, preferred_element_type=F32)


def turned_dot(a, b):
    return lax.dot_general(a, b, (((0,), (0,)), ((), ())), preferred_element_type=F32)


def odd_place():
    return lax.axis_index("ctx") % 2


def upstream_kernel(order, channels, first, pw_ref, cot_ref, x_ref, *rest):
    count = len(order)
    piece_refs, rest = rest[:count], rest[count:]
    columns_ref, total_ref, sems = rest[-3:]
    cot_in = rest[0] if first else cot_ref
    ch = lax.axis_index("ch")
    blocks = []
    for m in range(0, cot_in.shape[0], UPSTREAM_ROWS):
        rows = slice(m, m + UPSTREAM_ROWS)
        pairs = [(cot_ref.at[rows], cot_in.at[rows])] if first else []
        if channels % 128 == 0:
            for place, k in enumerate(order):
                columns = lanes((ch ^ k) * channels, channels)
                held = slice(place * channels, (place + 1) * channels)
                pairs.append((pw_ref.at[rows, columns], columns_ref.at[rows, held]))
        else:
            pairs.append((pw_ref.at[rows], columns_ref.at[rows]))
        copies = [
            pltpu.make_async_copy(source, place, sems.at[len(blocks), i])
            for i, (source, place) in enumerate(pairs)
        ]
        for copy in copies:
            copy.start()
        blocks.append((rows, copies))
    which = 1 - odd_place() if first else odd_place()
    length, halo = x_ref.shape[1], rest[-4].shape[1]
    end = pltpu.make_async_copy(
        x_ref.at[:, lanes(which * (length - halo), halo)], rest[-4], sems.at[0, count + 1]
    )
    end.start()
    for step, (rows, copies) in enumerate(blocks):
        for copy in copies:
            copy.wait()
        for place in range(count):
            held = slice(place * channels, (place + 1) * channels)
            part = turned_dot(columns_ref[rows, held], cot_in[rows, :])
            if step > 0:
                part = part + total_ref[held, :]
            if step < len(blocks) - 1:
                total_ref[held, :] = part
            else:
                piece_refs[place][...] = part.astype(BF16)
    end.wait()


def columns_of(pw_weight, channels, order):
    if channels % 128 == 0:
        return pw_weight
    ch = lax.axis_index("ch")
    return jnp.concatenate(
        [lax.dynamic_slice_in_dim(pw_weight, (ch ^ k) * channels, channels, 1) for k in order], axis=1
    )


def upstream(pw_weight, cotangent, inputs, order, first):
    channels = inputs.shape[0]
    total, width = cotangent.shape
    count = len(order)
    outs = [((channels, width), BF16, True)] * count
    outs += [(cotangent.shape, BF16, True)] * first
    outs += [((channels, DILATION_STEP), BF16, True)]
    results = kernel_call(
        "upstream", functools.partial(upstream_kernel, order, channels, first),
        [(columns_of(pw_weight, channels, order), False), (cotangent, not first), (inputs, False)], outs,
        [
            pltpu.VMEM((total, count * channels), BF16), pltpu.VMEM((count * channels, width), F32),
            DMA((total // UPSTREAM_ROWS, count + 2)),
        ],
    )
    return results[:count], *results[count:]


def is_inner(block_index, block, length):
    base = block_index * block
    return (base >= DILATION_STEP) & (base < length - DILATION_STEP)


def convolve_block(plain_ref, wide, base, active_ref, slope_ref):
    group, width = plain_ref.shape[2], active_ref.shape[1]
    unit = min(width, 256)
    for s in range(0, width, unit):
        for g in range(0, active_ref.shape[0], group):
            rows = slice(g, g + group)
            conv_out = sum(
                dot(plain_ref[t, rows, :], wide[rows, lanes(base + s + t * DILATION_STEP, unit)])
                for t in range(3)
            )
            active, slope = gelu_and_slope(conv_out)
            active_ref[rows, s:s + unit] = active.astype(BF16)
            slope_ref[rows, lanes(base + s, unit)] = slope


def interior_kernel(n, x_ref, w_ref, *rest):
    active_refs, (slope_ref, wide, plain_ref, turned_ref, own_ref, sem, own_sem) = rest[:n], rest[n:]
    ch = lax.axis_index("ch")
    channels, length = x_ref.shape
    group, halo = w_ref.shape[1], DILATION_STEP
    block = length // n
    own = w_ref.at[:, :, lanes(ch * channels, channels)] if w_ref.shape[2] > channels else w_ref
    own_copy = pltpu.make_async_copy(own, own_ref, own_sem)
    own_copy.start()
    copy = pltpu.make_async_copy(x_ref, wide.at[:, halo:halo + length], sem)
    copy.start()
    own_copy.wait()
    for t in range(3):
        for g in range(0, channels, group):
            square = own_ref[t, :, g:g + group]
            turned_ref[2 - t, g:g + group, :] = square
            plain_ref[t, g:g + group, :] = square.T
    copy.wait()
    for k in range(n):
        @pl.when(is_inner(ch ^ k, block, length))
        def _(k=k):
            convolve_block(plain_ref, wide, (ch ^ k) * block, active_refs[k], slope_ref)


def interior(inputs, weight, n):
    channels, length = inputs.shape
    group = weight.shape[1]
    outs = [((channels, length // n), BF16, True)] * n
    outs += [((channels, length), F32, True), ((channels, length + 2 * DILATION_STEP), BF16, True)]
    outs += [((3, channels, group), BF16, True)] * 2
    results = kernel_call(
        "interior", functools.partial(interior_kernel, n), [(inputs, False), (weight, False)], outs,
        [pltpu.VMEM((3, group, channels), BF16), DMA, DMA],
    )
    return results[:n], *results[n:]


def in_end(block_index, block, at_end, length):
    first = at_end * (length - DILATION_STEP)
    return (block_index * block >= first) & (block_index * block < first + DILATION_STEP)


def near_kernel(ks, waits, near_ref, *rest):
    plain_ref = rest[waits]
    n = len(ks)
    slope_ref, wide = rest[-(n + 2):-n]
    active_refs = rest[-n:]
    ch, at_end = lax.axis_index("ch"), 1 - odd_place()
    length, halo = slope_ref.shape[1], near_ref.shape[1]
    block = length // n
    wide[:, lanes(at_end * (halo + length), halo)] = near_ref[...]
    for k, active_ref in zip(ks, active_refs):
        @pl.when(in_end(ch ^ k, block, at_end, length))
        def _(k=k, active_ref=active_ref):
            convolve_block(plain_ref, wide, (ch ^ k) * block, active_ref, slope_ref)


def near_end(near, waited, plain, slope, wide, away, here, active):
    held = [active[k] for k in here]
    operands = [(o, True) for o in (near, *waited, plain, slope, wide, *held)]
    outs = [slope, wide, *[active[k] for k in away], *held]
    first_held, at = 2 + len(away), 2 + len(waited)
    results = kernel_call(
        "near_end", functools.partial(near_kernel, away + here, len(waited)), operands,
        [(o.shape, o.dtype, True) for o in outs],
        aliases={at: 0, at + 1: 1, **{at + 2 + i: first_held + i for i in range(len(here))}},
    )
    return results[0], results[1], dict(zip(away + here, results[2:]))


def grad_kernel(ks, slope_ref, *rest):
    up_refs, (grad_ref, near_out) = rest[:-2], rest[-2:]
    ch, odd = lax.axis_index("ch"), odd_place()
    length, halo = grad_ref.shape[1], near_out.shape[1]
    block = length // len(ks)
    for k, up_ref in zip(ks, up_refs):
        @pl.when(jnp.logical_not(in_end(ch ^ k, block, odd, length)))
        def _(k=k, up_ref=up_ref):
            here = lanes((ch ^ k) * block, block)
            grad_ref[:, here] = (up_ref[...].astype(F32) * slope_ref[:, here]).astype(BF16)
    near_out[...] = grad_ref[:, lanes((1 - odd) * (length - halo), halo)]


def grad_conv(slope, ks, ups):
    return kernel_call(
        "grad_conv", functools.partial(grad_kernel, ks),
        [(o, True) for o in (slope, *[ups[k] for k in ks])],
        [(slope.shape, BF16, True), ((slope.shape[0], DILATION_STEP), BF16, True)],
    )


def far_kernel(ks, _, __, far_ref, plain_ref, *rest):
    n = len(ks)
    up_refs, (slope_ref, far_out, wide, grad_ref), active_refs = rest[:n], rest[-(n + 4):-n], rest[-n:]
    ch, at_end = lax.axis_index("ch"), odd_place()
    length, halo = slope_ref.shape[1], far_ref.shape[1]
    block = length // n
    wide[:, lanes(at_end * (halo + length), halo)] = far_ref[...]
    for k, up_ref, active_ref in zip(ks, up_refs, active_refs):
        @pl.when(in_end(ch ^ k, block, at_end, length))
        def _(k=k, up_ref=up_ref, active_ref=active_ref):
            convolve_block(plain_ref, wide, (ch ^ k) * block, active_ref, slope_ref)
            here = lanes((ch ^ k) * block, block)
            grad = (up_ref[...].astype(F32) * slope_ref[:, here]).astype(BF16)
            grad_ref[:, here] = grad
            far_out[:, lanes((ch ^ k) * block - at_end * (length - halo), block)] = grad


def far_end(far, plain, slope, wide, grad, ks, ups, active):
    n = len(ks)
    operands = [(o, True) for o in (slope, wide, far, plain, *[ups[k] for k in ks], grad)]
    operands += [(active[k], True) for k in ks]
    outs = [slope, far, wide, grad, *[active[k] for k in ks]]
    results = kernel_call(
        "far_end", functools.partial(far_kernel, ks), operands, [(o.shape, o.dtype, True) for o in outs],
        aliases={0: 0, 1: 2, 4 + n: 3, **{5 + n + i: 4 + i for i in range(n)}},
    )
    return results[1], results[3], dict(zip(ks, results[4:]))


def columns_times(order, pw_ref, rows, pieces):
    channels = pieces.shape[0] // len(order)
    if channels % 128 != 0:
        return dot(pw_ref[rows, :], pieces)
    return sum(
        dot(
            pw_ref[rows, lanes((lax.axis_index("ch") ^ k) * channels, channels)],
            pieces[place * channels:(place + 1) * channels],
        )
        for place, k in enumerate(order)
    )


def gather(counts, refs, gathered):
    width = gathered.shape[1]
    inner = is_inner(lax.axis_index("ch"), width, lax.axis_size("ch") * width)
    refs, at = list(refs), 0
    channels = refs[0].shape[0]
    for count in counts:
        rows = slice(at, at + channels)
        if count == 1:
            gathered[rows, :] = refs.pop(0)[...]
        else:
            early, late = refs.pop(0), refs.pop(0)

            @pl.when(inner)
            def _(rows=rows, early=early):
                gathered[rows, :] = early[...]

            @pl.when(jnp.logical_not(inner))
            def _(rows=rows, late=late):
                gathered[rows, :] = late[...]
        at += channels


def mix_kernel(order, counts, adds, *refs):
    before, refs = refs[:adds], refs[-sum(counts) - 3:]
    pw_ref, piece_refs, sum_ref, gathered = refs[0], refs[1:-2], refs[-2], refs[-1]
    gather(counts, piece_refs, gathered)
    pieces = gathered[...]
    step = 512
    for m in range(0, sum_ref.shape[0], step):
        rows = slice(m, m + step)
        part = columns_times(order, pw_ref, rows, pieces)
        sum_ref[rows, :] = part + before[0][rows, :] if before else part


def mix(name, pw_weight, order, active, before, waited=()):
    channels, width = active[order[0]][0].shape
    operands = [*before, *waited, columns_of(pw_weight, channels, order), *[p for k in order for p in active[k]]]
    return kernel_call(
        name, functools.partial(mix_kernel, order, [len(active[k]) for k in order], len(before)),
        [(o, True) for o in operands], [((pw_weight.shape[0], width), F32, True)],
        [pltpu.VMEM((len(order) * channels, width), BF16)], {0: 0} if before else {},
    )


def back_interior_kernel(grad_ref, turned_ref, *rest):
    out_ref, ends_ref, held, sem = rest[-4:]
    channels, length = grad_ref.shape
    group, halo, unit = turned_ref.shape[2], DILATION_STEP, 256

    def taps(rows, start, which):
        return sum(
            dot(turned_ref[t, rows, :], grad_ref[rows, start + (t - 1) * halo:start + (t - 1) * halo + unit])
            for t in which
        )

    groups = [slice(g, g + group) for g in range(0, channels, group)]
    for rows in groups:
        for s in range(0, length - 2 * halo, unit):
            held[rows, s:s + unit] = taps(rows, halo + s, (0, 1, 2)).astype(BF16)
    copy = pltpu.make_async_copy(held, out_ref.at[:, halo:length - halo], sem)
    copy.start()
    for rows in groups:
        for s in range(0, halo, unit):
            ends_ref[rows, s:s + unit] = taps(rows, s, (1, 2))
            ends_ref[rows, halo + s:halo + s + unit] = taps(rows, length - halo + s, (0, 1))
    copy.wait()


def back_end(halo_ref, ends_ref, turned_ref, at_end, held):
    channels, halo = halo_ref.shape
    group, unit = turned_ref.shape[2], 256
    for g in range(0, channels, group):
        rows = slice(g, g + group)
        for s in range(0, halo, unit):
            outer = dot(turned_ref[2 * at_end, rows, :], halo_ref[rows, s:s + unit])
            held[rows, s:s + unit] = (ends_ref[rows, lanes(at_end * halo + s, unit)] + outer).astype(BF16)


def end_of(out_ref, at_end):
    return out_ref.at[:, lanes(at_end * (out_ref.shape[1] - DILATION_STEP), DILATION_STEP)]


def back_near_kernel(near_ref, ends_ref, turned_ref, _, out_ref, done_ref, held, sem):
    at_end = 1 - odd_place()
    back_end(near_ref, ends_ref, turned_ref, at_end, held)
    copy = pltpu.make_async_copy(held, end_of(out_ref, at_end), sem)
    copy.start()
    done_ref[...] = jnp.zeros_like(done_ref)
    copy.wait()


def back_near(near, ends, turned, grad_inputs):
    return kernel_call(
        "back_near", back_near_kernel, [(near, True), (ends, True), (turned, True), (grad_inputs, False)],
        [(grad_inputs.shape, BF16, False), ((8, 128), F32, True)], [pltpu.VMEM(near.shape, BF16), DMA], {3: 0},
    )


def tail_kernel(order, counts, far_ref, sum_ref, pw_ref, *rest):
    piece_refs, rest = rest[:-10], rest[-10:]
    ends_ref, turned_ref, _, mixed_ref, out_ref, gathered, held, end, sems, end_sem = rest
    copies = []

    def send(source, place, sem):
        copies.append(pltpu.make_async_copy(source, place, sem))
        copies[-1].start()

    gather(counts, piece_refs, gathered)
    pieces = gathered[...]
    step = 512
    for m in range(0, sum_ref.shape[0], step):
        rows = slice(m, m + step)
        held[rows, :] = (sum_ref[rows, :] + columns_times(order, pw_ref, rows, pieces)).astype(BF16)
        send(held.at[rows, :], mixed_ref.at[rows, :], sems.at[m // step])
    at_end = odd_place()
    back_end(far_ref, ends_ref, turned_ref, at_end, end)
    send(end, end_of(out_ref, at_end), end_sem)
    for copy in copies:
        copy.wait()


def tail(far, partial, pw_weight, order, active, ends, turned, grad_inputs):
    channels = far.shape[0]
    operands = [far, partial, columns_of(pw_weight, channels, order)]
    operands += [*[p for k in order for p in active[k]], ends, turned]
    operands = [(o, True) for o in operands] + [(grad_inputs, False)]
    return kernel_call(
        "tail", functools.partial(tail_kernel, order, [len(active[k]) for k in order]), operands,
        [(partial.shape, BF16, False), (grad_inputs.shape, BF16, False)],
        [
            pltpu.VMEM((len(order) * channels, partial.shape[1]), BF16), pltpu.VMEM(partial.shape, BF16),
            pltpu.VMEM(far.shape, BF16), DMA((partial.shape[0] // 512,)), DMA,
        ],
        {len(operands) - 1: 1},
    )


def exchange(piece, k):
    if k == 0:
        return piece
    return lax.ppermute(piece, "ch", [(i, i ^ k) for i in range(lax.axis_size("ch"))])


def exchange_part(piece, k, inner):
    n, block = lax.axis_size("ch"), piece.shape[1]
    return lax.ppermute(
        piece, "ch", [(i, i ^ k) for i in range(n) if is_inner(i ^ k, block, n * block) == inner]
    )


def swap(values, first):
    size = lax.axis_size("ctx")
    pairs = [(i, i + 1) for i in range(first, size - 1, 2)]
    return lax.ppermute(values, "ctx", pairs + [(b, a) for a, b in pairs])


def body(inputs, conv_weight, pw_weight, cotangent):
    n = lax.axis_size("ch")
    channels, length = inputs.shape
    halo = DILATION_STEP
    order = list(range(n - 1, -1, -1))
    first, second, rest = order[:n // 4], order[n // 4:n // 2], order[n // 2:]

    weight = jnp.swapaxes(conv_weight, 1, 2)
    if channels % 128 != 0:
        weight = lax.dynamic_slice_in_dim(weight, lax.axis_index("ch") * channels, channels, 2)
    pieces, cot_in, near = upstream(pw_weight, cotangent, inputs, first, True)
    near = swap(near, 0)
    ups = {k: exchange(p, k) for k, p in zip(first, pieces)}
    pieces, far = upstream(pw_weight, cot_in, inputs, second + rest, False)
    ups.update({k: exchange(p, k) for k, p in zip(second + rest, pieces)})
    far = swap(far, 1)

    active, slope, wide, plain, turned = interior(inputs, weight, n)
    inner = {k: exchange_part(active[k], k, True) for k in first}
    waited = [ups[k] for k in first + [k for k in rest if k > 0]]
    slope, wide, active = near_end(near, waited, plain, slope, wide, first, second + rest, active)
    grad, near_grad = grad_conv(slope, order, ups)
    near_grad = swap(near_grad, 0)
    far_grad, grad, active = far_end(far, plain, slope, wide, grad, order, ups, active)
    far_grad = swap(far_grad, 1)
    active = {
        k: (inner[k], exchange_part(active[k], k, False)) if k in first else (exchange(active[k], k),)
        for k in order
    }

    grad_inputs, ends = kernel_call(
        "back_interior", back_interior_kernel,
        [(grad, True), (turned, True), *[(inner[k], True) for k in first]],
        [((channels, length), BF16, False), ((channels, 2 * halo), F32, True)],
        [pltpu.VMEM((channels, length - 2 * halo), BF16), DMA],
    )
    grad_inputs, done = back_near(near_grad, ends, turned, grad_inputs)
    partial = mix("half_mix", pw_weight, rest, active, [], [done])
    (partial,) = mix("early_mix", pw_weight, second, active, partial)
    return tuple(tail(far_grad, partial, pw_weight, first, active, ends, turned, grad_inputs))


def solution(mesh):
    placed = (P("ch", "ctx"), P(), P(), P(None, ("ctx", "ch")))
    return jax.shard_map(
        body,
        mesh=mesh,
        in_specs=placed,
        out_specs=(P(None, ("ctx", "ch")), P("ch", "ctx")),
        check_vma=False,
    )
```

```python
import functools

import jax
import jax.numpy as jnp
from jax import lax
from jax.experimental import pallas as pl
from jax.experimental.pallas import tpu as pltpu
from jax.sharding import PartitionSpec as P

DILATION_STEP = 512
UPSTREAM_ROWS = 512
BF16, F32 = jnp.bfloat16, jnp.float32
ANY = pl.BlockSpec(memory_space=pl.ANY)
INSIDE = pl.BlockSpec(memory_space=pltpu.VMEM)
DMA = pltpu.SemaphoreType.DMA


TAKES = {
    "upstream": 3, "interior": 3, "near_end": 1, "grad_conv": 1, "far_end": 1, "back_interior": 2,
    "early_mix": 3, "tail": 2,
}


def kernel_call(name, kernel, operands, outs, scratch=(), aliases=None):
    return pl.pallas_call(
        kernel,
        in_specs=[INSIDE if held else ANY for _, held in operands],
        out_specs=[INSIDE if held else ANY for _, _, held in outs],
        out_shape=[
            pltpu.VMEM(shape, kind) if held else jax.ShapeDtypeStruct(shape, kind)
            for shape, kind, held in outs
        ],
        scratch_shapes=list(scratch),
        input_output_aliases=aliases or {},
        compiler_params=pltpu.CompilerParams(vmem_limit_bytes=16 << 20),
        cost_estimate=pl.CostEstimate(flops=0, transcendentals=0, bytes_accessed=TAKES[name] * 3_500_000),
        name=name,
    )(*[
        pltpu.with_memory_space_constraint(array, pltpu.VMEM if held else pltpu.HBM)
        for array, held in operands
    ])


def gelu_and_slope(v):
    square = v * v
    inner = v * (0.7978845608 + (0.7978845608 * 0.044715) * square)
    th = jnp.tanh(inner)
    half = 0.5 + 0.5 * th
    active = v * half
    inner_slope = 0.7978845608 + (3.0 * 0.7978845608 * 0.044715) * square
    slope = half + (0.5 * v) * (1.0 - th * th) * inner_slope
    return active, slope


def lanes(start, size):
    return pl.ds(pl.multiple_of(start, 128), size)


def dot(a, b):
    return jnp.dot(a, b, preferred_element_type=F32)


def turned_dot(a, b):
    return lax.dot_general(a, b, (((0,), (0,)), ((), ())), preferred_element_type=F32)


def odd_place():
    return lax.axis_index("ctx") % 2


def upstream_kernel(order, channels, first, pw_ref, cot_ref, x_ref, *rest):
    count = len(order)
    piece_refs, rest = rest[:count], rest[count:]
    columns_ref, total_ref, sems = rest[-3:]
    cot_in = rest[0] if first else cot_ref
    ch = lax.axis_index("ch")
    blocks = []
    for m in range(0, cot_in.shape[0], UPSTREAM_ROWS):
        rows = slice(m, m + UPSTREAM_ROWS)
        pairs = [(cot_ref.at[rows], cot_in.at[rows])] if first else []
        if channels % 128 == 0:
            for place, k in enumerate(order):
                columns = lanes((ch ^ k) * channels, channels)
                held = slice(place * channels, (place + 1) * channels)
                pairs.append((pw_ref.at[rows, columns], columns_ref.at[rows, held]))
        else:
            pairs.append((pw_ref.at[rows], columns_ref.at[rows]))
        copies = [
            pltpu.make_async_copy(source, place, sems.at[len(blocks), i])
            for i, (source, place) in enumerate(pairs)
        ]
        for copy in copies:
            copy.start()
        blocks.append((rows, copies))
    which = 1 - odd_place() if first else odd_place()
    length, halo = x_ref.shape[1], rest[-4].shape[1]
    end = pltpu.make_async_copy(
        x_ref.at[:, lanes(which * (length - halo), halo)], rest[-4], sems.at[0, count + 1]
    )
    end.start()
    for step, (rows, copies) in enumerate(blocks):
        for copy in copies:
            copy.wait()
        for place in range(count):
            held = slice(place * channels, (place + 1) * channels)
            part = turned_dot(columns_ref[rows, held], cot_in[rows, :])
            if step > 0:
                part = part + total_ref[held, :]
            if step < len(blocks) - 1:
                total_ref[held, :] = part
            else:
                piece_refs[place][...] = part.astype(BF16)
    end.wait()


def columns_of(pw_weight, channels, order):
    if channels % 128 == 0:
        return pw_weight
    ch = lax.axis_index("ch")
    return jnp.concatenate(
        [lax.dynamic_slice_in_dim(pw_weight, (ch ^ k) * channels, channels, 1) for k in order], axis=1
    )


def upstream(pw_weight, cotangent, inputs, order, first):
    channels = inputs.shape[0]
    total, width = cotangent.shape
    count = len(order)
    outs = [((channels, width), BF16, True)] * count
    outs += [(cotangent.shape, BF16, True)] * first
    outs += [((channels, DILATION_STEP), BF16, True)]
    results = kernel_call(
        "upstream", functools.partial(upstream_kernel, order, channels, first),
        [(columns_of(pw_weight, channels, order), False), (cotangent, not first), (inputs, False)], outs,
        [
            pltpu.VMEM((total, count * channels), BF16), pltpu.VMEM((count * channels, width), F32),
            DMA((total // UPSTREAM_ROWS, count + 2)),
        ],
    )
    return results[:count], *results[count:]


def is_inner(block_index, block, length):
    base = block_index * block
    return (base >= DILATION_STEP) & (base < length - DILATION_STEP)


def convolve_block(plain_ref, wide, base, active_ref, slope_ref):
    group, width = plain_ref.shape[2], active_ref.shape[1]
    unit = min(width, 256)
    for s in range(0, width, unit):
        for g in range(0, active_ref.shape[0], group):
            rows = slice(g, g + group)
            conv_out = sum(
                dot(plain_ref[t, rows, :], wide[rows, lanes(base + s + t * DILATION_STEP, unit)])
                for t in range(3)
            )
            active, slope = gelu_and_slope(conv_out)
            active_ref[rows, s:s + unit] = active.astype(BF16)
            slope_ref[rows, lanes(base + s, unit)] = slope


def interior_kernel(n, x_ref, w_ref, *rest):
    active_refs, (slope_ref, wide, plain_ref, turned_ref, own_ref, sem, own_sem) = rest[:n], rest[n:]
    ch = lax.axis_index("ch")
    channels, length = x_ref.shape
    group, halo = w_ref.shape[1], DILATION_STEP
    block = length // n
    own = w_ref.at[:, :, lanes(ch * channels, channels)] if w_ref.shape[2] > channels else w_ref
    own_copy = pltpu.make_async_copy(own, own_ref, own_sem)
    own_copy.start()
    copy = pltpu.make_async_copy(x_ref, wide.at[:, halo:halo + length], sem)
    copy.start()
    own_copy.wait()
    for t in range(3):
        for g in range(0, channels, group):
            square = own_ref[t, :, g:g + group]
            turned_ref[2 - t, g:g + group, :] = square
            plain_ref[t, g:g + group, :] = square.T
    copy.wait()
    for k in range(n):
        @pl.when(is_inner(ch ^ k, block, length))
        def _(k=k):
            convolve_block(plain_ref, wide, (ch ^ k) * block, active_refs[k], slope_ref)


def interior(inputs, weight, n):
    channels, length = inputs.shape
    group = weight.shape[1]
    outs = [((channels, length // n), BF16, True)] * n
    outs += [((channels, length), F32, True), ((channels, length + 2 * DILATION_STEP), BF16, True)]
    outs += [((3, channels, group), BF16, True)] * 2
    results = kernel_call(
        "interior", functools.partial(interior_kernel, n), [(inputs, False), (weight, False)], outs,
        [pltpu.VMEM((3, group, channels), BF16), DMA, DMA],
    )
    return results[:n], *results[n:]


def in_end(block_index, block, at_end, length):
    first = at_end * (length - DILATION_STEP)
    return (block_index * block >= first) & (block_index * block < first + DILATION_STEP)


def near_kernel(ks, waits, near_ref, *rest):
    plain_ref = rest[waits]
    n = len(ks)
    slope_ref, wide = rest[-(n + 2):-n]
    active_refs = rest[-n:]
    ch, at_end = lax.axis_index("ch"), 1 - odd_place()
    length, halo = slope_ref.shape[1], near_ref.shape[1]
    block = length // n
    wide[:, lanes(at_end * (halo + length), halo)] = near_ref[...]
    for k, active_ref in zip(ks, active_refs):
        @pl.when(in_end(ch ^ k, block, at_end, length))
        def _(k=k, active_ref=active_ref):
            convolve_block(plain_ref, wide, (ch ^ k) * block, active_ref, slope_ref)


def near_end(near, waited, plain, slope, wide, away, here, active):
    held = [active[k] for k in here]
    operands = [(o, True) for o in (near, *waited, plain, slope, wide, *held)]
    outs = [slope, wide, *[active[k] for k in away], *held]
    first_held, at = 2 + len(away), 2 + len(waited)
    results = kernel_call(
        "near_end", functools.partial(near_kernel, away + here, len(waited)), operands,
        [(o.shape, o.dtype, True) for o in outs],
        aliases={at: 0, at + 1: 1, **{at + 2 + i: first_held + i for i in range(len(here))}},
    )
    return results[0], results[1], dict(zip(away + here, results[2:]))


def far_kernel(ks, _, __, far_ref, plain_ref, *rest):
    n = len(ks)
    slope_ref, wide = rest[-(n + 2):-n]
    ch, at_end = lax.axis_index("ch"), odd_place()
    length, halo = slope_ref.shape[1], far_ref.shape[1]
    block = length // n
    wide[:, lanes(at_end * (halo + length), halo)] = far_ref[...]
    for k, active_ref in zip(ks, rest[-n:]):
        @pl.when(in_end(ch ^ k, block, at_end, length))
        def _(k=k, active_ref=active_ref):
            convolve_block(plain_ref, wide, (ch ^ k) * block, active_ref, slope_ref)


def far_end(far, plain, slope, wide, ks, active):
    outs = [slope, wide, *[active[k] for k in ks]]
    results = kernel_call(
        "far_end", functools.partial(far_kernel, ks), [(o, True) for o in (slope, wide, far, plain, *outs[2:])],
        [(o.shape, o.dtype, True) for o in outs],
        aliases={0: 0, 1: 1, **{2 + i: i for i in range(2, len(outs))}},
    )
    return results[0], dict(zip(ks, results[2:]))


def grad_kernel(ks, slope_ref, *rest):
    up_refs, (grad_ref, near_out, far_out) = rest[:-3], rest[-3:]
    ch, odd = lax.axis_index("ch"), odd_place()
    length, halo = grad_ref.shape[1], near_out.shape[1]
    block = length // len(ks)
    for k, up_ref in zip(ks, up_refs):
        here = lanes((ch ^ k) * block, block)
        grad_ref[:, here] = (up_ref[...].astype(F32) * slope_ref[:, here]).astype(BF16)
    near_out[...] = grad_ref[:, lanes((1 - odd) * (length - halo), halo)]
    far_out[...] = grad_ref[:, lanes(odd * (length - halo), halo)]


def grad_conv(slope, ks, ups):
    end = (slope.shape[0], DILATION_STEP)
    return kernel_call(
        "grad_conv", functools.partial(grad_kernel, ks), [(o, True) for o in (slope, *[ups[k] for k in ks])],
        [(slope.shape, BF16, True), (end, BF16, True), (end, BF16, True)],
    )


def columns_times(order, pw_ref, rows, pieces):
    channels = pieces.shape[0] // len(order)
    if channels % 128 != 0:
        return dot(pw_ref[rows, :], pieces)
    return sum(
        dot(
            pw_ref[rows, lanes((lax.axis_index("ch") ^ k) * channels, channels)],
            pieces[place * channels:(place + 1) * channels],
        )
        for place, k in enumerate(order)
    )


def gather(counts, refs, gathered):
    width = gathered.shape[1]
    inner = is_inner(lax.axis_index("ch"), width, lax.axis_size("ch") * width)
    refs, at = list(refs), 0
    channels = refs[0].shape[0]
    for count in counts:
        rows = slice(at, at + channels)
        if count == 1:
            gathered[rows, :] = refs.pop(0)[...]
        else:
            early, late = refs.pop(0), refs.pop(0)

            @pl.when(inner)
            def _(rows=rows, early=early):
                gathered[rows, :] = early[...]

            @pl.when(jnp.logical_not(inner))
            def _(rows=rows, late=late):
                gathered[rows, :] = late[...]
        at += channels


def mix_kernel(order, counts, *refs):
    refs = refs[-sum(counts) - 3:]
    pw_ref, piece_refs, sum_ref, gathered = refs[0], refs[1:-2], refs[-2], refs[-1]
    gather(counts, piece_refs, gathered)
    pieces = gathered[...]
    step = 512
    for m in range(0, sum_ref.shape[0], step):
        rows = slice(m, m + step)
        sum_ref[rows, :] = columns_times(order, pw_ref, rows, pieces)


def mix(name, pw_weight, order, active, waited):
    channels, width = active[order[0]][0].shape
    operands = [*waited, columns_of(pw_weight, channels, order), *[p for k in order for p in active[k]]]
    return kernel_call(
        name, functools.partial(mix_kernel, order, [len(active[k]) for k in order]),
        [(o, True) for o in operands], [((pw_weight.shape[0], width), F32, True)],
        [pltpu.VMEM((len(order) * channels, width), BF16)],
    )


def back_interior_kernel(grad_ref, turned_ref, *rest):
    out_ref, ends_ref, held, sem = rest[-4:]
    channels, length = grad_ref.shape
    group, halo, unit = turned_ref.shape[2], DILATION_STEP, 256

    def taps(rows, start, which):
        return sum(
            dot(turned_ref[t, rows, :], grad_ref[rows, start + (t - 1) * halo:start + (t - 1) * halo + unit])
            for t in which
        )

    groups = [slice(g, g + group) for g in range(0, channels, group)]
    for rows in groups:
        for s in range(0, length - 2 * halo, unit):
            held[rows, s:s + unit] = taps(rows, halo + s, (0, 1, 2)).astype(BF16)
    copy = pltpu.make_async_copy(held, out_ref.at[:, halo:length - halo], sem)
    copy.start()
    for rows in groups:
        for s in range(0, halo, unit):
            ends_ref[rows, s:s + unit] = taps(rows, s, (1, 2))
            ends_ref[rows, halo + s:halo + s + unit] = taps(rows, length - halo + s, (0, 1))
    copy.wait()


def back_end(halo_ref, ends_ref, turned_ref, at_end, held):
    channels, halo = halo_ref.shape
    group, unit = turned_ref.shape[2], 256
    for g in range(0, channels, group):
        rows = slice(g, g + group)
        for s in range(0, halo, unit):
            outer = dot(turned_ref[2 * at_end, rows, :], halo_ref[rows, s:s + unit])
            held[rows, s:s + unit] = (ends_ref[rows, lanes(at_end * halo + s, unit)] + outer).astype(BF16)


def end_of(out_ref, at_end):
    return out_ref.at[:, lanes(at_end * (out_ref.shape[1] - DILATION_STEP), DILATION_STEP)]


def tail_kernel(order, counts, near_ref, far_ref, sum_ref, pw_ref, *rest):
    piece_refs, rest = rest[:-10], rest[-10:]
    ends_ref, turned_ref, _, mixed_ref, out_ref, gathered, held, both, sems, end_sems = rest
    copies = []

    def send(source, place, sem):
        copies.append(pltpu.make_async_copy(source, place, sem))
        copies[-1].start()

    gather(counts, piece_refs, gathered)
    pieces = gathered[...]
    step = 512
    for m in range(0, sum_ref.shape[0], step):
        rows = slice(m, m + step)
        held[rows, :] = (sum_ref[rows, :] + columns_times(order, pw_ref, rows, pieces)).astype(BF16)
        send(held.at[rows, :], mixed_ref.at[rows, :], sems.at[m // step])
    odd = odd_place()
    for place, (halo_ref, at_end) in enumerate(((near_ref, 1 - odd), (far_ref, odd))):
        back_end(halo_ref, ends_ref, turned_ref, at_end, both.at[place])
        send(both.at[place], end_of(out_ref, at_end), end_sems.at[place])
    for copy in copies:
        copy.wait()


def tail(near, far, partial, pw_weight, order, active, ends, turned, grad_inputs):
    channels = far.shape[0]
    operands = [near, far, partial, columns_of(pw_weight, channels, order)]
    operands += [*[p for k in order for p in active[k]], ends, turned]
    operands = [(o, True) for o in operands] + [(grad_inputs, False)]
    return kernel_call(
        "tail", functools.partial(tail_kernel, order, [len(active[k]) for k in order]), operands,
        [(partial.shape, BF16, False), (grad_inputs.shape, BF16, False)],
        [
            pltpu.VMEM((len(order) * channels, partial.shape[1]), BF16), pltpu.VMEM(partial.shape, BF16),
            pltpu.VMEM((2, *far.shape), BF16), DMA((partial.shape[0] // 512,)), DMA((2,)),
        ],
        {len(operands) - 1: 1},
    )


def exchange(piece, k):
    if k == 0:
        return piece
    return lax.ppermute(piece, "ch", [(i, i ^ k) for i in range(lax.axis_size("ch"))])


def exchange_part(piece, k, inner):
    n, block = lax.axis_size("ch"), piece.shape[1]
    return lax.ppermute(
        piece, "ch", [(i, i ^ k) for i in range(n) if is_inner(i ^ k, block, n * block) == inner]
    )


def swap(values, first):
    size = lax.axis_size("ctx")
    pairs = [(i, i + 1) for i in range(first, size - 1, 2)]
    return lax.ppermute(values, "ctx", pairs + [(b, a) for a, b in pairs])


def body(inputs, conv_weight, pw_weight, cotangent):
    n = lax.axis_size("ch")
    channels, length = inputs.shape
    halo = DILATION_STEP
    order = list(range(n - 1, -1, -1))
    first, second, rest = order[:n // 4], order[n // 4:n // 2], order[n // 2:]

    weight = jnp.swapaxes(conv_weight, 1, 2)
    if channels % 128 != 0:
        weight = lax.dynamic_slice_in_dim(weight, lax.axis_index("ch") * channels, channels, 2)
    pieces, cot_in, near = upstream(pw_weight, cotangent, inputs, first, True)
    near = swap(near, 0)
    ups = {k: exchange(p, k) for k, p in zip(first, pieces)}
    pieces, far = upstream(pw_weight, cot_in, inputs, second + rest, False)
    ups.update({k: exchange(p, k) for k, p in zip(second + rest, pieces)})
    far = swap(far, 1)

    active, slope, wide, plain, turned = interior(inputs, weight, n)
    inner = {k: exchange_part(active[k], k, True) for k in first}
    waited = [ups[k] for k in first + [k for k in rest if k > 0]]
    slope, wide, active = near_end(near, waited, plain, slope, wide, first, second + rest, active)
    slope, active = far_end(far, plain, slope, wide, order, active)
    grad, near_grad, far_grad = grad_conv(slope, order, ups)
    near_grad, far_grad = swap(near_grad, 0), swap(far_grad, 1)
    active = {
        k: (inner[k], exchange_part(active[k], k, False)) if k in first else (exchange(active[k], k),)
        for k in order
    }

    grad_inputs, ends = kernel_call(
        "back_interior", back_interior_kernel,
        [(grad, True), (turned, True), *[(inner[k], True) for k in first]],
        [((channels, length), BF16, False), ((channels, 2 * halo), F32, True)],
        [pltpu.VMEM((channels, length - 2 * halo), BF16), DMA],
    )
    (partial,) = mix("early_mix", pw_weight, second + rest, active, [ends])
    return tuple(tail(near_grad, far_grad, partial, pw_weight, first, active, ends, turned, grad_inputs))


def solution(mesh):
    placed = (P("ch", "ctx"), P(), P(), P(None, ("ctx", "ch")))
    return jax.shard_map(
        body,
        mesh=mesh,
        in_specs=placed,
        out_specs=(P(None, ("ctx", "ch")), P("ch", "ctx")),
        check_vma=False,
    )
```

```python
import functools

import jax
import jax.numpy as jnp
from jax import lax
from jax.experimental import pallas as pl
from jax.experimental.pallas import tpu as pltpu
from jax.sharding import PartitionSpec as P

DILATION_STEP = 512
UPSTREAM_ROWS = 512
BF16, F32 = jnp.bfloat16, jnp.float32
ANY = pl.BlockSpec(memory_space=pl.ANY)
INSIDE = pl.BlockSpec(memory_space=pltpu.VMEM)
DMA = pltpu.SemaphoreType.DMA


def kernel_call(name, kernel, operands, outs, scratch=(), aliases=None):
    return pl.pallas_call(
        kernel,
        in_specs=[INSIDE if held else ANY for _, held in operands],
        out_specs=[INSIDE if held else ANY for _, _, held in outs],
        out_shape=[
            pltpu.VMEM(shape, kind) if held else jax.ShapeDtypeStruct(shape, kind)
            for shape, kind, held in outs
        ],
        scratch_shapes=list(scratch),
        input_output_aliases=aliases or {},
        compiler_params=pltpu.CompilerParams(vmem_limit_bytes=16 << 20),
        name=name,
    )(*[
        pltpu.with_memory_space_constraint(array, pltpu.VMEM if held else pltpu.HBM)
        for array, held in operands
    ])


def gelu_and_slope(v):
    square = v * v
    inner = v * (0.7978845608 + (0.7978845608 * 0.044715) * square)
    th = jnp.tanh(inner)
    half = 0.5 + 0.5 * th
    active = v * half
    inner_slope = 0.7978845608 + (3.0 * 0.7978845608 * 0.044715) * square
    slope = half + (0.5 * v) * (1.0 - th * th) * inner_slope
    return active, slope


def lanes(start, size):
    return pl.ds(pl.multiple_of(start, 128), size)


def dot(a, b):
    return jnp.dot(a, b, preferred_element_type=F32)


def turned_dot(a, b):
    return lax.dot_general(a, b, (((0,), (0,)), ((), ())), preferred_element_type=F32)


def odd_place():
    return lax.axis_index("ctx") % 2


def end_copy(x_ref, end_ref, at_end, sem):
    length, halo = x_ref.shape[1], end_ref.shape[1]
    return pltpu.make_async_copy(x_ref.at[:, lanes(at_end * (length - halo), halo)], end_ref, sem)


def near_source_kernel(x_ref, near_ref, sem):
    copy = end_copy(x_ref, near_ref, 1 - odd_place(), sem)
    copy.start()
    copy.wait()


def upstream_kernel(order, channels, first, pw_ref, cot_ref, x_ref, *rest):
    count = len(order)
    piece_refs, rest = rest[:count], rest[count:]
    columns_ref, total_ref, sems = rest[-3:]
    cot_in = rest[0] if first else cot_ref
    ch = lax.axis_index("ch")
    blocks = []
    for m in range(0, cot_in.shape[0], UPSTREAM_ROWS):
        rows = slice(m, m + UPSTREAM_ROWS)
        pairs = [(cot_ref.at[rows], cot_in.at[rows])] if first else []
        if channels % 128 == 0:
            for place, k in enumerate(order):
                columns = lanes((ch ^ k) * channels, channels)
                held = slice(place * channels, (place + 1) * channels)
                pairs.append((pw_ref.at[rows, columns], columns_ref.at[rows, held]))
        else:
            pairs.append((pw_ref.at[rows], columns_ref.at[rows]))
        copies = [
            pltpu.make_async_copy(source, place, sems.at[len(blocks), i])
            for i, (source, place) in enumerate(pairs)
        ]
        for copy in copies:
            copy.start()
        blocks.append((rows, copies))
    if not first:
        end = end_copy(x_ref, rest[-4], odd_place(), sems.at[0, count + 1])
        end.start()
    for step, (rows, copies) in enumerate(blocks):
        for copy in copies:
            copy.wait()
        for place in range(count):
            held = slice(place * channels, (place + 1) * channels)
            part = turned_dot(columns_ref[rows, held], cot_in[rows, :])
            if step > 0:
                part = part + total_ref[held, :]
            if step < len(blocks) - 1:
                total_ref[held, :] = part
            else:
                piece_refs[place][...] = part.astype(BF16)
    if not first:
        end.wait()


def columns_of(pw_weight, channels, order):
    if channels % 128 == 0:
        return pw_weight
    ch = lax.axis_index("ch")
    return jnp.concatenate(
        [lax.dynamic_slice_in_dim(pw_weight, (ch ^ k) * channels, channels, 1) for k in order], axis=1
    )


def upstream(pw_weight, cotangent, inputs, order, first):
    channels = inputs.shape[0]
    total, width = cotangent.shape
    count = len(order)
    outs = [((channels, width), BF16, True)] * count
    outs += [(cotangent.shape, BF16, True)] * first
    outs += [((channels, DILATION_STEP), BF16, True)] * (not first)
    results = kernel_call(
        "upstream", functools.partial(upstream_kernel, order, channels, first),
        [(columns_of(pw_weight, channels, order), False), (cotangent, not first), (inputs, False)], outs,
        [
            pltpu.VMEM((total, count * channels), BF16), pltpu.VMEM((count * channels, width), F32),
            DMA((total // UPSTREAM_ROWS, count + 2)),
        ],
    )
    return results[:count], *results[count:]


def convolve(w_ref, rows, wide, start, halo, unit):
    return sum(dot(w_ref[t, rows, :], wide[rows, lanes(start + t * halo, unit)]) for t in range(3))


def interior_kernel(n, x_ref, w_ref, *rest):
    active_refs, (slope_ref, wide, plain_ref, turned_ref, own_ref, sem, own_sem) = rest[:n], rest[n:]
    ch = lax.axis_index("ch")
    channels, length = x_ref.shape
    group = w_ref.shape[1]
    own = w_ref.at[:, :, lanes(ch * channels, channels)] if w_ref.shape[2] > channels else w_ref
    own_copy = pltpu.make_async_copy(own, own_ref, own_sem)
    own_copy.start()
    halo = DILATION_STEP
    block = length // n
    unit = min(block, 256)
    copy = pltpu.make_async_copy(x_ref, wide.at[:, halo:halo + length], sem)
    copy.start()
    groups = [slice(g, g + group) for g in range(0, channels, group)]
    own_copy.wait()
    for t in range(3):
        for rows in groups:
            square = own_ref[t, :, rows]
            turned_ref[2 - t, rows, :] = square
            plain_ref[t, rows, :] = square.T
    copy.wait()
    for k in range(n):
        base = (ch ^ k) * block

        @pl.when((base >= halo) & (base < length - halo))
        def _(k=k, base=base):
            for s in range(0, block, unit):
                for rows in groups:
                    active, slope = gelu_and_slope(convolve(plain_ref, rows, wide, base + s, halo, unit))
                    active_refs[k][rows, s:s + unit] = active.astype(BF16)
                    slope_ref[rows, lanes(base + s, unit)] = slope


def interior(inputs, weight, n):
    channels, length = inputs.shape
    group = weight.shape[1]
    block = length // n
    outs = [((channels, block), BF16, True)] * n
    outs += [((channels, length), F32, True), ((channels, length + 2 * DILATION_STEP), BF16, True)]
    outs += [((3, channels, group), BF16, True)] * 2
    results = kernel_call(
        "interior", functools.partial(interior_kernel, n), [(inputs, False), (weight, False)], outs,
        [pltpu.VMEM((3, group, channels), BF16), DMA, DMA],
    )
    return results[:n], *results[n:]


def end_kernel(n, near, waits, *refs):
    halo_ref, plain_ref, rest = refs[waits], refs[waits + 1], refs[-(n + 2):]
    active_refs, (slope_ref, wide) = rest[:n], rest[n:]
    ch, odd = lax.axis_index("ch"), odd_place()
    channels, length = slope_ref.shape
    group = plain_ref.shape[2]
    halo = halo_ref.shape[1]
    block = length // n
    unit = min(block, 256)
    groups = [slice(g, g + group) for g in range(0, channels, group)]
    at_end = 1 - odd if near else odd
    wide[:, lanes(at_end * (halo + length), halo)] = halo_ref[...]
    first = at_end * (length - halo)
    for k in range(n):
        base = (ch ^ k) * block

        @pl.when((base >= first) & (base < first + halo))
        def _(k=k, base=base):
            for s in range(0, block, unit):
                for rows in groups:
                    active, slope = gelu_and_slope(convolve(plain_ref, rows, wide, base + s, halo, unit))
                    active_refs[k][rows, s:s + unit] = active.astype(BF16)
                    slope_ref[rows, lanes(base + s, unit)] = slope


def one_end(near, halo, plain, active, slope, wide, waited):
    n = len(active)
    operands = [(o, True) for o in (*waited, halo, plain, *active, slope, wide)]
    results = kernel_call(
        "near_end" if near else "far_end", functools.partial(end_kernel, n, near, len(waited)), operands,
        [(a.shape, a.dtype, True) for a in (*active, slope, wide)],
        aliases={len(waited) + 2 + i: i for i in range(n + 2)},
    )
    return results[:n], *results[n:]


def grad_kernel(order, slope_ref, *rest):
    up_refs, (grad_ref, near_out, far_out) = rest[:-3], rest[-3:]
    ch, odd = lax.axis_index("ch"), odd_place()
    length, halo = grad_ref.shape[1], near_out.shape[1]
    block = up_refs[0].shape[1]
    for k, up_ref in zip(order, up_refs):
        here = lanes((ch ^ k) * block, block)
        grad_ref[:, here] = (up_ref[...].astype(F32) * slope_ref[:, here]).astype(BF16)
    near_out[...] = grad_ref[:, lanes((1 - odd) * (length - halo), halo)]
    far_out[...] = grad_ref[:, lanes(odd * (length - halo), halo)]


def grad_conv(slope, order, ups):
    channels = slope.shape[0]
    return kernel_call(
        "grad_conv", functools.partial(grad_kernel, order),
        [(o, True) for o in (slope, *[ups[k] for k in order])],
        [(slope.shape, BF16, True)] + [((channels, DILATION_STEP), BF16, True)] * 2,
    )


def columns_times(order, pw_ref, rows, pieces):
    channels = pieces.shape[0] // len(order)
    if channels % 128 != 0:
        return dot(pw_ref[rows, :], pieces)
    return sum(
        dot(
            pw_ref[rows, lanes((lax.axis_index("ch") ^ k) * channels, channels)],
            pieces[place * channels:(place + 1) * channels],
        )
        for place, k in enumerate(order)
    )


def mix_kernel(order, pw_ref, *rest):
    piece_refs, before, sum_ref = rest[:len(order)], rest[len(order):-1], rest[-1]
    pieces = jnp.concatenate([p[...] for p in piece_refs], axis=0)
    step = 512
    for m in range(0, sum_ref.shape[0], step):
        rows = slice(m, m + step)
        part = columns_times(order, pw_ref, rows, pieces)
        sum_ref[rows, :] = part + before[0][rows, :] if before else part


def mix(name, pw_weight, order, active, before):
    channels, width = active[order[0]].shape
    operands = [columns_of(pw_weight, channels, order), *[active[k] for k in order], *before]
    return kernel_call(
        name, functools.partial(mix_kernel, order), [(o, True) for o in operands],
        [((pw_weight.shape[0], width), F32, True)],
        aliases={len(operands) - 1: 0} if before else {},
    )


def back_interior_kernel(grad_ref, turned_ref, out_ref, ends_ref, held, sem):
    channels, length = grad_ref.shape
    group, halo, unit = turned_ref.shape[2], DILATION_STEP, 256

    def taps(rows, start, which):
        return sum(
            dot(turned_ref[t, rows, :], grad_ref[rows, start + (t - 1) * halo:start + (t - 1) * halo + unit])
            for t in which
        )

    groups = [slice(g, g + group) for g in range(0, channels, group)]
    for rows in groups:
        for s in range(0, length - 2 * halo, unit):
            held[rows, s:s + unit] = taps(rows, halo + s, (0, 1, 2)).astype(BF16)
    copy = pltpu.make_async_copy(held, out_ref.at[:, halo:length - halo], sem)
    copy.start()
    for rows in groups:
        for s in range(0, halo, unit):
            ends_ref[rows, s:s + unit] = taps(rows, s, (1, 2))
            ends_ref[rows, halo + s:halo + s + unit] = taps(rows, length - halo + s, (0, 1))
    copy.wait()


def back_end(halo_ref, ends_ref, turned_ref, at_end, held):
    channels, halo = halo_ref.shape
    group, unit = turned_ref.shape[2], 256
    for g in range(0, channels, group):
        rows = slice(g, g + group)
        for s in range(0, halo, unit):
            outer = dot(turned_ref[2 * at_end, rows, :], halo_ref[rows, s:s + unit])
            held[rows, s:s + unit] = (ends_ref[rows, lanes(at_end * halo + s, unit)] + outer).astype(BF16)


def end_of(out_ref, at_end):
    return out_ref.at[:, lanes(at_end * (out_ref.shape[1] - DILATION_STEP), DILATION_STEP)]


def tail_kernel(order, near_ref, far_ref, pw_ref, sum_ref, *rest):
    piece_refs, rest = rest[:len(order)], rest[len(order):]
    ends_ref, turned_ref, _, mixed_ref, out_ref, held, both, sems = rest
    pieces = jnp.concatenate([p[...] for p in piece_refs], axis=0)
    copies = []

    def send(source, place):
        copies.append(pltpu.make_async_copy(source, place, sems.at[len(copies)]))
        copies[-1].start()

    step = 512
    for m in range(0, sum_ref.shape[0], step):
        rows = slice(m, m + step)
        held[rows, :] = (sum_ref[rows, :] + columns_times(order, pw_ref, rows, pieces)).astype(BF16)
        send(held.at[rows, :], mixed_ref.at[rows, :])
    odd = odd_place()
    for place, (halo_ref, at_end) in enumerate(((near_ref, 1 - odd), (far_ref, odd))):
        back_end(halo_ref, ends_ref, turned_ref, at_end, both.at[place])
        send(both.at[place], end_of(out_ref, at_end))
    for copy in copies:
        copy.wait()


def tail(pw_weight, order, partial, active, near, far, ends, turned, grad_inputs):
    channels, halo = near.shape
    operands = [near, far, columns_of(pw_weight, channels, order), partial, *[active[k] for k in order]]
    operands = [(o, True) for o in (*operands, ends, turned)] + [(grad_inputs, False)]
    return kernel_call(
        "tail", functools.partial(tail_kernel, order), operands,
        [(partial.shape, BF16, False), (grad_inputs.shape, BF16, False)],
        [
            pltpu.VMEM(partial.shape, BF16), pltpu.VMEM((2, channels, halo), BF16),
            DMA((partial.shape[0] // 512 + 2,)),
        ],
        {len(operands) - 1: 1},
    )


def exchange(piece, k):
    if k == 0:
        return piece
    return lax.ppermute(piece, "ch", [(i, i ^ k) for i in range(lax.axis_size("ch"))])


def swap(values, first):
    size = lax.axis_size("ctx")
    pairs = [(i, i + 1) for i in range(first, size - 1, 2)]
    return lax.ppermute(values, "ctx", pairs + [(b, a) for a, b in pairs])


def body(inputs, conv_weight, pw_weight, cotangent):
    n = lax.axis_size("ch")
    channels, length = inputs.shape
    halo = DILATION_STEP
    order = list(range(n - 1, -1, -1))
    first, second, rest = order[:n // 4], order[n // 4:n // 2], order[n // 2:]

    weight = jnp.swapaxes(conv_weight, 1, 2)
    if channels % 128 != 0:
        weight = lax.dynamic_slice_in_dim(weight, lax.axis_index("ch") * channels, channels, 2)
    (near,) = kernel_call(
        "near_source", near_source_kernel, [(inputs, False)], [((channels, halo), BF16, True)], [DMA]
    )
    near = swap(near, 0)
    pieces, cot_in = upstream(pw_weight, cotangent, inputs, first, True)
    ups = {k: exchange(p, k) for k, p in zip(first, pieces)}
    pieces, far = upstream(pw_weight, cot_in, inputs, second + rest, False)
    ups.update({k: exchange(p, k) for k, p in zip(second + rest, pieces)})
    far = swap(far, 1)

    active, slope, wide, plain, turned = interior(inputs, weight, n)
    active, slope, wide = one_end(True, near, plain, active, slope, wide, [ups[first[0]]])
    active, slope, wide = one_end(False, far, plain, active, slope, wide, [])
    grad, near_grad, far_grad = grad_conv(slope, order, ups)
    active = {k: exchange(active[k], k) for k in order}
    near_grad, far_grad = swap(near_grad, 0), swap(far_grad, 1)

    grad_inputs, ends = kernel_call(
        "back_interior", back_interior_kernel, [(grad, True), (turned, True)],
        [((channels, length), BF16, False), ((channels, 2 * halo), F32, True)],
        [pltpu.VMEM((channels, length - 2 * halo), BF16), DMA],
    )
    partial = mix("early_mix", pw_weight, first, active, [])
    (partial,) = mix("half_mix", pw_weight, rest, active, partial)
    return tuple(tail(pw_weight, second, partial, active, near_grad, far_grad, ends, turned, grad_inputs))


def solution(mesh):
    placed = (P("ch", "ctx"), P(), P(), P(None, ("ctx", "ch")))
    return jax.shard_map(
        body,
        mesh=mesh,
        in_specs=placed,
        out_specs=(P(None, ("ctx", "ch")), P("ch", "ctx")),
        check_vma=False,
    )
```

```python
import functools

import jax
import jax.numpy as jnp
from jax import lax
from jax.experimental import pallas as pl
from jax.experimental.pallas import tpu as pltpu
from jax.sharding import PartitionSpec as P

DILATION_STEP = 512
UPSTREAM_ROWS = 512
BF16, F32 = jnp.bfloat16, jnp.float32
ANY = pl.BlockSpec(memory_space=pl.ANY)
INSIDE = pl.BlockSpec(memory_space=pltpu.VMEM)
DMA = pltpu.SemaphoreType.DMA


def kernel_call(name, kernel, operands, outs, scratch=(), aliases=None):
    return pl.pallas_call(
        kernel,
        in_specs=[INSIDE if held else ANY for _, held in operands],
        out_specs=[INSIDE if held else ANY for _, _, held in outs],
        out_shape=[
            pltpu.VMEM(shape, kind) if held else jax.ShapeDtypeStruct(shape, kind)
            for shape, kind, held in outs
        ],
        scratch_shapes=list(scratch),
        input_output_aliases=aliases or {},
        compiler_params=pltpu.CompilerParams(vmem_limit_bytes=16 << 20),
        name=name,
    )(*[
        pltpu.with_memory_space_constraint(array, pltpu.VMEM if held else pltpu.HBM)
        for array, held in operands
    ])


def gelu_and_slope(v):
    square = v * v
    inner = v * (0.7978845608 + (0.7978845608 * 0.044715) * square)
    th = jnp.tanh(inner)
    half = 0.5 + 0.5 * th
    active = v * half
    inner_slope = 0.7978845608 + (3.0 * 0.7978845608 * 0.044715) * square
    slope = half + (0.5 * v) * (1.0 - th * th) * inner_slope
    return active, slope


def lanes(start, size):
    return pl.ds(pl.multiple_of(start, 128), size)


def dot(a, b):
    return jnp.dot(a, b, preferred_element_type=F32)


def turned_dot(a, b):
    return lax.dot_general(a, b, (((0,), (0,)), ((), ())), preferred_element_type=F32)


def odd_place():
    return lax.axis_index("ctx") % 2


def end_copy(x_ref, end_ref, at_end, sem):
    length, halo = x_ref.shape[1], end_ref.shape[1]
    return pltpu.make_async_copy(x_ref.at[:, lanes(at_end * (length - halo), halo)], end_ref, sem)


def near_source_kernel(x_ref, near_ref, sem):
    copy = end_copy(x_ref, near_ref, 1 - odd_place(), sem)
    copy.start()
    copy.wait()


def upstream_kernel(order, channels, first, with_far, pw_ref, cot_ref, x_ref, *rest):
    count = len(order)
    piece_refs, rest = rest[:count], rest[count:]
    columns_ref, total_ref, sems = rest[-3:]
    cot_in = rest[0] if first else cot_ref
    ch = lax.axis_index("ch")
    blocks = []
    for m in range(0, cot_in.shape[0], UPSTREAM_ROWS):
        rows = slice(m, m + UPSTREAM_ROWS)
        pairs = [(cot_ref.at[rows], cot_in.at[rows])] if first else []
        if channels % 128 == 0:
            for place, k in enumerate(order):
                columns = lanes((ch ^ k) * channels, channels)
                held = slice(place * channels, (place + 1) * channels)
                pairs.append((pw_ref.at[rows, columns], columns_ref.at[rows, held]))
        else:
            pairs.append((pw_ref.at[rows], columns_ref.at[rows]))
        copies = [
            pltpu.make_async_copy(source, place, sems.at[len(blocks), i])
            for i, (source, place) in enumerate(pairs)
        ]
        for copy in copies:
            copy.start()
        blocks.append((rows, copies))
    if with_far:
        end = end_copy(x_ref, rest[-4], odd_place(), sems.at[0, count + 1])
        end.start()
    for step, (rows, copies) in enumerate(blocks):
        for copy in copies:
            copy.wait()
        for place in range(count):
            held = slice(place * channels, (place + 1) * channels)
            part = turned_dot(columns_ref[rows, held], cot_in[rows, :])
            if step > 0:
                part = part + total_ref[held, :]
            if step < len(blocks) - 1:
                total_ref[held, :] = part
            else:
                piece_refs[place][...] = part.astype(BF16)
    if with_far:
        end.wait()


def columns_of(pw_weight, channels, order):
    if channels % 128 == 0:
        return pw_weight
    ch = lax.axis_index("ch")
    return jnp.concatenate(
        [lax.dynamic_slice_in_dim(pw_weight, (ch ^ k) * channels, channels, 1) for k in order], axis=1
    )


def upstream(pw_weight, cotangent, inputs, order, first=False, with_far=False):
    channels = inputs.shape[0]
    total, width = cotangent.shape
    count = len(order)
    outs = [((channels, width), BF16, True)] * count
    outs += [(cotangent.shape, BF16, True)] * first
    outs += [((channels, DILATION_STEP), BF16, True)] * with_far
    results = kernel_call(
        "upstream", functools.partial(upstream_kernel, order, channels, first, with_far),
        [(columns_of(pw_weight, channels, order), False), (cotangent, not first), (inputs, False)], outs,
        [
            pltpu.VMEM((total, count * channels), BF16), pltpu.VMEM((count * channels, width), F32),
            DMA((total // UPSTREAM_ROWS, count + 2)),
        ],
    )
    return results[:count], *results[count:]


def convolve(w_ref, rows, wide, start, halo, unit):
    return sum(dot(w_ref[t, rows, :], wide[rows, lanes(start + t * halo, unit)]) for t in range(3))


def interior_kernel(n, x_ref, w_ref, *rest):
    active_refs, (slope_ref, wide, plain_ref, turned_ref, own_ref, sem, own_sem) = rest[:n], rest[n:]
    ch = lax.axis_index("ch")
    channels, length = x_ref.shape
    group = w_ref.shape[1]
    own = w_ref.at[:, :, lanes(ch * channels, channels)] if w_ref.shape[2] > channels else w_ref
    own_copy = pltpu.make_async_copy(own, own_ref, own_sem)
    own_copy.start()
    halo = DILATION_STEP
    block = length // n
    unit = min(block, 256)
    copy = pltpu.make_async_copy(x_ref, wide.at[:, halo:halo + length], sem)
    copy.start()
    groups = [slice(g, g + group) for g in range(0, channels, group)]
    own_copy.wait()
    for t in range(3):
        for rows in groups:
            square = own_ref[t, :, rows]
            turned_ref[2 - t, rows, :] = square
            plain_ref[t, rows, :] = square.T
    copy.wait()
    for k in range(n):
        base = (ch ^ k) * block

        @pl.when((base >= halo) & (base < length - halo))
        def _(k=k, base=base):
            for s in range(0, block, unit):
                for rows in groups:
                    active, slope = gelu_and_slope(convolve(plain_ref, rows, wide, base + s, halo, unit))
                    active_refs[k][rows, s:s + unit] = active.astype(BF16)
                    slope_ref[rows, lanes(base + s, unit)] = slope


def interior(inputs, weight, n):
    channels, length = inputs.shape
    group = weight.shape[1]
    block = length // n
    outs = [((channels, block), BF16, True)] * n
    outs += [((channels, length), F32, True), ((channels, length + 2 * DILATION_STEP), BF16, True)]
    outs += [((3, channels, group), BF16, True)] * 2
    results = kernel_call(
        "interior", functools.partial(interior_kernel, n), [(inputs, False), (weight, False)], outs,
        [pltpu.VMEM((3, group, channels), BF16), DMA, DMA],
    )
    return results[:n], *results[n:]


def end_kernel(n, near, waits, *refs):
    halo_ref, plain_ref, rest = refs[waits], refs[waits + 1], refs[-(n + 2):]
    active_refs, (slope_ref, wide) = rest[:n], rest[n:]
    ch, odd = lax.axis_index("ch"), odd_place()
    channels, length = slope_ref.shape
    group = plain_ref.shape[2]
    halo = halo_ref.shape[1]
    block = length // n
    unit = min(block, 256)
    groups = [slice(g, g + group) for g in range(0, channels, group)]
    at_end = 1 - odd if near else odd
    wide[:, lanes(at_end * (halo + length), halo)] = halo_ref[...]
    first = at_end * (length - halo)
    for k in range(n):
        base = (ch ^ k) * block

        @pl.when((base >= first) & (base < first + halo))
        def _(k=k, base=base):
            for s in range(0, block, unit):
                for rows in groups:
                    active, slope = gelu_and_slope(convolve(plain_ref, rows, wide, base + s, halo, unit))
                    active_refs[k][rows, s:s + unit] = active.astype(BF16)
                    slope_ref[rows, lanes(base + s, unit)] = slope


def one_end(near, halo, plain, active, slope, wide, waited):
    n = len(active)
    operands = [(o, True) for o in (*waited, halo, plain, *active, slope, wide)]
    results = kernel_call(
        "near_end" if near else "far_end", functools.partial(end_kernel, n, near, len(waited)), operands,
        [(a.shape, a.dtype, True) for a in (*active, slope, wide)],
        aliases={len(waited) + 2 + i: i for i in range(n + 2)},
    )
    return results[:n], *results[n:]


def grad_kernel(order, slope_ref, *rest):
    up_refs, (grad_ref, near_out, far_out) = rest[:-3], rest[-3:]
    ch, odd = lax.axis_index("ch"), odd_place()
    length, halo = grad_ref.shape[1], near_out.shape[1]
    block = up_refs[0].shape[1]
    for k, up_ref in zip(order, up_refs):
        here = lanes((ch ^ k) * block, block)
        grad_ref[:, here] = (up_ref[...].astype(F32) * slope_ref[:, here]).astype(BF16)
    near_out[...] = grad_ref[:, lanes((1 - odd) * (length - halo), halo)]
    far_out[...] = grad_ref[:, lanes(odd * (length - halo), halo)]


def grad_conv(slope, order, ups):
    channels = slope.shape[0]
    return kernel_call(
        "grad_conv", functools.partial(grad_kernel, order),
        [(o, True) for o in (slope, *[ups[k] for k in order])],
        [(slope.shape, BF16, True)] + [((channels, DILATION_STEP), BF16, True)] * 2,
    )


def columns_times(order, pw_ref, rows, pieces):
    channels = pieces.shape[0] // len(order)
    if channels % 128 != 0:
        return dot(pw_ref[rows, :], pieces)
    return sum(
        dot(
            pw_ref[rows, lanes((lax.axis_index("ch") ^ k) * channels, channels)],
            pieces[place * channels:(place + 1) * channels],
        )
        for place, k in enumerate(order)
    )


def mix_kernel(order, pw_ref, *rest):
    piece_refs, before, sum_ref = rest[:len(order)], rest[len(order):-1], rest[-1]
    pieces = jnp.concatenate([p[...] for p in piece_refs], axis=0)
    step = 512
    for m in range(0, sum_ref.shape[0], step):
        rows = slice(m, m + step)
        part = columns_times(order, pw_ref, rows, pieces)
        sum_ref[rows, :] = part + before[0][rows, :] if before else part


def mix(name, pw_weight, order, active, before):
    channels, width = active[order[0]].shape
    operands = [columns_of(pw_weight, channels, order), *[active[k] for k in order], *before]
    return kernel_call(
        name, functools.partial(mix_kernel, order), [(o, True) for o in operands],
        [((pw_weight.shape[0], width), F32, True)],
        aliases={len(operands) - 1: 0} if before else {},
    )


def back_interior_kernel(grad_ref, turned_ref, out_ref, ends_ref, held, sem):
    channels, length = grad_ref.shape
    group, halo, unit = turned_ref.shape[2], DILATION_STEP, 256

    def taps(rows, start, which):
        return sum(
            dot(turned_ref[t, rows, :], grad_ref[rows, start + (t - 1) * halo:start + (t - 1) * halo + unit])
            for t in which
        )

    groups = [slice(g, g + group) for g in range(0, channels, group)]
    for rows in groups:
        for s in range(0, length - 2 * halo, unit):
            held[rows, s:s + unit] = taps(rows, halo + s, (0, 1, 2)).astype(BF16)
    copy = pltpu.make_async_copy(held, out_ref.at[:, halo:length - halo], sem)
    copy.start()
    for rows in groups:
        for s in range(0, halo, unit):
            ends_ref[rows, s:s + unit] = taps(rows, s, (1, 2))
            ends_ref[rows, halo + s:halo + s + unit] = taps(rows, length - halo + s, (0, 1))
    copy.wait()


def back_end(halo_ref, ends_ref, turned_ref, at_end, held):
    channels, halo = halo_ref.shape
    group, unit = turned_ref.shape[2], 256
    for g in range(0, channels, group):
        rows = slice(g, g + group)
        for s in range(0, halo, unit):
            outer = dot(turned_ref[2 * at_end, rows, :], halo_ref[rows, s:s + unit])
            held[rows, s:s + unit] = (ends_ref[rows, lanes(at_end * halo + s, unit)] + outer).astype(BF16)


def end_of(out_ref, at_end):
    return out_ref.at[:, lanes(at_end * (out_ref.shape[1] - DILATION_STEP), DILATION_STEP)]


def tail_kernel(order, near_ref, far_ref, pw_ref, sum_ref, *rest):
    piece_refs, rest = rest[:len(order)], rest[len(order):]
    ends_ref, turned_ref, _, mixed_ref, out_ref, held, both, sems = rest
    pieces = jnp.concatenate([p[...] for p in piece_refs], axis=0)
    copies = []

    def send(source, place):
        copies.append(pltpu.make_async_copy(source, place, sems.at[len(copies)]))
        copies[-1].start()

    step = 512
    for m in range(0, sum_ref.shape[0], step):
        rows = slice(m, m + step)
        held[rows, :] = (sum_ref[rows, :] + columns_times(order, pw_ref, rows, pieces)).astype(BF16)
        send(held.at[rows, :], mixed_ref.at[rows, :])
    odd = odd_place()
    for place, (halo_ref, at_end) in enumerate(((near_ref, 1 - odd), (far_ref, odd))):
        back_end(halo_ref, ends_ref, turned_ref, at_end, both.at[place])
        send(both.at[place], end_of(out_ref, at_end))
    for copy in copies:
        copy.wait()


def tail(pw_weight, order, partial, active, near, far, ends, turned, grad_inputs):
    channels, halo = near.shape
    operands = [near, far, columns_of(pw_weight, channels, order), partial, *[active[k] for k in order]]
    operands = [(o, True) for o in (*operands, ends, turned)] + [(grad_inputs, False)]
    return kernel_call(
        "tail", functools.partial(tail_kernel, order), operands,
        [(partial.shape, BF16, False), (grad_inputs.shape, BF16, False)],
        [
            pltpu.VMEM(partial.shape, BF16), pltpu.VMEM((2, channels, halo), BF16),
            DMA((partial.shape[0] // 512 + 2,)),
        ],
        {len(operands) - 1: 1},
    )


def exchange(piece, k):
    if k == 0:
        return piece
    return lax.ppermute(piece, "ch", [(i, i ^ k) for i in range(lax.axis_size("ch"))])


def swap(values, first):
    size = lax.axis_size("ctx")
    pairs = [(i, i + 1) for i in range(first, size - 1, 2)]
    return lax.ppermute(values, "ctx", pairs + [(b, a) for a, b in pairs])


def body(inputs, conv_weight, pw_weight, cotangent):
    n = lax.axis_size("ch")
    channels, length = inputs.shape
    halo = DILATION_STEP
    order = list(range(n - 1, -1, -1))
    first, second, rest = order[:n // 4], order[n // 4:n // 2], order[n // 2:]

    weight = jnp.swapaxes(conv_weight, 1, 2)
    if channels % 128 != 0:
        weight = lax.dynamic_slice_in_dim(weight, lax.axis_index("ch") * channels, channels, 2)
    (near,) = kernel_call(
        "near_source", near_source_kernel, [(inputs, False)], [((channels, halo), BF16, True)], [DMA]
    )
    near = swap(near, 0)
    pieces, cot_in = upstream(pw_weight, cotangent, inputs, first, first=True)
    ups = {k: exchange(p, k) for k, p in zip(first, pieces)}
    pieces, far = upstream(pw_weight, cot_in, inputs, second, with_far=True)
    far = swap(far, 1)
    ups.update({k: exchange(p, k) for k, p in zip(second, pieces)})
    (pieces,) = upstream(pw_weight, cot_in, inputs, rest)
    ups.update({k: exchange(p, k) for k, p in zip(rest, pieces)})

    active, slope, wide, plain, turned = interior(inputs, weight, n)
    active, slope, wide = one_end(True, near, plain, active, slope, wide, [ups[first[0]]])
    active, slope, wide = one_end(False, far, plain, active, slope, wide, [])
    grad, near_grad, far_grad = grad_conv(slope, rest + second + first, ups)
    active = {k: exchange(active[k], k) for k in order}
    near_grad, far_grad = swap(near_grad, 0), swap(far_grad, 1)

    grad_inputs, ends = kernel_call(
        "back_interior", back_interior_kernel, [(grad, True), (turned, True)],
        [((channels, length), BF16, False), ((channels, 2 * halo), F32, True)],
        [pltpu.VMEM((channels, length - 2 * halo), BF16), DMA],
    )
    partial = mix("early_mix", pw_weight, first, active, [])
    (partial,) = mix("half_mix", pw_weight, rest, active, partial)
    return tuple(tail(pw_weight, second, partial, active, near_grad, far_grad, ends, turned, grad_inputs))


def solution(mesh):
    placed = (P("ch", "ctx"), P(), P(), P(None, ("ctx", "ch")))
    return jax.shard_map(
        body,
        mesh=mesh,
        in_specs=placed,
        out_specs=(P(None, ("ctx", "ch")), P("ch", "ctx")),
        check_vma=False,
    )
```

```python
import functools

import jax
import jax.numpy as jnp
from jax import lax
from jax.experimental import pallas as pl
from jax.experimental.pallas import tpu as pltpu
from jax.sharding import PartitionSpec as P

DILATION_STEP = 512
UPSTREAM_ROWS = 512
BF16, F32 = jnp.bfloat16, jnp.float32
ANY = pl.BlockSpec(memory_space=pl.ANY)
INSIDE = pl.BlockSpec(memory_space=pltpu.VMEM)
DMA = pltpu.SemaphoreType.DMA


def kernel_call(name, kernel, operands, outs, scratch=(), aliases=None):
    return pl.pallas_call(
        kernel,
        in_specs=[INSIDE if held else ANY for _, held in operands],
        out_specs=[INSIDE if held else ANY for _, _, held in outs],
        out_shape=[
            pltpu.VMEM(shape, kind) if held else jax.ShapeDtypeStruct(shape, kind)
            for shape, kind, held in outs
        ],
        scratch_shapes=list(scratch),
        input_output_aliases=aliases or {},
        compiler_params=pltpu.CompilerParams(vmem_limit_bytes=16 << 20),
        name=name,
    )(*[
        pltpu.with_memory_space_constraint(array, pltpu.VMEM if held else pltpu.HBM)
        for array, held in operands
    ])


def gelu_and_slope(v):
    square = v * v
    inner = v * (0.7978845608 + (0.7978845608 * 0.044715) * square)
    th = jnp.tanh(inner)
    half = 0.5 + 0.5 * th
    active = v * half
    inner_slope = 0.7978845608 + (3.0 * 0.7978845608 * 0.044715) * square
    slope = half + (0.5 * v) * (1.0 - th * th) * inner_slope
    return active, slope


def lanes(start, size):
    return pl.ds(pl.multiple_of(start, 128), size)


def dot(a, b):
    return jnp.dot(a, b, preferred_element_type=F32)


def turned_dot(a, b):
    return lax.dot_general(a, b, (((0,), (0,)), ((), ())), preferred_element_type=F32)


def odd_place():
    return lax.axis_index("ctx") % 2


def end_copy(x_ref, end_ref, at_end, sem):
    length, halo = x_ref.shape[1], end_ref.shape[1]
    return pltpu.make_async_copy(x_ref.at[:, lanes(at_end * (length - halo), halo)], end_ref, sem)


def near_source_kernel(x_ref, near_ref, sem):
    copy = end_copy(x_ref, near_ref, 1 - odd_place(), sem)
    copy.start()
    copy.wait()


def upstream_kernel(order, channels, first, with_far, pw_ref, cot_ref, x_ref, *rest):
    count = len(order)
    piece_refs, rest = rest[:count], rest[count:]
    columns_ref, total_ref, sems = rest[-3:]
    cot_in = rest[0] if first else cot_ref
    ch = lax.axis_index("ch")
    blocks = []
    for m in range(0, cot_in.shape[0], UPSTREAM_ROWS):
        rows = slice(m, m + UPSTREAM_ROWS)
        pairs = [(cot_ref.at[rows], cot_in.at[rows])] if first else []
        if channels % 128 == 0:
            for place, k in enumerate(order):
                columns = lanes((ch ^ k) * channels, channels)
                held = slice(place * channels, (place + 1) * channels)
                pairs.append((pw_ref.at[rows, columns], columns_ref.at[rows, held]))
        else:
            pairs.append((pw_ref.at[rows], columns_ref.at[rows]))
        copies = [
            pltpu.make_async_copy(source, place, sems.at[len(blocks), i])
            for i, (source, place) in enumerate(pairs)
        ]
        for copy in copies:
            copy.start()
        blocks.append((rows, copies))
    if with_far:
        end = end_copy(x_ref, rest[-4], odd_place(), sems.at[0, count + 1])
        end.start()
    for step, (rows, copies) in enumerate(blocks):
        for copy in copies:
            copy.wait()
        for place in range(count):
            held = slice(place * channels, (place + 1) * channels)
            part = turned_dot(columns_ref[rows, held], cot_in[rows, :])
            if step > 0:
                part = part + total_ref[held, :]
            if step < len(blocks) - 1:
                total_ref[held, :] = part
            else:
                piece_refs[place][...] = part.astype(BF16)
    if with_far:
        end.wait()


def columns_of(pw_weight, channels, order):
    if channels % 128 == 0:
        return pw_weight
    ch = lax.axis_index("ch")
    return jnp.concatenate(
        [lax.dynamic_slice_in_dim(pw_weight, (ch ^ k) * channels, channels, 1) for k in order], axis=1
    )


def upstream(pw_weight, cotangent, inputs, order, first=False, with_far=False):
    channels = inputs.shape[0]
    total, width = cotangent.shape
    count = len(order)
    outs = [((channels, width), BF16, True)] * count
    outs += [(cotangent.shape, BF16, True)] * first
    outs += [((channels, DILATION_STEP), BF16, True)] * with_far
    results = kernel_call(
        "upstream", functools.partial(upstream_kernel, order, channels, first, with_far),
        [(columns_of(pw_weight, channels, order), False), (cotangent, not first), (inputs, False)], outs,
        [
            pltpu.VMEM((total, count * channels), BF16), pltpu.VMEM((count * channels, width), F32),
            DMA((total // UPSTREAM_ROWS, count + 2)),
        ],
    )
    return results[:count], *results[count:]


def convolve(w_ref, rows, wide, start, halo, unit):
    return sum(dot(w_ref[t, rows, :], wide[rows, lanes(start + t * halo, unit)]) for t in range(3))


def interior_kernel(n, x_ref, w_ref, *rest):
    active_refs, (slope_ref, wide, plain_ref, turned_ref, own_ref, sem, own_sem) = rest[:n], rest[n:]
    ch = lax.axis_index("ch")
    channels, length = x_ref.shape
    group = w_ref.shape[1]
    own = w_ref.at[:, :, lanes(ch * channels, channels)] if w_ref.shape[2] > channels else w_ref
    own_copy = pltpu.make_async_copy(own, own_ref, own_sem)
    own_copy.start()
    halo = DILATION_STEP
    block = length // n
    unit = min(block, 256)
    copy = pltpu.make_async_copy(x_ref, wide.at[:, halo:halo + length], sem)
    copy.start()
    groups = [slice(g, g + group) for g in range(0, channels, group)]
    own_copy.wait()
    for t in range(3):
        for rows in groups:
            square = own_ref[t, :, rows]
            turned_ref[2 - t, rows, :] = square
            plain_ref[t, rows, :] = square.T
    copy.wait()
    for k in range(n):
        base = (ch ^ k) * block

        @pl.when((base >= halo) & (base < length - halo))
        def _(k=k, base=base):
            for s in range(0, block, unit):
                for rows in groups:
                    active, slope = gelu_and_slope(convolve(plain_ref, rows, wide, base + s, halo, unit))
                    active_refs[k][rows, s:s + unit] = active.astype(BF16)
                    slope_ref[rows, lanes(base + s, unit)] = slope


def interior(inputs, weight, n):
    channels, length = inputs.shape
    group = weight.shape[1]
    block = length // n
    outs = [((channels, block), BF16, True)] * n
    outs += [((channels, length), F32, True), ((channels, length + 2 * DILATION_STEP), BF16, True)]
    outs += [((3, channels, group), BF16, True)] * 2
    results = kernel_call(
        "interior", functools.partial(interior_kernel, n), [(inputs, False), (weight, False)], outs,
        [pltpu.VMEM((3, group, channels), BF16), DMA, DMA],
    )
    return results[:n], *results[n:]


def end_kernel(n, near, waits, *refs):
    halo_ref, plain_ref, rest = refs[waits], refs[waits + 1], refs[-(n + 2):]
    active_refs, (slope_ref, wide) = rest[:n], rest[n:]
    ch, odd = lax.axis_index("ch"), odd_place()
    channels, length = slope_ref.shape
    group = plain_ref.shape[2]
    halo = halo_ref.shape[1]
    block = length // n
    unit = min(block, 256)
    groups = [slice(g, g + group) for g in range(0, channels, group)]
    at_end = 1 - odd if near else odd
    wide[:, lanes(at_end * (halo + length), halo)] = halo_ref[...]
    first = at_end * (length - halo)
    for k in range(n):
        base = (ch ^ k) * block

        @pl.when((base >= first) & (base < first + halo))
        def _(k=k, base=base):
            for s in range(0, block, unit):
                for rows in groups:
                    active, slope = gelu_and_slope(convolve(plain_ref, rows, wide, base + s, halo, unit))
                    active_refs[k][rows, s:s + unit] = active.astype(BF16)
                    slope_ref[rows, lanes(base + s, unit)] = slope


def one_end(near, halo, plain, active, slope, wide, waited):
    n = len(active)
    operands = [(o, True) for o in (*waited, halo, plain, *active, slope, wide)]
    results = kernel_call(
        "near_end" if near else "far_end", functools.partial(end_kernel, n, near, len(waited)), operands,
        [(a.shape, a.dtype, True) for a in (*active, slope, wide)],
        aliases={len(waited) + 2 + i: i for i in range(n + 2)},
    )
    return results[:n], *results[n:]


def grad_kernel(order, slope_ref, *rest):
    up_refs, (grad_ref, near_out, far_out) = rest[:-3], rest[-3:]
    ch, odd = lax.axis_index("ch"), odd_place()
    length, halo = grad_ref.shape[1], near_out.shape[1]
    block = up_refs[0].shape[1]
    for k, up_ref in zip(order, up_refs):
        here = lanes((ch ^ k) * block, block)
        grad_ref[:, here] = (up_ref[...].astype(F32) * slope_ref[:, here]).astype(BF16)
    near_out[...] = grad_ref[:, lanes((1 - odd) * (length - halo), halo)]
    far_out[...] = grad_ref[:, lanes(odd * (length - halo), halo)]


def grad_conv(slope, order, ups):
    channels = slope.shape[0]
    return kernel_call(
        "grad_conv", functools.partial(grad_kernel, order),
        [(o, True) for o in (slope, *[ups[k] for k in order])],
        [(slope.shape, BF16, True)] + [((channels, DILATION_STEP), BF16, True)] * 2,
    )


def columns_times(order, pw_ref, rows, pieces):
    channels = pieces.shape[0] // len(order)
    if channels % 128 != 0:
        return dot(pw_ref[rows, :], pieces)
    return sum(
        dot(
            pw_ref[rows, lanes((lax.axis_index("ch") ^ k) * channels, channels)],
            pieces[place * channels:(place + 1) * channels],
        )
        for place, k in enumerate(order)
    )


def mix_kernel(order, pw_ref, *rest):
    piece_refs, before, sum_ref = rest[:len(order)], rest[len(order):-1], rest[-1]
    pieces = jnp.concatenate([p[...] for p in piece_refs], axis=0)
    step = 512
    for m in range(0, sum_ref.shape[0], step):
        rows = slice(m, m + step)
        part = columns_times(order, pw_ref, rows, pieces)
        sum_ref[rows, :] = part + before[0][rows, :] if before else part


def mix(name, pw_weight, order, active, before):
    channels, width = active[order[0]].shape
    operands = [columns_of(pw_weight, channels, order), *[active[k] for k in order], *before]
    return kernel_call(
        name, functools.partial(mix_kernel, order), [(o, True) for o in operands],
        [((pw_weight.shape[0], width), F32, True)],
        aliases={len(operands) - 1: 0} if before else {},
    )


def back_interior_kernel(grad_ref, turned_ref, out_ref, ends_ref, held, sem):
    channels, length = grad_ref.shape
    group, halo, unit = turned_ref.shape[2], DILATION_STEP, 256

    def taps(rows, start, which):
        return sum(
            dot(turned_ref[t, rows, :], grad_ref[rows, start + (t - 1) * halo:start + (t - 1) * halo + unit])
            for t in which
        )

    groups = [slice(g, g + group) for g in range(0, channels, group)]
    for rows in groups:
        for s in range(0, length - 2 * halo, unit):
            held[rows, s:s + unit] = taps(rows, halo + s, (0, 1, 2)).astype(BF16)
    copy = pltpu.make_async_copy(held, out_ref.at[:, halo:length - halo], sem)
    copy.start()
    for rows in groups:
        for s in range(0, halo, unit):
            ends_ref[rows, s:s + unit] = taps(rows, s, (1, 2))
            ends_ref[rows, halo + s:halo + s + unit] = taps(rows, length - halo + s, (0, 1))
    copy.wait()


def back_end(halo_ref, ends_ref, turned_ref, at_end, held):
    channels, halo = halo_ref.shape
    group, unit = turned_ref.shape[2], 256
    for g in range(0, channels, group):
        rows = slice(g, g + group)
        for s in range(0, halo, unit):
            outer = dot(turned_ref[2 * at_end, rows, :], halo_ref[rows, s:s + unit])
            held[rows, s:s + unit] = (ends_ref[rows, lanes(at_end * halo + s, unit)] + outer).astype(BF16)


def end_of(out_ref, at_end):
    return out_ref.at[:, lanes(at_end * (out_ref.shape[1] - DILATION_STEP), DILATION_STEP)]


def tail_kernel(order, near_ref, far_ref, pw_ref, sum_ref, *rest):
    piece_refs, rest = rest[:len(order)], rest[len(order):]
    ends_ref, turned_ref, _, mixed_ref, out_ref, held, both, sems = rest
    pieces = jnp.concatenate([p[...] for p in piece_refs], axis=0)
    copies = []

    def send(source, place):
        copies.append(pltpu.make_async_copy(source, place, sems.at[len(copies)]))
        copies[-1].start()

    step = 512
    for m in range(0, sum_ref.shape[0], step):
        rows = slice(m, m + step)
        held[rows, :] = (sum_ref[rows, :] + columns_times(order, pw_ref, rows, pieces)).astype(BF16)
        send(held.at[rows, :], mixed_ref.at[rows, :])
    odd = odd_place()
    for place, (halo_ref, at_end) in enumerate(((near_ref, 1 - odd), (far_ref, odd))):
        back_end(halo_ref, ends_ref, turned_ref, at_end, both.at[place])
        send(both.at[place], end_of(out_ref, at_end))
    for copy in copies:
        copy.wait()


def tail(pw_weight, order, partial, active, near, far, ends, turned, grad_inputs):
    channels, halo = near.shape
    operands = [near, far, columns_of(pw_weight, channels, order), partial, *[active[k] for k in order]]
    operands = [(o, True) for o in (*operands, ends, turned)] + [(grad_inputs, False)]
    return kernel_call(
        "tail", functools.partial(tail_kernel, order), operands,
        [(partial.shape, BF16, False), (grad_inputs.shape, BF16, False)],
        [
            pltpu.VMEM(partial.shape, BF16), pltpu.VMEM((2, channels, halo), BF16),
            DMA((partial.shape[0] // 512 + 2,)),
        ],
        {len(operands) - 1: 1},
    )


def arrived(arrays):
    return kernel_call(
        "arrived", lambda *refs: None, [(o, True) for o in arrays], [(o.shape, o.dtype, True) for o in arrays],
        aliases={i: i for i in range(len(arrays))},
    )


def exchange(piece, k):
    if k == 0:
        return piece
    return lax.ppermute(piece, "ch", [(i, i ^ k) for i in range(lax.axis_size("ch"))])


def swap(values, first):
    size = lax.axis_size("ctx")
    pairs = [(i, i + 1) for i in range(first, size - 1, 2)]
    return lax.ppermute(values, "ctx", pairs + [(b, a) for a, b in pairs])


def body(inputs, conv_weight, pw_weight, cotangent):
    n = lax.axis_size("ch")
    channels, length = inputs.shape
    halo = DILATION_STEP
    order = list(range(n - 1, -1, -1))
    first, second, rest = order[:n // 4], order[n // 4:n // 2], order[n // 2:]

    weight = jnp.swapaxes(conv_weight, 1, 2)
    if channels % 128 != 0:
        weight = lax.dynamic_slice_in_dim(weight, lax.axis_index("ch") * channels, channels, 2)
    (near,) = kernel_call(
        "near_source", near_source_kernel, [(inputs, False)], [((channels, halo), BF16, True)], [DMA]
    )
    near = swap(near, 0)
    pieces, cot_in = upstream(pw_weight, cotangent, inputs, first, first=True)
    ups = {k: exchange(p, k) for k, p in zip(first, pieces)}
    pieces, far = upstream(pw_weight, cot_in, inputs, second, with_far=True)
    far = swap(far, 1)
    ups.update({k: exchange(p, k) for k, p in zip(second, pieces)})
    (pieces,) = upstream(pw_weight, cot_in, inputs, rest)
    ups.update({k: exchange(p, k) for k, p in zip(rest, pieces)})

    active, slope, wide, plain, turned = interior(inputs, weight, n)
    active, slope, wide = one_end(True, near, plain, active, slope, wide, [ups[first[0]]])
    active, slope, wide = one_end(False, far, plain, active, slope, wide, [])
    ups.update(zip(second, arrived([ups[k] for k in second])))
    grad, near_grad, far_grad = grad_conv(slope, order, ups)
    active = {k: exchange(active[k], k) for k in order}
    near_grad, far_grad = swap(near_grad, 0), swap(far_grad, 1)

    grad_inputs, ends = kernel_call(
        "back_interior", back_interior_kernel, [(grad, True), (turned, True)],
        [((channels, length), BF16, False), ((channels, 2 * halo), F32, True)],
        [pltpu.VMEM((channels, length - 2 * halo), BF16), DMA],
    )
    partial = mix("early_mix", pw_weight, first, active, [])
    (partial,) = mix("half_mix", pw_weight, rest, active, partial)
    return tuple(tail(pw_weight, second, partial, active, near_grad, far_grad, ends, turned, grad_inputs))


def solution(mesh):
    placed = (P("ch", "ctx"), P(), P(), P(None, ("ctx", "ch")))
    return jax.shard_map(
        body,
        mesh=mesh,
        in_specs=placed,
        out_specs=(P(None, ("ctx", "ch")), P("ch", "ctx")),
        check_vma=False,
    )
```

```python
import functools

import jax
import jax.numpy as jnp
from jax import lax
from jax.experimental import pallas as pl
from jax.experimental.pallas import tpu as pltpu
from jax.sharding import PartitionSpec as P

DILATION_STEP = 512
UPSTREAM_ROWS = 512
BF16, F32 = jnp.bfloat16, jnp.float32
ANY = pl.BlockSpec(memory_space=pl.ANY)
INSIDE = pl.BlockSpec(memory_space=pltpu.VMEM)
DMA = pltpu.SemaphoreType.DMA


def kernel_call(name, kernel, operands, outs, scratch=(), aliases=None):
    return pl.pallas_call(
        kernel,
        in_specs=[INSIDE if held else ANY for _, held in operands],
        out_specs=[INSIDE if held else ANY for _, _, held in outs],
        out_shape=[
            pltpu.VMEM(shape, kind) if held else jax.ShapeDtypeStruct(shape, kind)
            for shape, kind, held in outs
        ],
        scratch_shapes=list(scratch),
        input_output_aliases=aliases or {},
        compiler_params=pltpu.CompilerParams(vmem_limit_bytes=16 << 20),
        name=name,
    )(*[
        pltpu.with_memory_space_constraint(array, pltpu.VMEM if held else pltpu.HBM)
        for array, held in operands
    ])


def gelu_and_slope(v):
    square = v * v
    inner = v * (0.7978845608 + (0.7978845608 * 0.044715) * square)
    th = jnp.tanh(inner)
    half = 0.5 + 0.5 * th
    active = v * half
    inner_slope = 0.7978845608 + (3.0 * 0.7978845608 * 0.044715) * square
    slope = half + (0.5 * v) * (1.0 - th * th) * inner_slope
    return active, slope


def lanes(start, size):
    return pl.ds(pl.multiple_of(start, 128), size)


def dot(a, b):
    return jnp.dot(a, b, preferred_element_type=F32)


def turned_dot(a, b):
    return lax.dot_general(a, b, (((0,), (0,)), ((), ())), preferred_element_type=F32)


def odd_place():
    return lax.axis_index("ctx") % 2


def end_copy(x_ref, end_ref, at_end, sem):
    length, halo = x_ref.shape[1], end_ref.shape[1]
    return pltpu.make_async_copy(x_ref.at[:, lanes(at_end * (length - halo), halo)], end_ref, sem)


def near_source_kernel(x_ref, near_ref, sem):
    copy = end_copy(x_ref, near_ref, 1 - odd_place(), sem)
    copy.start()
    copy.wait()


def upstream_kernel(order, channels, first, with_far, pw_ref, cot_ref, x_ref, *rest):
    count = len(order)
    piece_refs, rest = rest[:count], rest[count:]
    columns_ref, total_ref, sems = rest[-3:]
    cot_in = rest[0] if first else cot_ref
    ch = lax.axis_index("ch")
    blocks = []
    for m in range(0, cot_in.shape[0], UPSTREAM_ROWS):
        rows = slice(m, m + UPSTREAM_ROWS)
        pairs = [(cot_ref.at[rows], cot_in.at[rows])] if first else []
        if channels % 128 == 0:
            for place, k in enumerate(order):
                columns = lanes((ch ^ k) * channels, channels)
                held = slice(place * channels, (place + 1) * channels)
                pairs.append((pw_ref.at[rows, columns], columns_ref.at[rows, held]))
        else:
            pairs.append((pw_ref.at[rows], columns_ref.at[rows]))
        copies = [
            pltpu.make_async_copy(source, place, sems.at[len(blocks), i])
            for i, (source, place) in enumerate(pairs)
        ]
        for copy in copies:
            copy.start()
        blocks.append((rows, copies))
    if with_far:
        end = end_copy(x_ref, rest[-4], odd_place(), sems.at[0, count + 1])
        end.start()
    for step, (rows, copies) in enumerate(blocks):
        for copy in copies:
            copy.wait()
        for place in range(count):
            held = slice(place * channels, (place + 1) * channels)
            part = turned_dot(columns_ref[rows, held], cot_in[rows, :])
            if step > 0:
                part = part + total_ref[held, :]
            if step < len(blocks) - 1:
                total_ref[held, :] = part
            else:
                piece_refs[place][...] = part.astype(BF16)
    if with_far:
        end.wait()


def columns_of(pw_weight, channels, order):
    if channels % 128 == 0:
        return pw_weight
    ch = lax.axis_index("ch")
    return jnp.concatenate(
        [lax.dynamic_slice_in_dim(pw_weight, (ch ^ k) * channels, channels, 1) for k in order], axis=1
    )


def upstream(pw_weight, cotangent, inputs, order, first=False, with_far=False):
    channels = inputs.shape[0]
    total, width = cotangent.shape
    count = len(order)
    outs = [((channels, width), BF16, True)] * count
    outs += [(cotangent.shape, BF16, True)] * first
    outs += [((channels, DILATION_STEP), BF16, True)] * with_far
    results = kernel_call(
        "upstream", functools.partial(upstream_kernel, order, channels, first, with_far),
        [(columns_of(pw_weight, channels, order), False), (cotangent, not first), (inputs, False)], outs,
        [
            pltpu.VMEM((total, count * channels), BF16), pltpu.VMEM((count * channels, width), F32),
            DMA((total // UPSTREAM_ROWS, count + 2)),
        ],
    )
    return results[:count], *results[count:]


def convolve(w_ref, rows, wide, start, halo, unit):
    return sum(dot(w_ref[t, rows, :], wide[rows, lanes(start + t * halo, unit)]) for t in range(3))


def interior_kernel(n, x_ref, w_ref, *rest):
    active_refs, (slope_ref, wide, plain_ref, turned_ref, own_ref, sem, own_sem) = rest[:n], rest[n:]
    ch = lax.axis_index("ch")
    channels, length = x_ref.shape
    group = w_ref.shape[1]
    own = w_ref.at[:, :, lanes(ch * channels, channels)] if w_ref.shape[2] > channels else w_ref
    own_copy = pltpu.make_async_copy(own, own_ref, own_sem)
    own_copy.start()
    halo = DILATION_STEP
    block = length // n
    unit = min(block, 256)
    copy = pltpu.make_async_copy(x_ref, wide.at[:, halo:halo + length], sem)
    copy.start()
    groups = [slice(g, g + group) for g in range(0, channels, group)]
    own_copy.wait()
    for t in range(3):
        for rows in groups:
            square = own_ref[t, :, rows]
            turned_ref[2 - t, rows, :] = square
            plain_ref[t, rows, :] = square.T
    copy.wait()
    for k in range(n):
        base = (ch ^ k) * block

        @pl.when((base >= halo) & (base < length - halo))
        def _(k=k, base=base):
            for s in range(0, block, unit):
                for rows in groups:
                    active, slope = gelu_and_slope(convolve(plain_ref, rows, wide, base + s, halo, unit))
                    active_refs[k][rows, s:s + unit] = active.astype(BF16)
                    slope_ref[rows, lanes(base + s, unit)] = slope


def interior(inputs, weight, n):
    channels, length = inputs.shape
    group = weight.shape[1]
    block = length // n
    outs = [((channels, block), BF16, True)] * n
    outs += [((channels, length), F32, True), ((channels, length + 2 * DILATION_STEP), BF16, True)]
    outs += [((3, channels, group), BF16, True)] * 2
    results = kernel_call(
        "interior", functools.partial(interior_kernel, n), [(inputs, False), (weight, False)], outs,
        [pltpu.VMEM((3, group, channels), BF16), DMA, DMA],
    )
    return results[:n], *results[n:]


def end_kernel(n, near, waits, *refs):
    halo_ref, plain_ref, rest = refs[waits], refs[waits + 1], refs[-(n + 2):]
    active_refs, (slope_ref, wide) = rest[:n], rest[n:]
    ch, odd = lax.axis_index("ch"), odd_place()
    channels, length = slope_ref.shape
    group = plain_ref.shape[2]
    halo = halo_ref.shape[1]
    block = length // n
    unit = min(block, 256)
    groups = [slice(g, g + group) for g in range(0, channels, group)]
    at_end = 1 - odd if near else odd
    wide[:, lanes(at_end * (halo + length), halo)] = halo_ref[...]
    first = at_end * (length - halo)
    for k in range(n):
        base = (ch ^ k) * block

        @pl.when((base >= first) & (base < first + halo))
        def _(k=k, base=base):
            for s in range(0, block, unit):
                for rows in groups:
                    active, slope = gelu_and_slope(convolve(plain_ref, rows, wide, base + s, halo, unit))
                    active_refs[k][rows, s:s + unit] = active.astype(BF16)
                    slope_ref[rows, lanes(base + s, unit)] = slope


def one_end(near, halo, plain, active, slope, wide, waited):
    n = len(active)
    operands = [(o, True) for o in (*waited, halo, plain, *active, slope, wide)]
    results = kernel_call(
        "near_end" if near else "far_end", functools.partial(end_kernel, n, near, len(waited)), operands,
        [(a.shape, a.dtype, True) for a in (*active, slope, wide)],
        aliases={len(waited) + 2 + i: i for i in range(n + 2)},
    )
    return results[:n], *results[n:]


def grad_kernel(order, slope_ref, *rest):
    up_refs, (grad_ref, near_out, far_out) = rest[:-3], rest[-3:]
    ch, odd = lax.axis_index("ch"), odd_place()
    length, halo = grad_ref.shape[1], near_out.shape[1]
    block = up_refs[0].shape[1]
    for k, up_ref in zip(order, up_refs):
        here = lanes((ch ^ k) * block, block)
        grad_ref[:, here] = (up_ref[...].astype(F32) * slope_ref[:, here]).astype(BF16)
    near_out[...] = grad_ref[:, lanes((1 - odd) * (length - halo), halo)]
    far_out[...] = grad_ref[:, lanes(odd * (length - halo), halo)]


def grad_conv(slope, order, ups):
    channels = slope.shape[0]
    return kernel_call(
        "grad_conv", functools.partial(grad_kernel, order),
        [(o, True) for o in (slope, *[ups[k] for k in order])],
        [(slope.shape, BF16, True)] + [((channels, DILATION_STEP), BF16, True)] * 2,
    )


def columns_times(order, pw_ref, rows, pieces):
    channels = pieces.shape[0] // len(order)
    if channels % 128 != 0:
        return dot(pw_ref[rows, :], pieces)
    return sum(
        dot(
            pw_ref[rows, lanes((lax.axis_index("ch") ^ k) * channels, channels)],
            pieces[place * channels:(place + 1) * channels],
        )
        for place, k in enumerate(order)
    )


def mix_kernel(order, pw_ref, *rest):
    piece_refs, before, sum_ref = rest[:len(order)], rest[len(order):-1], rest[-1]
    pieces = jnp.concatenate([p[...] for p in piece_refs], axis=0)
    step = 512
    for m in range(0, sum_ref.shape[0], step):
        rows = slice(m, m + step)
        part = columns_times(order, pw_ref, rows, pieces)
        sum_ref[rows, :] = part + before[0][rows, :] if before else part


def mix(name, pw_weight, order, active, before):
    channels, width = active[order[0]].shape
    operands = [columns_of(pw_weight, channels, order), *[active[k] for k in order], *before]
    return kernel_call(
        name, functools.partial(mix_kernel, order), [(o, True) for o in operands],
        [((pw_weight.shape[0], width), F32, True)],
        aliases={len(operands) - 1: 0} if before else {},
    )


def back_interior_kernel(grad_ref, turned_ref, out_ref, ends_ref, held, sem):
    channels, length = grad_ref.shape
    group, halo, unit = turned_ref.shape[2], DILATION_STEP, 256

    def taps(rows, start, which):
        return sum(
            dot(turned_ref[t, rows, :], grad_ref[rows, start + (t - 1) * halo:start + (t - 1) * halo + unit])
            for t in which
        )

    groups = [slice(g, g + group) for g in range(0, channels, group)]
    for rows in groups:
        for s in range(0, length - 2 * halo, unit):
            held[rows, s:s + unit] = taps(rows, halo + s, (0, 1, 2)).astype(BF16)
    copy = pltpu.make_async_copy(held, out_ref.at[:, halo:length - halo], sem)
    copy.start()
    for rows in groups:
        for s in range(0, halo, unit):
            ends_ref[rows, s:s + unit] = taps(rows, s, (1, 2))
            ends_ref[rows, halo + s:halo + s + unit] = taps(rows, length - halo + s, (0, 1))
    copy.wait()


def back_end(halo_ref, ends_ref, turned_ref, at_end, held):
    channels, halo = halo_ref.shape
    group, unit = turned_ref.shape[2], 256
    for g in range(0, channels, group):
        rows = slice(g, g + group)
        for s in range(0, halo, unit):
            outer = dot(turned_ref[2 * at_end, rows, :], halo_ref[rows, s:s + unit])
            held[rows, s:s + unit] = (ends_ref[rows, lanes(at_end * halo + s, unit)] + outer).astype(BF16)


def end_of(out_ref, at_end):
    return out_ref.at[:, lanes(at_end * (out_ref.shape[1] - DILATION_STEP), DILATION_STEP)]


def late_mix_kernel(order, pw_ref, sum_ref, *rest):
    piece_refs, (out_ref, done_ref, held, sems) = rest[:len(order)], rest[len(order):]
    pieces = jnp.concatenate([p[...] for p in piece_refs], axis=0)
    step = 512
    copies = []
    for m in range(0, sum_ref.shape[0], step):
        rows = slice(m, m + step)
        held[rows, :] = (sum_ref[rows, :] + columns_times(order, pw_ref, rows, pieces)).astype(BF16)
        copies.append(pltpu.make_async_copy(held.at[rows, :], out_ref.at[rows, :], sems.at[len(copies)]))
        copies[-1].start()
    done_ref[...] = jnp.zeros_like(done_ref)
    for copy in copies:
        copy.wait()


def late_mix(pw_weight, order, partial, active):
    channels = active[order[0]].shape[0]
    operands = [columns_of(pw_weight, channels, order), partial, *[active[k] for k in order]]
    return kernel_call(
        "late_mix", functools.partial(late_mix_kernel, order), [(o, True) for o in operands],
        [(partial.shape, BF16, False), ((8, 128), F32, True)],
        [pltpu.VMEM(partial.shape, BF16), DMA((partial.shape[0] // 512,))],
    )


def back_ends_kernel(near_ref, far_ref, ends_ref, turned_ref, _, __, out_ref, both, sems):
    odd = odd_place()
    copies = []
    for place, (halo_ref, at_end) in enumerate(((near_ref, 1 - odd), (far_ref, odd))):
        back_end(halo_ref, ends_ref, turned_ref, at_end, both.at[place])
        copies.append(pltpu.make_async_copy(both.at[place], end_of(out_ref, at_end), sems.at[place]))
        copies[-1].start()
    for copy in copies:
        copy.wait()


def back_ends(near, far, ends, turned, done, grad_inputs):
    operands = [(o, True) for o in (near, far, ends, turned, done)] + [(grad_inputs, False)]
    (result,) = kernel_call(
        "back_ends", back_ends_kernel, operands, [(grad_inputs.shape, BF16, False)],
        [pltpu.VMEM((2, *near.shape), BF16), DMA((2,))], {5: 0},
    )
    return result


def arrived(arrays):
    return kernel_call(
        "arrived", lambda *refs: None, [(o, True) for o in arrays], [(o.shape, o.dtype, True) for o in arrays],
        aliases={i: i for i in range(len(arrays))},
    )


def exchange(piece, k):
    if k == 0:
        return piece
    return lax.ppermute(piece, "ch", [(i, i ^ k) for i in range(lax.axis_size("ch"))])


def swap(values, first):
    size = lax.axis_size("ctx")
    pairs = [(i, i + 1) for i in range(first, size - 1, 2)]
    return lax.ppermute(values, "ctx", pairs + [(b, a) for a, b in pairs])


def body(inputs, conv_weight, pw_weight, cotangent):
    n = lax.axis_size("ch")
    channels, length = inputs.shape
    halo = DILATION_STEP
    order = list(range(n - 1, -1, -1))
    first, second, rest = order[:n // 4], order[n // 4:n // 2], order[n // 2:]

    weight = jnp.swapaxes(conv_weight, 1, 2)
    if channels % 128 != 0:
        weight = lax.dynamic_slice_in_dim(weight, lax.axis_index("ch") * channels, channels, 2)
    (near,) = kernel_call(
        "near_source", near_source_kernel, [(inputs, False)], [((channels, halo), BF16, True)], [DMA]
    )
    near = swap(near, 0)
    pieces, cot_in = upstream(pw_weight, cotangent, inputs, first, first=True)
    ups = {k: exchange(p, k) for k, p in zip(first, pieces)}
    pieces, far = upstream(pw_weight, cot_in, inputs, second, with_far=True)
    far = swap(far, 1)
    ups.update({k: exchange(p, k) for k, p in zip(second, pieces)})
    (pieces,) = upstream(pw_weight, cot_in, inputs, rest)
    ups.update({k: exchange(p, k) for k, p in zip(rest, pieces)})

    active, slope, wide, plain, turned = interior(inputs, weight, n)
    active, slope, wide = one_end(True, near, plain, active, slope, wide, [ups[first[0]]])
    active, slope, wide = one_end(False, far, plain, active, slope, wide, [])
    ups.update(zip(second, arrived([ups[k] for k in second])))
    grad, near_grad, far_grad = grad_conv(slope, order, ups)
    active = {k: exchange(active[k], k) for k in order}
    near_grad, far_grad = swap(near_grad, 0), swap(far_grad, 1)

    grad_inputs, ends = kernel_call(
        "back_interior", back_interior_kernel, [(grad, True), (turned, True)],
        [((channels, length), BF16, False), ((channels, 2 * halo), F32, True)],
        [pltpu.VMEM((channels, length - 2 * halo), BF16), DMA],
    )
    partial = mix("early_mix", pw_weight, first, active, [])
    (partial,) = mix("half_mix", pw_weight, rest, active, partial)
    mixed, done = late_mix(pw_weight, second, partial, active)
    return mixed, back_ends(near_grad, far_grad, ends, turned, done, grad_inputs)


def solution(mesh):
    placed = (P("ch", "ctx"), P(), P(), P(None, ("ctx", "ch")))
    return jax.shard_map(
        body,
        mesh=mesh,
        in_specs=placed,
        out_specs=(P(None, ("ctx", "ch")), P("ch", "ctx")),
        check_vma=False,
    )
```

```python
import functools

import jax
import jax.numpy as jnp
from jax import lax
from jax.experimental import pallas as pl
from jax.experimental.pallas import tpu as pltpu
from jax.sharding import PartitionSpec as P

DILATION_STEP = 512
UPSTREAM_ROWS = 512
BF16, F32 = jnp.bfloat16, jnp.float32
ANY = pl.BlockSpec(memory_space=pl.ANY)
INSIDE = pl.BlockSpec(memory_space=pltpu.VMEM)
DMA = pltpu.SemaphoreType.DMA


def kernel_call(name, kernel, operands, outs, scratch=(), aliases=None):
    return pl.pallas_call(
        kernel,
        in_specs=[INSIDE if held else ANY for _, held in operands],
        out_specs=[INSIDE if held else ANY for _, _, held in outs],
        out_shape=[
            pltpu.VMEM(shape, kind) if held else jax.ShapeDtypeStruct(shape, kind)
            for shape, kind, held in outs
        ],
        scratch_shapes=list(scratch),
        input_output_aliases=aliases or {},
        compiler_params=pltpu.CompilerParams(vmem_limit_bytes=16 << 20),
        name=name,
    )(*[
        pltpu.with_memory_space_constraint(array, pltpu.VMEM if held else pltpu.HBM)
        for array, held in operands
    ])


def gelu_and_slope(v):
    square = v * v
    inner = v * (0.7978845608 + (0.7978845608 * 0.044715) * square)
    th = jnp.tanh(inner)
    half = 0.5 + 0.5 * th
    active = v * half
    inner_slope = 0.7978845608 + (3.0 * 0.7978845608 * 0.044715) * square
    slope = half + (0.5 * v) * (1.0 - th * th) * inner_slope
    return active, slope


def lanes(start, size):
    return pl.ds(pl.multiple_of(start, 128), size)


def dot(a, b):
    return jnp.dot(a, b, preferred_element_type=F32)


def turned_dot(a, b):
    return lax.dot_general(a, b, (((0,), (0,)), ((), ())), preferred_element_type=F32)


def odd_place():
    return lax.axis_index("ctx") % 2


def end_copy(x_ref, end_ref, at_end, sem):
    length, halo = x_ref.shape[1], end_ref.shape[1]
    return pltpu.make_async_copy(x_ref.at[:, lanes(at_end * (length - halo), halo)], end_ref, sem)


def near_source_kernel(x_ref, near_ref, sem):
    copy = end_copy(x_ref, near_ref, 1 - odd_place(), sem)
    copy.start()
    copy.wait()


def upstream_kernel(order, channels, first, with_far, pw_ref, cot_ref, x_ref, *rest):
    count = len(order)
    piece_refs, rest = rest[:count], rest[count:]
    columns_ref, total_ref, sems = rest[-3:]
    cot_in = rest[0] if first else cot_ref
    ch = lax.axis_index("ch")
    blocks = []
    for m in range(0, cot_in.shape[0], UPSTREAM_ROWS):
        rows = slice(m, m + UPSTREAM_ROWS)
        pairs = [(cot_ref.at[rows], cot_in.at[rows])] if first else []
        if channels % 128 == 0:
            for place, k in enumerate(order):
                columns = lanes((ch ^ k) * channels, channels)
                held = slice(place * channels, (place + 1) * channels)
                pairs.append((pw_ref.at[rows, columns], columns_ref.at[rows, held]))
        else:
            pairs.append((pw_ref.at[rows], columns_ref.at[rows]))
        copies = [
            pltpu.make_async_copy(source, place, sems.at[len(blocks), i])
            for i, (source, place) in enumerate(pairs)
        ]
        for copy in copies:
            copy.start()
        blocks.append((rows, copies))
    if with_far:
        end = end_copy(x_ref, rest[-4], odd_place(), sems.at[0, count + 1])
        end.start()
    for step, (rows, copies) in enumerate(blocks):
        for copy in copies:
            copy.wait()
        for place in range(count):
            held = slice(place * channels, (place + 1) * channels)
            part = turned_dot(columns_ref[rows, held], cot_in[rows, :])
            if step > 0:
                part = part + total_ref[held, :]
            if step < len(blocks) - 1:
                total_ref[held, :] = part
            else:
                piece_refs[place][...] = part.astype(BF16)
    if with_far:
        end.wait()


def columns_of(pw_weight, channels, order):
    if channels % 128 == 0:
        return pw_weight
    ch = lax.axis_index("ch")
    return jnp.concatenate(
        [lax.dynamic_slice_in_dim(pw_weight, (ch ^ k) * channels, channels, 1) for k in order], axis=1
    )


def upstream(pw_weight, cotangent, inputs, order, first=False, with_far=False):
    channels = inputs.shape[0]
    total, width = cotangent.shape
    count = len(order)
    outs = [((channels, width), BF16, True)] * count
    outs += [(cotangent.shape, BF16, True)] * first
    outs += [((channels, DILATION_STEP), BF16, True)] * with_far
    results = kernel_call(
        "upstream", functools.partial(upstream_kernel, order, channels, first, with_far),
        [(columns_of(pw_weight, channels, order), False), (cotangent, not first), (inputs, False)], outs,
        [
            pltpu.VMEM((total, count * channels), BF16), pltpu.VMEM((count * channels, width), F32),
            DMA((total // UPSTREAM_ROWS, count + 2)),
        ],
    )
    return results[:count], *results[count:]


def convolve(w_ref, rows, wide, start, halo, unit):
    return sum(dot(w_ref[t, rows, :], wide[rows, lanes(start + t * halo, unit)]) for t in range(3))


def interior_kernel(n, x_ref, w_ref, *rest):
    active_refs, (slope_ref, wide, plain_ref, turned_ref, own_ref, sem, own_sem) = rest[:n], rest[n:]
    ch = lax.axis_index("ch")
    channels, length = x_ref.shape
    group = w_ref.shape[1]
    own = w_ref.at[:, :, lanes(ch * channels, channels)] if w_ref.shape[2] > channels else w_ref
    own_copy = pltpu.make_async_copy(own, own_ref, own_sem)
    own_copy.start()
    halo = DILATION_STEP
    block = length // n
    unit = min(block, 256)
    copy = pltpu.make_async_copy(x_ref, wide.at[:, halo:halo + length], sem)
    copy.start()
    groups = [slice(g, g + group) for g in range(0, channels, group)]
    own_copy.wait()
    for t in range(3):
        for rows in groups:
            square = own_ref[t, :, rows]
            turned_ref[2 - t, rows, :] = square
            plain_ref[t, rows, :] = square.T
    copy.wait()
    for k in range(n):
        base = (ch ^ k) * block

        @pl.when((base >= halo) & (base < length - halo))
        def _(k=k, base=base):
            for s in range(0, block, unit):
                for rows in groups:
                    active, slope = gelu_and_slope(convolve(plain_ref, rows, wide, base + s, halo, unit))
                    active_refs[k][rows, s:s + unit] = active.astype(BF16)
                    slope_ref[rows, lanes(base + s, unit)] = slope


def interior(inputs, weight, n):
    channels, length = inputs.shape
    group = weight.shape[1]
    block = length // n
    outs = [((channels, block), BF16, True)] * n
    outs += [((channels, length), F32, True), ((channels, length + 2 * DILATION_STEP), BF16, True)]
    outs += [((3, channels, group), BF16, True)] * 2
    results = kernel_call(
        "interior", functools.partial(interior_kernel, n), [(inputs, False), (weight, False)], outs,
        [pltpu.VMEM((3, group, channels), BF16), DMA, DMA],
    )
    return results[:n], *results[n:]


def end_kernel(n, near, waits, *refs):
    halo_ref, plain_ref, rest = refs[waits], refs[waits + 1], refs[-(n + 2):]
    active_refs, (slope_ref, wide) = rest[:n], rest[n:]
    ch, odd = lax.axis_index("ch"), odd_place()
    channels, length = slope_ref.shape
    group = plain_ref.shape[2]
    halo = halo_ref.shape[1]
    block = length // n
    unit = min(block, 256)
    groups = [slice(g, g + group) for g in range(0, channels, group)]
    at_end = 1 - odd if near else odd
    wide[:, lanes(at_end * (halo + length), halo)] = halo_ref[...]
    first = at_end * (length - halo)
    for k in range(n):
        base = (ch ^ k) * block

        @pl.when((base >= first) & (base < first + halo))
        def _(k=k, base=base):
            for s in range(0, block, unit):
                for rows in groups:
                    active, slope = gelu_and_slope(convolve(plain_ref, rows, wide, base + s, halo, unit))
                    active_refs[k][rows, s:s + unit] = active.astype(BF16)
                    slope_ref[rows, lanes(base + s, unit)] = slope


def one_end(near, halo, plain, active, slope, wide, waited):
    n = len(active)
    operands = [(o, True) for o in (*waited, halo, plain, *active, slope, wide)]
    results = kernel_call(
        "near_end" if near else "far_end", functools.partial(end_kernel, n, near, len(waited)), operands,
        [(a.shape, a.dtype, True) for a in (*active, slope, wide)],
        aliases={len(waited) + 2 + i: i for i in range(n + 2)},
    )
    return results[:n], *results[n:]


def grad_kernel(order, slope_ref, *rest):
    up_refs, (grad_ref, near_out, far_out) = rest[:-3], rest[-3:]
    ch, odd = lax.axis_index("ch"), odd_place()
    length, halo = grad_ref.shape[1], near_out.shape[1]
    block = up_refs[0].shape[1]
    for k, up_ref in zip(order, up_refs):
        here = lanes((ch ^ k) * block, block)
        grad_ref[:, here] = (up_ref[...].astype(F32) * slope_ref[:, here]).astype(BF16)
    near_out[...] = grad_ref[:, lanes((1 - odd) * (length - halo), halo)]
    far_out[...] = grad_ref[:, lanes(odd * (length - halo), halo)]


def grad_conv(slope, order, ups):
    channels = slope.shape[0]
    return kernel_call(
        "grad_conv", functools.partial(grad_kernel, order),
        [(o, True) for o in (slope, *[ups[k] for k in order])],
        [(slope.shape, BF16, True)] + [((channels, DILATION_STEP), BF16, True)] * 2,
    )


def columns_times(order, pw_ref, rows, pieces):
    channels = pieces.shape[0] // len(order)
    if channels % 128 != 0:
        return dot(pw_ref[rows, :], pieces)
    return sum(
        dot(
            pw_ref[rows, lanes((lax.axis_index("ch") ^ k) * channels, channels)],
            pieces[place * channels:(place + 1) * channels],
        )
        for place, k in enumerate(order)
    )


def mix_kernel(order, pw_ref, *rest):
    piece_refs, before, sum_ref = rest[:len(order)], rest[len(order):-1], rest[-1]
    pieces = jnp.concatenate([p[...] for p in piece_refs], axis=0)
    step = 512
    for m in range(0, sum_ref.shape[0], step):
        rows = slice(m, m + step)
        part = columns_times(order, pw_ref, rows, pieces)
        sum_ref[rows, :] = part + before[0][rows, :] if before else part


def mix(name, pw_weight, order, active, before):
    channels, width = active[order[0]].shape
    operands = [columns_of(pw_weight, channels, order), *[active[k] for k in order], *before]
    return kernel_call(
        name, functools.partial(mix_kernel, order), [(o, True) for o in operands],
        [((pw_weight.shape[0], width), F32, True)],
        aliases={len(operands) - 1: 0} if before else {},
    )


def back_interior_kernel(grad_ref, turned_ref, out_ref, ends_ref, held, sem):
    channels, length = grad_ref.shape
    group, halo, unit = turned_ref.shape[2], DILATION_STEP, 256

    def taps(rows, start, which):
        return sum(
            dot(turned_ref[t, rows, :], grad_ref[rows, start + (t - 1) * halo:start + (t - 1) * halo + unit])
            for t in which
        )

    groups = [slice(g, g + group) for g in range(0, channels, group)]
    for rows in groups:
        for s in range(0, length - 2 * halo, unit):
            held[rows, s:s + unit] = taps(rows, halo + s, (0, 1, 2)).astype(BF16)
    copy = pltpu.make_async_copy(held, out_ref.at[:, halo:length - halo], sem)
    copy.start()
    for rows in groups:
        for s in range(0, halo, unit):
            ends_ref[rows, s:s + unit] = taps(rows, s, (1, 2))
            ends_ref[rows, halo + s:halo + s + unit] = taps(rows, length - halo + s, (0, 1))
    copy.wait()


def back_end(halo_ref, ends_ref, turned_ref, at_end, held):
    channels, halo = halo_ref.shape
    group, unit = turned_ref.shape[2], 256
    for g in range(0, channels, group):
        rows = slice(g, g + group)
        for s in range(0, halo, unit):
            outer = dot(turned_ref[2 * at_end, rows, :], halo_ref[rows, s:s + unit])
            held[rows, s:s + unit] = (ends_ref[rows, lanes(at_end * halo + s, unit)] + outer).astype(BF16)


def end_of(out_ref, at_end):
    return out_ref.at[:, lanes(at_end * (out_ref.shape[1] - DILATION_STEP), DILATION_STEP)]


def late_mix_kernel(order, pw_ref, sum_ref, *rest):
    piece_refs, out_ref = rest[:-1], rest[-1]
    pieces = jnp.concatenate([p[...] for p in piece_refs], axis=0)
    step = 512
    for m in range(0, sum_ref.shape[0], step):
        rows = slice(m, m + step)
        out_ref[rows, :] = (sum_ref[rows, :] + columns_times(order, pw_ref, rows, pieces)).astype(BF16)


def late_mix(pw_weight, order, partial, active):
    channels = active[order[0]].shape[0]
    operands = [columns_of(pw_weight, channels, order), partial, *[active[k] for k in order]]
    (mixed,) = kernel_call(
        "late_mix", functools.partial(late_mix_kernel, order), [(o, True) for o in operands],
        [(partial.shape, BF16, True)],
    )
    return mixed


def last_kernel(mixed_ref, near_ref, far_ref, ends_ref, turned_ref, _, mixed_out, out_ref, both, sems):
    odd = odd_place()
    copies = [pltpu.make_async_copy(mixed_ref, mixed_out, sems.at[2])]
    copies[0].start()
    for place, (halo_ref, at_end) in enumerate(((near_ref, 1 - odd), (far_ref, odd))):
        back_end(halo_ref, ends_ref, turned_ref, at_end, both.at[place])
        copies.append(pltpu.make_async_copy(both.at[place], end_of(out_ref, at_end), sems.at[place]))
        copies[-1].start()
    for copy in copies:
        copy.wait()


def last(mixed, near, far, ends, turned, grad_inputs):
    operands = [(o, True) for o in (mixed, near, far, ends, turned)] + [(grad_inputs, False)]
    return kernel_call(
        "last", last_kernel, operands, [(mixed.shape, BF16, False), (grad_inputs.shape, BF16, False)],
        [pltpu.VMEM((2, *near.shape), BF16), DMA((3,))], {5: 1},
    )


def arrived(arrays):
    return kernel_call(
        "arrived", lambda *refs: None, [(o, True) for o in arrays], [(o.shape, o.dtype, True) for o in arrays],
        aliases={i: i for i in range(len(arrays))},
    )


def exchange(piece, k):
    if k == 0:
        return piece
    return lax.ppermute(piece, "ch", [(i, i ^ k) for i in range(lax.axis_size("ch"))])


def swap(values, first):
    size = lax.axis_size("ctx")
    pairs = [(i, i + 1) for i in range(first, size - 1, 2)]
    return lax.ppermute(values, "ctx", pairs + [(b, a) for a, b in pairs])


def body(inputs, conv_weight, pw_weight, cotangent):
    n = lax.axis_size("ch")
    channels, length = inputs.shape
    halo = DILATION_STEP
    order = list(range(n - 1, -1, -1))
    first, second, rest = order[:n // 4], order[n // 4:n // 2], order[n // 2:]

    weight = jnp.swapaxes(conv_weight, 1, 2)
    if channels % 128 != 0:
        weight = lax.dynamic_slice_in_dim(weight, lax.axis_index("ch") * channels, channels, 2)
    (near,) = kernel_call(
        "near_source", near_source_kernel, [(inputs, False)], [((channels, halo), BF16, True)], [DMA]
    )
    near = swap(near, 0)
    pieces, cot_in = upstream(pw_weight, cotangent, inputs, first, first=True)
    ups = {k: exchange(p, k) for k, p in zip(first, pieces)}
    pieces, far = upstream(pw_weight, cot_in, inputs, second, with_far=True)
    far = swap(far, 1)
    ups.update({k: exchange(p, k) for k, p in zip(second, pieces)})
    (pieces,) = upstream(pw_weight, cot_in, inputs, rest)
    ups.update({k: exchange(p, k) for k, p in zip(rest, pieces)})

    active, slope, wide, plain, turned = interior(inputs, weight, n)
    active, slope, wide = one_end(True, near, plain, active, slope, wide, [ups[first[0]]])
    active, slope, wide = one_end(False, far, plain, active, slope, wide, [])
    ups.update(zip(second, arrived([ups[k] for k in second])))
    grad, near_grad, far_grad = grad_conv(slope, order, ups)
    active = {k: exchange(active[k], k) for k in order}
    near_grad, far_grad = swap(near_grad, 0), swap(far_grad, 1)

    grad_inputs, ends = kernel_call(
        "back_interior", back_interior_kernel, [(grad, True), (turned, True)],
        [((channels, length), BF16, False), ((channels, 2 * halo), F32, True)],
        [pltpu.VMEM((channels, length - 2 * halo), BF16), DMA],
    )
    partial = mix("early_mix", pw_weight, first, active, [])
    (partial,) = mix("half_mix", pw_weight, rest, active, partial)
    mixed = late_mix(pw_weight, second, partial, active)
    return tuple(last(mixed, near_grad, far_grad, ends, turned, grad_inputs))


def solution(mesh):
    placed = (P("ch", "ctx"), P(), P(), P(None, ("ctx", "ch")))
    return jax.shard_map(
        body,
        mesh=mesh,
        in_specs=placed,
        out_specs=(P(None, ("ctx", "ch")), P("ch", "ctx")),
        check_vma=False,
    )
```

```python
import functools

import jax
import jax.numpy as jnp
from jax import lax
from jax.experimental import pallas as pl
from jax.experimental.pallas import tpu as pltpu
from jax.sharding import PartitionSpec as P

DILATION_STEP = 512
UPSTREAM_ROWS = 512
BF16, F32 = jnp.bfloat16, jnp.float32
ANY = pl.BlockSpec(memory_space=pl.ANY)
INSIDE = pl.BlockSpec(memory_space=pltpu.VMEM)
DMA = pltpu.SemaphoreType.DMA


def kernel_call(name, kernel, operands, outs, scratch=(), aliases=None):
    return pl.pallas_call(
        kernel,
        in_specs=[INSIDE if held else ANY for _, held in operands],
        out_specs=[INSIDE if held else ANY for _, _, held in outs],
        out_shape=[
            pltpu.VMEM(shape, kind) if held else jax.ShapeDtypeStruct(shape, kind)
            for shape, kind, held in outs
        ],
        scratch_shapes=list(scratch),
        input_output_aliases=aliases or {},
        compiler_params=pltpu.CompilerParams(vmem_limit_bytes=16 << 20),
        name=name,
    )(*[
        pltpu.with_memory_space_constraint(array, pltpu.VMEM if held else pltpu.HBM)
        for array, held in operands
    ])


def gelu_and_slope(v):
    square = v * v
    inner = v * (0.7978845608 + (0.7978845608 * 0.044715) * square)
    th = jnp.tanh(inner)
    half = 0.5 + 0.5 * th
    active = v * half
    inner_slope = 0.7978845608 + (3.0 * 0.7978845608 * 0.044715) * square
    slope = half + (0.5 * v) * (1.0 - th * th) * inner_slope
    return active, slope


def lanes(start, size):
    return pl.ds(pl.multiple_of(start, 128), size)


def dot(a, b):
    return jnp.dot(a, b, preferred_element_type=F32)


def turned_dot(a, b):
    return lax.dot_general(a, b, (((0,), (0,)), ((), ())), preferred_element_type=F32)


def odd_place():
    return lax.axis_index("ctx") % 2


def end_copy(x_ref, end_ref, at_end, sem):
    length, halo = x_ref.shape[1], end_ref.shape[1]
    return pltpu.make_async_copy(x_ref.at[:, lanes(at_end * (length - halo), halo)], end_ref, sem)


def near_source_kernel(x_ref, near_ref, sem):
    copy = end_copy(x_ref, near_ref, 1 - odd_place(), sem)
    copy.start()
    copy.wait()


def upstream_kernel(order, channels, first, with_far, pw_ref, cot_ref, x_ref, *rest):
    count = len(order)
    piece_refs, rest = rest[:count], rest[count:]
    columns_ref, total_ref, sems = rest[-3:]
    cot_in = rest[0] if first else cot_ref
    ch = lax.axis_index("ch")
    blocks = []
    for m in range(0, cot_in.shape[0], UPSTREAM_ROWS):
        rows = slice(m, m + UPSTREAM_ROWS)
        pairs = [(cot_ref.at[rows], cot_in.at[rows])] if first else []
        if channels % 128 == 0:
            for place, k in enumerate(order):
                columns = lanes((ch ^ k) * channels, channels)
                held = slice(place * channels, (place + 1) * channels)
                pairs.append((pw_ref.at[rows, columns], columns_ref.at[rows, held]))
        else:
            pairs.append((pw_ref.at[rows], columns_ref.at[rows]))
        copies = [
            pltpu.make_async_copy(source, place, sems.at[len(blocks), i])
            for i, (source, place) in enumerate(pairs)
        ]
        for copy in copies:
            copy.start()
        blocks.append((rows, copies))
    if with_far:
        end = end_copy(x_ref, rest[-4], odd_place(), sems.at[0, count + 1])
        end.start()
    for step, (rows, copies) in enumerate(blocks):
        for copy in copies:
            copy.wait()
        for place in range(count):
            held = slice(place * channels, (place + 1) * channels)
            part = turned_dot(columns_ref[rows, held], cot_in[rows, :])
            if step > 0:
                part = part + total_ref[held, :]
            if step < len(blocks) - 1:
                total_ref[held, :] = part
            else:
                piece_refs[place][...] = part.astype(BF16)
    if with_far:
        end.wait()


def columns_of(pw_weight, channels, order):
    if channels % 128 == 0:
        return pw_weight
    ch = lax.axis_index("ch")
    return jnp.concatenate(
        [lax.dynamic_slice_in_dim(pw_weight, (ch ^ k) * channels, channels, 1) for k in order], axis=1
    )


def upstream(pw_weight, cotangent, inputs, order, first=False, with_far=False):
    channels = inputs.shape[0]
    total, width = cotangent.shape
    count = len(order)
    outs = [((channels, width), BF16, True)] * count
    outs += [(cotangent.shape, BF16, True)] * first
    outs += [((channels, DILATION_STEP), BF16, True)] * with_far
    results = kernel_call(
        "upstream", functools.partial(upstream_kernel, order, channels, first, with_far),
        [(columns_of(pw_weight, channels, order), False), (cotangent, not first), (inputs, False)], outs,
        [
            pltpu.VMEM((total, count * channels), BF16), pltpu.VMEM((count * channels, width), F32),
            DMA((total // UPSTREAM_ROWS, count + 2)),
        ],
    )
    return results[:count], *results[count:]


def convolve(w_ref, rows, wide, start, halo, unit):
    return sum(dot(w_ref[t, rows, :], wide[rows, lanes(start + t * halo, unit)]) for t in range(3))


def interior_kernel(n, x_ref, w_ref, *rest):
    active_refs, (slope_ref, wide, plain_ref, turned_ref, own_ref, sem, own_sem) = rest[:n], rest[n:]
    ch = lax.axis_index("ch")
    channels, length = x_ref.shape
    group = w_ref.shape[1]
    own = w_ref.at[:, :, lanes(ch * channels, channels)] if w_ref.shape[2] > channels else w_ref
    own_copy = pltpu.make_async_copy(own, own_ref, own_sem)
    own_copy.start()
    halo = DILATION_STEP
    block = length // n
    unit = min(block, 256)
    copy = pltpu.make_async_copy(x_ref, wide.at[:, halo:halo + length], sem)
    copy.start()
    groups = [slice(g, g + group) for g in range(0, channels, group)]
    own_copy.wait()
    for t in range(3):
        for rows in groups:
            square = own_ref[t, :, rows]
            turned_ref[2 - t, rows, :] = square
            plain_ref[t, rows, :] = square.T
    copy.wait()
    for k in range(n):
        base = (ch ^ k) * block

        @pl.when((base >= halo) & (base < length - halo))
        def _(k=k, base=base):
            for s in range(0, block, unit):
                for rows in groups:
                    active, slope = gelu_and_slope(convolve(plain_ref, rows, wide, base + s, halo, unit))
                    active_refs[k][rows, s:s + unit] = active.astype(BF16)
                    slope_ref[rows, lanes(base + s, unit)] = slope


def interior(inputs, weight, n):
    channels, length = inputs.shape
    group = weight.shape[1]
    block = length // n
    outs = [((channels, block), BF16, True)] * n
    outs += [((channels, length), F32, True), ((channels, length + 2 * DILATION_STEP), BF16, True)]
    outs += [((3, channels, group), BF16, True)] * 2
    results = kernel_call(
        "interior", functools.partial(interior_kernel, n), [(inputs, False), (weight, False)], outs,
        [pltpu.VMEM((3, group, channels), BF16), DMA, DMA],
    )
    return results[:n], *results[n:]


def end_kernel(n, near, waits, *refs):
    halo_ref, plain_ref, rest = refs[waits], refs[waits + 1], refs[-(n + 2):]
    active_refs, (slope_ref, wide) = rest[:n], rest[n:]
    ch, odd = lax.axis_index("ch"), odd_place()
    channels, length = slope_ref.shape
    group = plain_ref.shape[2]
    halo = halo_ref.shape[1]
    block = length // n
    unit = min(block, 256)
    groups = [slice(g, g + group) for g in range(0, channels, group)]
    at_end = 1 - odd if near else odd
    wide[:, lanes(at_end * (halo + length), halo)] = halo_ref[...]
    first = at_end * (length - halo)
    for k in range(n):
        base = (ch ^ k) * block

        @pl.when((base >= first) & (base < first + halo))
        def _(k=k, base=base):
            for s in range(0, block, unit):
                for rows in groups:
                    active, slope = gelu_and_slope(convolve(plain_ref, rows, wide, base + s, halo, unit))
                    active_refs[k][rows, s:s + unit] = active.astype(BF16)
                    slope_ref[rows, lanes(base + s, unit)] = slope


def one_end(near, halo, plain, active, slope, wide, waited):
    n = len(active)
    operands = [(o, True) for o in (*waited, halo, plain, *active, slope, wide)]
    results = kernel_call(
        "near_end" if near else "far_end", functools.partial(end_kernel, n, near, len(waited)), operands,
        [(a.shape, a.dtype, True) for a in (*active, slope, wide)],
        aliases={len(waited) + 2 + i: i for i in range(n + 2)},
    )
    return results[:n], *results[n:]


def grad_kernel(order, slope_ref, *rest):
    up_refs, passed = rest[:len(order)], (len(rest) - len(order) - 3) // 2
    grad_ref, near_out, far_out = rest[len(order) + passed:len(order) + passed + 3]
    ch, odd = lax.axis_index("ch"), odd_place()
    length, halo = grad_ref.shape[1], near_out.shape[1]
    block = up_refs[0].shape[1]
    for k, up_ref in zip(order, up_refs):
        here = lanes((ch ^ k) * block, block)
        grad_ref[:, here] = (up_ref[...].astype(F32) * slope_ref[:, here]).astype(BF16)
    near_out[...] = grad_ref[:, lanes((1 - odd) * (length - halo), halo)]
    far_out[...] = grad_ref[:, lanes(odd * (length - halo), halo)]


def grad_conv(slope, order, ups, passed):
    end = (slope.shape[0], DILATION_STEP)
    grad, near, far, *passed = kernel_call(
        "grad_conv", functools.partial(grad_kernel, order),
        [(o, True) for o in (slope, *[ups[k] for k in order], *passed)],
        [(slope.shape, BF16, True), (end, BF16, True), (end, BF16, True)] + [(o.shape, BF16, True) for o in passed],
        aliases={1 + len(order) + i: 3 + i for i in range(len(passed))},
    )
    return grad, near, far, passed


def columns_times(order, pw_ref, rows, pieces):
    channels = pieces.shape[0] // len(order)
    if channels % 128 != 0:
        return dot(pw_ref[rows, :], pieces)
    return sum(
        dot(
            pw_ref[rows, lanes((lax.axis_index("ch") ^ k) * channels, channels)],
            pieces[place * channels:(place + 1) * channels],
        )
        for place, k in enumerate(order)
    )


def mix_kernel(order, pw_ref, *rest):
    piece_refs, before, sum_ref = rest[:len(order)], rest[len(order):-1], rest[-1]
    pieces = jnp.concatenate([p[...] for p in piece_refs], axis=0)
    step = 512
    for m in range(0, sum_ref.shape[0], step):
        rows = slice(m, m + step)
        part = columns_times(order, pw_ref, rows, pieces)
        sum_ref[rows, :] = part + before[0][rows, :] if before else part


def mix(name, pw_weight, order, active, before):
    channels, width = active[order[0]].shape
    operands = [columns_of(pw_weight, channels, order), *[active[k] for k in order], *before]
    return kernel_call(
        name, functools.partial(mix_kernel, order), [(o, True) for o in operands],
        [((pw_weight.shape[0], width), F32, True)],
        aliases={len(operands) - 1: 0} if before else {},
    )


def back_interior_kernel(grad_ref, turned_ref, out_ref, ends_ref, held, sem):
    channels, length = grad_ref.shape
    group, halo, unit = turned_ref.shape[2], DILATION_STEP, 256

    def taps(rows, start, which):
        return sum(
            dot(turned_ref[t, rows, :], grad_ref[rows, start + (t - 1) * halo:start + (t - 1) * halo + unit])
            for t in which
        )

    groups = [slice(g, g + group) for g in range(0, channels, group)]
    for rows in groups:
        for s in range(0, length - 2 * halo, unit):
            held[rows, s:s + unit] = taps(rows, halo + s, (0, 1, 2)).astype(BF16)
    copy = pltpu.make_async_copy(held, out_ref.at[:, halo:length - halo], sem)
    copy.start()
    for rows in groups:
        for s in range(0, halo, unit):
            ends_ref[rows, s:s + unit] = taps(rows, s, (1, 2))
            ends_ref[rows, halo + s:halo + s + unit] = taps(rows, length - halo + s, (0, 1))
    copy.wait()


def back_end(halo_ref, ends_ref, turned_ref, at_end, held):
    channels, halo = halo_ref.shape
    group, unit = turned_ref.shape[2], 256
    for g in range(0, channels, group):
        rows = slice(g, g + group)
        for s in range(0, halo, unit):
            outer = dot(turned_ref[2 * at_end, rows, :], halo_ref[rows, s:s + unit])
            held[rows, s:s + unit] = (ends_ref[rows, lanes(at_end * halo + s, unit)] + outer).astype(BF16)


def end_of(out_ref, at_end):
    return out_ref.at[:, lanes(at_end * (out_ref.shape[1] - DILATION_STEP), DILATION_STEP)]


def late_mix_kernel(order, pw_ref, sum_ref, *rest):
    piece_refs, (out_ref, done_ref, held, sems) = rest[:len(order)], rest[len(order):]
    pieces = jnp.concatenate([p[...] for p in piece_refs], axis=0)
    step = 512
    copies = []
    for m in range(0, sum_ref.shape[0], step):
        rows = slice(m, m + step)
        held[rows, :] = (sum_ref[rows, :] + columns_times(order, pw_ref, rows, pieces)).astype(BF16)
        copies.append(pltpu.make_async_copy(held.at[rows, :], out_ref.at[rows, :], sems.at[len(copies)]))
        copies[-1].start()
    done_ref[...] = jnp.zeros_like(done_ref)
    for copy in copies:
        copy.wait()


def late_mix(pw_weight, order, partial, active):
    channels = active[order[0]].shape[0]
    operands = [columns_of(pw_weight, channels, order), partial, *[active[k] for k in order]]
    return kernel_call(
        "late_mix", functools.partial(late_mix_kernel, order), [(o, True) for o in operands],
        [(partial.shape, BF16, False), ((8, 128), F32, True)],
        [pltpu.VMEM(partial.shape, BF16), DMA((partial.shape[0] // 512,))],
    )


def back_ends_kernel(near_ref, far_ref, ends_ref, turned_ref, _, __, out_ref, both, sems):
    odd = odd_place()
    copies = []
    for place, (halo_ref, at_end) in enumerate(((near_ref, 1 - odd), (far_ref, odd))):
        back_end(halo_ref, ends_ref, turned_ref, at_end, both.at[place])
        copies.append(pltpu.make_async_copy(both.at[place], end_of(out_ref, at_end), sems.at[place]))
        copies[-1].start()
    for copy in copies:
        copy.wait()


def back_ends(near, far, ends, turned, done, grad_inputs):
    operands = [(o, True) for o in (near, far, ends, turned, done)] + [(grad_inputs, False)]
    (result,) = kernel_call(
        "back_ends", back_ends_kernel, operands, [(grad_inputs.shape, BF16, False)],
        [pltpu.VMEM((2, *near.shape), BF16), DMA((2,))], {5: 0},
    )
    return result


def arrived(arrays):
    return kernel_call(
        "arrived", lambda *refs: None, [(o, True) for o in arrays], [(o.shape, o.dtype, True) for o in arrays],
        aliases={i: i for i in range(len(arrays))},
    )


def exchange(piece, k):
    if k == 0:
        return piece
    return lax.ppermute(piece, "ch", [(i, i ^ k) for i in range(lax.axis_size("ch"))])


def swap(values, first):
    size = lax.axis_size("ctx")
    pairs = [(i, i + 1) for i in range(first, size - 1, 2)]
    return lax.ppermute(values, "ctx", pairs + [(b, a) for a, b in pairs])


def body(inputs, conv_weight, pw_weight, cotangent):
    n = lax.axis_size("ch")
    channels, length = inputs.shape
    halo = DILATION_STEP
    order = list(range(n - 1, -1, -1))
    first, second, rest = order[:n // 4], order[n // 4:n // 2], order[n // 2:]

    weight = jnp.swapaxes(conv_weight, 1, 2)
    if channels % 128 != 0:
        weight = lax.dynamic_slice_in_dim(weight, lax.axis_index("ch") * channels, channels, 2)
    (near,) = kernel_call(
        "near_source", near_source_kernel, [(inputs, False)], [((channels, halo), BF16, True)], [DMA]
    )
    near = swap(near, 0)
    pieces, cot_in = upstream(pw_weight, cotangent, inputs, first, first=True)
    ups = {k: exchange(p, k) for k, p in zip(first, pieces)}
    pieces, far = upstream(pw_weight, cot_in, inputs, second, with_far=True)
    far = swap(far, 1)
    ups.update({k: exchange(p, k) for k, p in zip(second, pieces)})
    (pieces,) = upstream(pw_weight, cot_in, inputs, rest)
    ups.update({k: exchange(p, k) for k, p in zip(rest, pieces)})

    active, slope, wide, plain, turned = interior(inputs, weight, n)
    active, slope, wide = one_end(True, near, plain, active, slope, wide, [ups[first[0]]])
    active, slope, wide = one_end(False, far, plain, active, slope, wide, [])
    ups.update(zip(second, arrived([ups[k] for k in second])))
    grad, near_grad, far_grad, late = grad_conv(slope, order, ups, [active[k] for k in second])
    late = dict(zip(second, late))
    active = {k: exchange(late.get(k, active[k]), k) for k in order}
    near_grad, far_grad = swap(near_grad, 0), swap(far_grad, 1)

    grad_inputs, ends = kernel_call(
        "back_interior", back_interior_kernel, [(grad, True), (turned, True)],
        [((channels, length), BF16, False), ((channels, 2 * halo), F32, True)],
        [pltpu.VMEM((channels, length - 2 * halo), BF16), DMA],
    )
    partial = mix("early_mix", pw_weight, first, active, [])
    (partial,) = mix("half_mix", pw_weight, rest, active, partial)
    mixed, done = late_mix(pw_weight, second, partial, active)
    return mixed, back_ends(near_grad, far_grad, ends, turned, done, grad_inputs)


def solution(mesh):
    placed = (P("ch", "ctx"), P(), P(), P(None, ("ctx", "ch")))
    return jax.shard_map(
        body,
        mesh=mesh,
        in_specs=placed,
        out_specs=(P(None, ("ctx", "ch")), P("ch", "ctx")),
        check_vma=False,
    )
```

```python
import functools

import jax
import jax.numpy as jnp
from jax import lax
from jax.experimental import pallas as pl
from jax.experimental.pallas import tpu as pltpu
from jax.sharding import PartitionSpec as P

DILATION_STEP = 512
UPSTREAM_ROWS = 512
BF16, F32 = jnp.bfloat16, jnp.float32
ANY = pl.BlockSpec(memory_space=pl.ANY)
INSIDE = pl.BlockSpec(memory_space=pltpu.VMEM)
DMA = pltpu.SemaphoreType.DMA


def kernel_call(name, kernel, operands, outs, scratch=(), aliases=None):
    return pl.pallas_call(
        kernel,
        in_specs=[INSIDE if held else ANY for _, held in operands],
        out_specs=[INSIDE if held else ANY for _, _, held in outs],
        out_shape=[
            pltpu.VMEM(shape, kind) if held else jax.ShapeDtypeStruct(shape, kind)
            for shape, kind, held in outs
        ],
        scratch_shapes=list(scratch),
        input_output_aliases=aliases or {},
        compiler_params=pltpu.CompilerParams(vmem_limit_bytes=16 << 20),
        name=name,
    )(*[
        pltpu.with_memory_space_constraint(array, pltpu.VMEM if held else pltpu.HBM)
        for array, held in operands
    ])


def gelu_and_slope(v):
    square = v * v
    inner = v * (0.7978845608 + (0.7978845608 * 0.044715) * square)
    th = jnp.tanh(inner)
    half = 0.5 + 0.5 * th
    active = v * half
    inner_slope = 0.7978845608 + (3.0 * 0.7978845608 * 0.044715) * square
    slope = half + (0.5 * v) * (1.0 - th * th) * inner_slope
    return active, slope


def lanes(start, size):
    return pl.ds(pl.multiple_of(start, 128), size)


def dot(a, b):
    return jnp.dot(a, b, preferred_element_type=F32)


def turned_dot(a, b):
    return lax.dot_general(a, b, (((0,), (0,)), ((), ())), preferred_element_type=F32)


def odd_place():
    return lax.axis_index("ctx") % 2


def end_copy(x_ref, end_ref, at_end, sem):
    length, halo = x_ref.shape[1], end_ref.shape[1]
    return pltpu.make_async_copy(x_ref.at[:, lanes(at_end * (length - halo), halo)], end_ref, sem)


def near_source_kernel(x_ref, near_ref, sem):
    copy = end_copy(x_ref, near_ref, 1 - odd_place(), sem)
    copy.start()
    copy.wait()


def upstream_kernel(order, channels, first, with_far, pw_ref, cot_ref, x_ref, *rest):
    count = len(order)
    piece_refs, rest = rest[:count], rest[count:]
    columns_ref, total_ref, sems = rest[-3:]
    cot_in = rest[0] if first else cot_ref
    ch = lax.axis_index("ch")
    blocks = []
    for m in range(0, cot_in.shape[0], UPSTREAM_ROWS):
        rows = slice(m, m + UPSTREAM_ROWS)
        pairs = [(cot_ref.at[rows], cot_in.at[rows])] if first else []
        if channels % 128 == 0:
            for place, k in enumerate(order):
                columns = lanes((ch ^ k) * channels, channels)
                held = slice(place * channels, (place + 1) * channels)
                pairs.append((pw_ref.at[rows, columns], columns_ref.at[rows, held]))
        else:
            pairs.append((pw_ref.at[rows], columns_ref.at[rows]))
        copies = [
            pltpu.make_async_copy(source, place, sems.at[len(blocks), i])
            for i, (source, place) in enumerate(pairs)
        ]
        for copy in copies:
            copy.start()
        blocks.append((rows, copies))
    if with_far:
        end = end_copy(x_ref, rest[-4], odd_place(), sems.at[0, count + 1])
        end.start()
    for step, (rows, copies) in enumerate(blocks):
        for copy in copies:
            copy.wait()
        for place in range(count):
            held = slice(place * channels, (place + 1) * channels)
            part = turned_dot(columns_ref[rows, held], cot_in[rows, :])
            if step > 0:
                part = part + total_ref[held, :]
            if step < len(blocks) - 1:
                total_ref[held, :] = part
            else:
                piece_refs[place][...] = part.astype(BF16)
    if with_far:
        end.wait()


def columns_of(pw_weight, channels, order):
    if channels % 128 == 0:
        return pw_weight
    ch = lax.axis_index("ch")
    return jnp.concatenate(
        [lax.dynamic_slice_in_dim(pw_weight, (ch ^ k) * channels, channels, 1) for k in order], axis=1
    )


def upstream(pw_weight, cotangent, inputs, order, first=False, with_far=False):
    channels = inputs.shape[0]
    total, width = cotangent.shape
    count = len(order)
    outs = [((channels, width), BF16, True)] * count
    outs += [(cotangent.shape, BF16, True)] * first
    outs += [((channels, DILATION_STEP), BF16, True)] * with_far
    results = kernel_call(
        "upstream", functools.partial(upstream_kernel, order, channels, first, with_far),
        [(columns_of(pw_weight, channels, order), False), (cotangent, not first), (inputs, False)], outs,
        [
            pltpu.VMEM((total, count * channels), BF16), pltpu.VMEM((count * channels, width), F32),
            DMA((total // UPSTREAM_ROWS, count + 2)),
        ],
    )
    return results[:count], *results[count:]


def convolve(w_ref, rows, wide, start, halo, unit):
    return sum(dot(w_ref[t, rows, :], wide[rows, lanes(start + t * halo, unit)]) for t in range(3))


def interior_kernel(n, x_ref, w_ref, *rest):
    active_refs, (slope_ref, wide, plain_ref, turned_ref, own_ref, sem, own_sem) = rest[:n], rest[n:]
    ch = lax.axis_index("ch")
    channels, length = x_ref.shape
    group = w_ref.shape[1]
    own = w_ref.at[:, :, lanes(ch * channels, channels)] if w_ref.shape[2] > channels else w_ref
    own_copy = pltpu.make_async_copy(own, own_ref, own_sem)
    own_copy.start()
    halo = DILATION_STEP
    block = length // n
    unit = min(block, 256)
    copy = pltpu.make_async_copy(x_ref, wide.at[:, halo:halo + length], sem)
    copy.start()
    groups = [slice(g, g + group) for g in range(0, channels, group)]
    own_copy.wait()
    for t in range(3):
        for rows in groups:
            square = own_ref[t, :, rows]
            turned_ref[2 - t, rows, :] = square
            plain_ref[t, rows, :] = square.T
    copy.wait()
    for k in range(n):
        base = (ch ^ k) * block

        @pl.when((base >= halo) & (base < length - halo))
        def _(k=k, base=base):
            for s in range(0, block, unit):
                for rows in groups:
                    active, slope = gelu_and_slope(convolve(plain_ref, rows, wide, base + s, halo, unit))
                    active_refs[k][rows, s:s + unit] = active.astype(BF16)
                    slope_ref[rows, lanes(base + s, unit)] = slope


def interior(inputs, weight, n):
    channels, length = inputs.shape
    group = weight.shape[1]
    block = length // n
    outs = [((channels, block), BF16, True)] * n
    outs += [((channels, length), F32, True), ((channels, length + 2 * DILATION_STEP), BF16, True)]
    outs += [((3, channels, group), BF16, True)] * 2
    results = kernel_call(
        "interior", functools.partial(interior_kernel, n), [(inputs, False), (weight, False)], outs,
        [pltpu.VMEM((3, group, channels), BF16), DMA, DMA],
    )
    return results[:n], *results[n:]


def end_kernel(n, near, waits, *refs):
    halo_ref, plain_ref, rest = refs[waits], refs[waits + 1], refs[-(n + 2):]
    active_refs, (slope_ref, wide) = rest[:n], rest[n:]
    ch, odd = lax.axis_index("ch"), odd_place()
    channels, length = slope_ref.shape
    group = plain_ref.shape[2]
    halo = halo_ref.shape[1]
    block = length // n
    unit = min(block, 256)
    groups = [slice(g, g + group) for g in range(0, channels, group)]
    at_end = 1 - odd if near else odd
    wide[:, lanes(at_end * (halo + length), halo)] = halo_ref[...]
    first = at_end * (length - halo)
    for k in range(n):
        base = (ch ^ k) * block

        @pl.when((base >= first) & (base < first + halo))
        def _(k=k, base=base):
            for s in range(0, block, unit):
                for rows in groups:
                    active, slope = gelu_and_slope(convolve(plain_ref, rows, wide, base + s, halo, unit))
                    active_refs[k][rows, s:s + unit] = active.astype(BF16)
                    slope_ref[rows, lanes(base + s, unit)] = slope


def one_end(near, halo, plain, active, slope, wide, waited):
    n = len(active)
    operands = [(o, True) for o in (*waited, halo, plain, *active, slope, wide)]
    results = kernel_call(
        "near_end" if near else "far_end", functools.partial(end_kernel, n, near, len(waited)), operands,
        [(a.shape, a.dtype, True) for a in (*active, slope, wide)],
        aliases={len(waited) + 2 + i: i for i in range(n + 2)},
    )
    return results[:n], *results[n:]


def grad_kernel(order, slope_ref, *rest):
    up_refs, (grad_ref, near_out, far_out) = rest[:-3], rest[-3:]
    ch, odd = lax.axis_index("ch"), odd_place()
    length, halo = grad_ref.shape[1], near_out.shape[1]
    block = up_refs[0].shape[1]
    for k, up_ref in zip(order, up_refs):
        here = lanes((ch ^ k) * block, block)
        grad_ref[:, here] = (up_ref[...].astype(F32) * slope_ref[:, here]).astype(BF16)
    near_out[...] = grad_ref[:, lanes((1 - odd) * (length - halo), halo)]
    far_out[...] = grad_ref[:, lanes(odd * (length - halo), halo)]


def grad_conv(slope, order, ups):
    channels = slope.shape[0]
    return kernel_call(
        "grad_conv", functools.partial(grad_kernel, order),
        [(o, True) for o in (slope, *[ups[k] for k in order])],
        [(slope.shape, BF16, True)] + [((channels, DILATION_STEP), BF16, True)] * 2,
    )


def columns_times(order, pw_ref, rows, pieces):
    channels = pieces.shape[0] // len(order)
    if channels % 128 != 0:
        return dot(pw_ref[rows, :], pieces)
    return sum(
        dot(
            pw_ref[rows, lanes((lax.axis_index("ch") ^ k) * channels, channels)],
            pieces[place * channels:(place + 1) * channels],
        )
        for place, k in enumerate(order)
    )


def mix_kernel(order, pw_ref, *rest):
    piece_refs, before, sum_ref = rest[:len(order)], rest[len(order):-1], rest[-1]
    pieces = jnp.concatenate([p[...] for p in piece_refs], axis=0)
    step = 512
    for m in range(0, sum_ref.shape[0], step):
        rows = slice(m, m + step)
        part = columns_times(order, pw_ref, rows, pieces)
        sum_ref[rows, :] = part + before[0][rows, :] if before else part


def mix(name, pw_weight, order, active, before):
    channels, width = active[order[0]].shape
    operands = [columns_of(pw_weight, channels, order), *[active[k] for k in order], *before]
    return kernel_call(
        name, functools.partial(mix_kernel, order), [(o, True) for o in operands],
        [((pw_weight.shape[0], width), F32, True)],
        aliases={len(operands) - 1: 0} if before else {},
    )


def back_interior_kernel(grad_ref, turned_ref, out_ref, ends_ref, held, sem):
    channels, length = grad_ref.shape
    group, halo, unit = turned_ref.shape[2], DILATION_STEP, 256

    def taps(rows, start, which):
        return sum(
            dot(turned_ref[t, rows, :], grad_ref[rows, start + (t - 1) * halo:start + (t - 1) * halo + unit])
            for t in which
        )

    groups = [slice(g, g + group) for g in range(0, channels, group)]
    for rows in groups:
        for s in range(0, length - 2 * halo, unit):
            held[rows, s:s + unit] = taps(rows, halo + s, (0, 1, 2)).astype(BF16)
    copy = pltpu.make_async_copy(held, out_ref.at[:, halo:length - halo], sem)
    copy.start()
    for rows in groups:
        for s in range(0, halo, unit):
            ends_ref[rows, s:s + unit] = taps(rows, s, (1, 2))
            ends_ref[rows, halo + s:halo + s + unit] = taps(rows, length - halo + s, (0, 1))
    copy.wait()


def back_end(halo_ref, ends_ref, turned_ref, at_end, held):
    channels, halo = halo_ref.shape
    group, unit = turned_ref.shape[2], 256
    for g in range(0, channels, group):
        rows = slice(g, g + group)
        for s in range(0, halo, unit):
            outer = dot(turned_ref[2 * at_end, rows, :], halo_ref[rows, s:s + unit])
            held[rows, s:s + unit] = (ends_ref[rows, lanes(at_end * halo + s, unit)] + outer).astype(BF16)


def end_of(out_ref, at_end):
    return out_ref.at[:, lanes(at_end * (out_ref.shape[1] - DILATION_STEP), DILATION_STEP)]


def late_mix_kernel(order, pw_ref, sum_ref, *rest):
    piece_refs, (out_ref, done_ref, held, sems) = rest[:len(order)], rest[len(order):]
    pieces = jnp.concatenate([p[...] for p in piece_refs], axis=0)
    step = 512
    copies = []
    for m in range(0, sum_ref.shape[0], step):
        rows = slice(m, m + step)
        held[rows, :] = (sum_ref[rows, :] + columns_times(order, pw_ref, rows, pieces)).astype(BF16)
        copies.append(pltpu.make_async_copy(held.at[rows, :], out_ref.at[rows, :], sems.at[len(copies)]))
        copies[-1].start()
    done_ref[...] = jnp.zeros_like(done_ref)
    for copy in copies:
        copy.wait()


def late_mix(pw_weight, order, partial, active):
    channels = active[order[0]].shape[0]
    operands = [columns_of(pw_weight, channels, order), partial, *[active[k] for k in order]]
    return kernel_call(
        "late_mix", functools.partial(late_mix_kernel, order), [(o, True) for o in operands],
        [(partial.shape, BF16, False), ((8, 128), F32, True)],
        [pltpu.VMEM(partial.shape, BF16), DMA((partial.shape[0] // 512,))],
    )


def back_ends_kernel(near_ref, far_ref, ends_ref, turned_ref, _, __, out_ref, both, sems):
    odd = odd_place()
    copies = []
    for place, (halo_ref, at_end) in enumerate(((near_ref, 1 - odd), (far_ref, odd))):
        back_end(halo_ref, ends_ref, turned_ref, at_end, both.at[place])
        copies.append(pltpu.make_async_copy(both.at[place], end_of(out_ref, at_end), sems.at[place]))
        copies[-1].start()
    for copy in copies:
        copy.wait()


def back_ends(near, far, ends, turned, done, grad_inputs):
    operands = [(o, True) for o in (near, far, ends, turned, done)] + [(grad_inputs, False)]
    (result,) = kernel_call(
        "back_ends", back_ends_kernel, operands, [(grad_inputs.shape, BF16, False)],
        [pltpu.VMEM((2, *near.shape), BF16), DMA((2,))], {5: 0},
    )
    return result


def arrived(arrays):
    return kernel_call(
        "arrived", lambda *refs: None, [(o, True) for o in arrays], [(o.shape, o.dtype, True) for o in arrays],
        aliases={i: i for i in range(len(arrays))},
    )


def exchange(piece, k):
    if k == 0:
        return piece
    return lax.ppermute(piece, "ch", [(i, i ^ k) for i in range(lax.axis_size("ch"))])


def swap(values, first):
    size = lax.axis_size("ctx")
    pairs = [(i, i + 1) for i in range(first, size - 1, 2)]
    return lax.ppermute(values, "ctx", pairs + [(b, a) for a, b in pairs])


def body(inputs, conv_weight, pw_weight, cotangent):
    n = lax.axis_size("ch")
    channels, length = inputs.shape
    halo = DILATION_STEP
    order = [*range(n // 2, n), *range(n // 2 - 1, -1, -1)]
    first, second, rest = order[:n // 4], order[n // 4:n // 2], order[n // 2:]

    weight = jnp.swapaxes(conv_weight, 1, 2)
    if channels % 128 != 0:
        weight = lax.dynamic_slice_in_dim(weight, lax.axis_index("ch") * channels, channels, 2)
    (near,) = kernel_call(
        "near_source", near_source_kernel, [(inputs, False)], [((channels, halo), BF16, True)], [DMA]
    )
    near = swap(near, 0)
    pieces, cot_in = upstream(pw_weight, cotangent, inputs, first, first=True)
    ups = {k: exchange(p, k) for k, p in zip(first, pieces)}
    pieces, far = upstream(pw_weight, cot_in, inputs, second, with_far=True)
    far = swap(far, 1)
    ups.update({k: exchange(p, k) for k, p in zip(second, pieces)})
    (pieces,) = upstream(pw_weight, cot_in, inputs, rest)
    ups.update({k: exchange(p, k) for k, p in zip(rest, pieces)})

    active, slope, wide, plain, turned = interior(inputs, weight, n)
    active, slope, wide = one_end(True, near, plain, active, slope, wide, [ups[first[0]]])
    active, slope, wide = one_end(False, far, plain, active, slope, wide, [])
    ups.update(zip(second, arrived([ups[k] for k in second])))
    grad, near_grad, far_grad = grad_conv(slope, order, ups)
    active = {k: exchange(active[k], k) for k in order}
    near_grad, far_grad = swap(near_grad, 0), swap(far_grad, 1)

    grad_inputs, ends = kernel_call(
        "back_interior", back_interior_kernel, [(grad, True), (turned, True)],
        [((channels, length), BF16, False), ((channels, 2 * halo), F32, True)],
        [pltpu.VMEM((channels, length - 2 * halo), BF16), DMA],
    )
    partial = mix("early_mix", pw_weight, first, active, [])
    (partial,) = mix("half_mix", pw_weight, rest, active, partial)
    mixed, done = late_mix(pw_weight, second, partial, active)
    return mixed, back_ends(near_grad, far_grad, ends, turned, done, grad_inputs)


def solution(mesh):
    placed = (P("ch", "ctx"), P(), P(), P(None, ("ctx", "ch")))
    return jax.shard_map(
        body,
        mesh=mesh,
        in_specs=placed,
        out_specs=(P(None, ("ctx", "ch")), P("ch", "ctx")),
        check_vma=False,
    )
```

```python
import functools

import jax
import jax.numpy as jnp
from jax import lax
from jax.experimental import pallas as pl
from jax.experimental.pallas import tpu as pltpu
from jax.sharding import PartitionSpec as P

DILATION_STEP = 512
UPSTREAM_ROWS = 512
BF16, F32 = jnp.bfloat16, jnp.float32
ANY = pl.BlockSpec(memory_space=pl.ANY)
INSIDE = pl.BlockSpec(memory_space=pltpu.VMEM)
DMA = pltpu.SemaphoreType.DMA


def kernel_call(name, kernel, operands, outs, scratch=(), aliases=None):
    return pl.pallas_call(
        kernel,
        in_specs=[INSIDE if held else ANY for _, held in operands],
        out_specs=[INSIDE if held else ANY for _, _, held in outs],
        out_shape=[
            pltpu.VMEM(shape, kind) if held else jax.ShapeDtypeStruct(shape, kind)
            for shape, kind, held in outs
        ],
        scratch_shapes=list(scratch),
        input_output_aliases=aliases or {},
        compiler_params=pltpu.CompilerParams(vmem_limit_bytes=16 << 20),
        name=name,
    )(*[
        pltpu.with_memory_space_constraint(array, pltpu.VMEM if held else pltpu.HBM)
        for array, held in operands
    ])


def gelu_and_slope(v):
    square = v * v
    inner = v * (0.7978845608 + (0.7978845608 * 0.044715) * square)
    th = jnp.tanh(inner)
    half = 0.5 + 0.5 * th
    active = v * half
    inner_slope = 0.7978845608 + (3.0 * 0.7978845608 * 0.044715) * square
    slope = half + (0.5 * v) * (1.0 - th * th) * inner_slope
    return active, slope


def lanes(start, size):
    return pl.ds(pl.multiple_of(start, 128), size)


def dot(a, b):
    return jnp.dot(a, b, preferred_element_type=F32)


def turned_dot(a, b):
    return lax.dot_general(a, b, (((0,), (0,)), ((), ())), preferred_element_type=F32)


def odd_place():
    return lax.axis_index("ctx") % 2


def end_copy(x_ref, end_ref, at_end, sem):
    length, halo = x_ref.shape[1], end_ref.shape[1]
    return pltpu.make_async_copy(x_ref.at[:, lanes(at_end * (length - halo), halo)], end_ref, sem)


def near_source_kernel(x_ref, near_ref, sem):
    copy = end_copy(x_ref, near_ref, 1 - odd_place(), sem)
    copy.start()
    copy.wait()


def upstream_kernel(order, channels, first, with_far, pw_ref, cot_ref, x_ref, *rest):
    count = len(order)
    piece_refs, rest = rest[:count], rest[count:]
    columns_ref, total_ref, sems = rest[-3:]
    cot_in = rest[0] if first else cot_ref
    ch = lax.axis_index("ch")
    blocks = []
    for m in range(0, cot_in.shape[0], UPSTREAM_ROWS):
        rows = slice(m, m + UPSTREAM_ROWS)
        pairs = [(cot_ref.at[rows], cot_in.at[rows])] if first else []
        if channels % 128 == 0:
            for place, k in enumerate(order):
                columns = lanes((ch ^ k) * channels, channels)
                held = slice(place * channels, (place + 1) * channels)
                pairs.append((pw_ref.at[rows, columns], columns_ref.at[rows, held]))
        else:
            pairs.append((pw_ref.at[rows], columns_ref.at[rows]))
        copies = [
            pltpu.make_async_copy(source, place, sems.at[len(blocks), i])
            for i, (source, place) in enumerate(pairs)
        ]
        for copy in copies:
            copy.start()
        blocks.append((rows, copies))
    if with_far:
        end = end_copy(x_ref, rest[-4], odd_place(), sems.at[0, count + 1])
        end.start()
    for step, (rows, copies) in enumerate(blocks):
        for copy in copies:
            copy.wait()
        for place in range(count):
            held = slice(place * channels, (place + 1) * channels)
            part = turned_dot(columns_ref[rows, held], cot_in[rows, :])
            if step > 0:
                part = part + total_ref[held, :]
            if step < len(blocks) - 1:
                total_ref[held, :] = part
            else:
                piece_refs[place][...] = part.astype(BF16)
    if with_far:
        end.wait()


def columns_of(pw_weight, channels, order):
    if channels % 128 == 0:
        return pw_weight
    ch = lax.axis_index("ch")
    return jnp.concatenate(
        [lax.dynamic_slice_in_dim(pw_weight, (ch ^ k) * channels, channels, 1) for k in order], axis=1
    )


def upstream(pw_weight, cotangent, inputs, order, first=False, with_far=False):
    channels = inputs.shape[0]
    total, width = cotangent.shape
    count = len(order)
    outs = [((channels, width), BF16, True)] * count
    outs += [(cotangent.shape, BF16, True)] * first
    outs += [((channels, DILATION_STEP), BF16, True)] * with_far
    results = kernel_call(
        "upstream", functools.partial(upstream_kernel, order, channels, first, with_far),
        [(columns_of(pw_weight, channels, order), False), (cotangent, not first), (inputs, False)], outs,
        [
            pltpu.VMEM((total, count * channels), BF16), pltpu.VMEM((count * channels, width), F32),
            DMA((total // UPSTREAM_ROWS, count + 2)),
        ],
    )
    return results[:count], *results[count:]


def convolve(w_ref, rows, wide, start, halo, unit):
    return sum(dot(w_ref[t, rows, :], wide[rows, lanes(start + t * halo, unit)]) for t in range(3))


def interior_kernel(n, x_ref, w_ref, *rest):
    active_refs, (slope_ref, wide, plain_ref, turned_ref, own_ref, sem, own_sem) = rest[:n], rest[n:]
    ch = lax.axis_index("ch")
    channels, length = x_ref.shape
    group = w_ref.shape[1]
    own = w_ref.at[:, :, lanes(ch * channels, channels)] if w_ref.shape[2] > channels else w_ref
    own_copy = pltpu.make_async_copy(own, own_ref, own_sem)
    own_copy.start()
    halo = DILATION_STEP
    block = length // n
    unit = min(block, 256)
    copy = pltpu.make_async_copy(x_ref, wide.at[:, halo:halo + length], sem)
    copy.start()
    groups = [slice(g, g + group) for g in range(0, channels, group)]
    own_copy.wait()
    for t in range(3):
        for rows in groups:
            square = own_ref[t, :, rows]
            turned_ref[2 - t, rows, :] = square
            plain_ref[t, rows, :] = square.T
    copy.wait()
    for k in range(n):
        base = (ch ^ k) * block

        @pl.when((base >= halo) & (base < length - halo))
        def _(k=k, base=base):
            for s in range(0, block, unit):
                for rows in groups:
                    active, slope = gelu_and_slope(convolve(plain_ref, rows, wide, base + s, halo, unit))
                    active_refs[k][rows, s:s + unit] = active.astype(BF16)
                    slope_ref[rows, lanes(base + s, unit)] = slope.astype(BF16)


def interior(inputs, weight, n):
    channels, length = inputs.shape
    group = weight.shape[1]
    block = length // n
    outs = [((channels, block), BF16, True)] * n
    outs += [((channels, length), BF16, True), ((channels, length + 2 * DILATION_STEP), BF16, True)]
    outs += [((3, channels, group), BF16, True)] * 2
    results = kernel_call(
        "interior", functools.partial(interior_kernel, n), [(inputs, False), (weight, False)], outs,
        [pltpu.VMEM((3, group, channels), BF16), DMA, DMA],
    )
    return results[:n], *results[n:]


def end_kernel(n, near, waits, *refs):
    halo_ref, plain_ref, rest = refs[waits], refs[waits + 1], refs[-(n + 2):]
    active_refs, (slope_ref, wide) = rest[:n], rest[n:]
    ch, odd = lax.axis_index("ch"), odd_place()
    channels, length = slope_ref.shape
    group = plain_ref.shape[2]
    halo = halo_ref.shape[1]
    block = length // n
    unit = min(block, 256)
    groups = [slice(g, g + group) for g in range(0, channels, group)]
    at_end = 1 - odd if near else odd
    wide[:, lanes(at_end * (halo + length), halo)] = halo_ref[...]
    first = at_end * (length - halo)
    for k in range(n):
        base = (ch ^ k) * block

        @pl.when((base >= first) & (base < first + halo))
        def _(k=k, base=base):
            for s in range(0, block, unit):
                for rows in groups:
                    active, slope = gelu_and_slope(convolve(plain_ref, rows, wide, base + s, halo, unit))
                    active_refs[k][rows, s:s + unit] = active.astype(BF16)
                    slope_ref[rows, lanes(base + s, unit)] = slope.astype(BF16)


def one_end(near, halo, plain, active, slope, wide, waited):
    n = len(active)
    operands = [(o, True) for o in (*waited, halo, plain, *active, slope, wide)]
    results = kernel_call(
        "near_end" if near else "far_end", functools.partial(end_kernel, n, near, len(waited)), operands,
        [(a.shape, a.dtype, True) for a in (*active, slope, wide)],
        aliases={len(waited) + 2 + i: i for i in range(n + 2)},
    )
    return results[:n], *results[n:]


def grad_kernel(order, slope_ref, *rest):
    up_refs, (grad_ref, near_out, far_out) = rest[:-3], rest[-3:]
    ch, odd = lax.axis_index("ch"), odd_place()
    length, halo = grad_ref.shape[1], near_out.shape[1]
    block = up_refs[0].shape[1]
    for k, up_ref in zip(order, up_refs):
        base = (ch ^ k) * block

        def product(end_ref=None, first=0, base=base, up_ref=up_ref):
            for g in range(0, up_ref.shape[0], 16):
                rows = slice(g, g + 16)
                value = up_ref[rows, :].astype(F32) * slope_ref[rows, lanes(base, block)].astype(F32)
                grad_ref[rows, lanes(base, block)] = value.astype(BF16)
                if end_ref is not None:
                    end_ref[rows, lanes(base - first, block)] = value.astype(BF16)

        inside = (base >= halo) & (base < length - halo)
        pl.when(inside)(product)
        for end_ref, first in ((near_out, (1 - odd) * (length - halo)), (far_out, odd * (length - halo))):
            pl.when((base >= first) & (base < first + halo))(functools.partial(product, end_ref, first))


def grad_conv(slope, order, ups):
    channels = slope.shape[0]
    return kernel_call(
        "grad_conv", functools.partial(grad_kernel, order),
        [(o, True) for o in (slope, *[ups[k] for k in order])],
        [(slope.shape, BF16, True)] + [((channels, DILATION_STEP), BF16, True)] * 2,
    )


def columns_times(order, pw_ref, rows, pieces):
    channels = pieces.shape[0] // len(order)
    if channels % 128 != 0:
        return dot(pw_ref[rows, :], pieces)
    return sum(
        dot(
            pw_ref[rows, lanes((lax.axis_index("ch") ^ k) * channels, channels)],
            pieces[place * channels:(place + 1) * channels],
        )
        for place, k in enumerate(order)
    )


def mix_kernel(order, pw_ref, *rest):
    piece_refs, before, sum_ref = rest[:len(order)], rest[len(order):-1], rest[-1]
    pieces = jnp.concatenate([p[...] for p in piece_refs], axis=0)
    step = 512
    for m in range(0, sum_ref.shape[0], step):
        rows = slice(m, m + step)
        part = columns_times(order, pw_ref, rows, pieces)
        sum_ref[rows, :] = part + before[0][rows, :] if before else part


def mix(name, pw_weight, order, active, before):
    channels, width = active[order[0]].shape
    operands = [columns_of(pw_weight, channels, order), *[active[k] for k in order], *before]
    return kernel_call(
        name, functools.partial(mix_kernel, order), [(o, True) for o in operands],
        [((pw_weight.shape[0], width), F32, True)],
        aliases={len(operands) - 1: 0} if before else {},
    )


def back_interior_kernel(grad_ref, turned_ref, out_ref, ends_ref, held, sem):
    channels, length = grad_ref.shape
    group, halo, unit = turned_ref.shape[2], DILATION_STEP, 256

    def taps(rows, start, which):
        return sum(
            dot(turned_ref[t, rows, :], grad_ref[rows, start + (t - 1) * halo:start + (t - 1) * halo + unit])
            for t in which
        )

    groups = [slice(g, g + group) for g in range(0, channels, group)]
    for rows in groups:
        for s in range(0, length - 2 * halo, unit):
            held[rows, s:s + unit] = taps(rows, halo + s, (0, 1, 2)).astype(BF16)
    copy = pltpu.make_async_copy(held, out_ref.at[:, halo:length - halo], sem)
    copy.start()
    for rows in groups:
        for s in range(0, halo, unit):
            ends_ref[rows, s:s + unit] = taps(rows, s, (1, 2))
            ends_ref[rows, halo + s:halo + s + unit] = taps(rows, length - halo + s, (0, 1))
    copy.wait()


def back_end(halo_ref, ends_ref, turned_ref, at_end, held):
    channels, halo = halo_ref.shape
    group, unit = turned_ref.shape[2], 256
    for g in range(0, channels, group):
        rows = slice(g, g + group)
        for s in range(0, halo, unit):
            outer = dot(turned_ref[2 * at_end, rows, :], halo_ref[rows, s:s + unit])
            held[rows, s:s + unit] = (ends_ref[rows, lanes(at_end * halo + s, unit)] + outer).astype(BF16)


def end_of(out_ref, at_end):
    return out_ref.at[:, lanes(at_end * (out_ref.shape[1] - DILATION_STEP), DILATION_STEP)]


def late_mix_kernel(order, pw_ref, sum_ref, *rest):
    piece_refs, (out_ref, done_ref, held, sems) = rest[:len(order)], rest[len(order):]
    pieces = jnp.concatenate([p[...] for p in piece_refs], axis=0)
    step = 512
    copies = []
    for m in range(0, sum_ref.shape[0], step):
        rows = slice(m, m + step)
        held[rows, :] = (sum_ref[rows, :] + columns_times(order, pw_ref, rows, pieces)).astype(BF16)
        copies.append(pltpu.make_async_copy(held.at[rows, :], out_ref.at[rows, :], sems.at[len(copies)]))
        copies[-1].start()
    done_ref[...] = jnp.zeros_like(done_ref)
    for copy in copies:
        copy.wait()


def late_mix(pw_weight, order, partial, active):
    channels = active[order[0]].shape[0]
    operands = [columns_of(pw_weight, channels, order), partial, *[active[k] for k in order]]
    return kernel_call(
        "late_mix", functools.partial(late_mix_kernel, order), [(o, True) for o in operands],
        [(partial.shape, BF16, False), ((8, 128), F32, True)],
        [pltpu.VMEM(partial.shape, BF16), DMA((partial.shape[0] // 512,))],
    )


def back_ends_kernel(near_ref, far_ref, ends_ref, turned_ref, _, __, out_ref, both, sems):
    odd = odd_place()
    copies = []
    for place, (halo_ref, at_end) in enumerate(((near_ref, 1 - odd), (far_ref, odd))):
        back_end(halo_ref, ends_ref, turned_ref, at_end, both.at[place])
        copies.append(pltpu.make_async_copy(both.at[place], end_of(out_ref, at_end), sems.at[place]))
        copies[-1].start()
    for copy in copies:
        copy.wait()


def back_ends(near, far, ends, turned, done, grad_inputs):
    operands = [(o, True) for o in (near, far, ends, turned, done)] + [(grad_inputs, False)]
    (result,) = kernel_call(
        "back_ends", back_ends_kernel, operands, [(grad_inputs.shape, BF16, False)],
        [pltpu.VMEM((2, *near.shape), BF16), DMA((2,))], {5: 0},
    )
    return result


def arrived(arrays):
    return kernel_call(
        "arrived", lambda *refs: None, [(o, True) for o in arrays], [(o.shape, o.dtype, True) for o in arrays],
        aliases={i: i for i in range(len(arrays))},
    )


def exchange(piece, k):
    if k == 0:
        return piece
    return lax.ppermute(piece, "ch", [(i, i ^ k) for i in range(lax.axis_size("ch"))])


def swap(values, first):
    size = lax.axis_size("ctx")
    pairs = [(i, i + 1) for i in range(first, size - 1, 2)]
    return lax.ppermute(values, "ctx", pairs + [(b, a) for a, b in pairs])


def body(inputs, conv_weight, pw_weight, cotangent):
    n = lax.axis_size("ch")
    channels, length = inputs.shape
    halo = DILATION_STEP
    order = [*range(n // 2, n), *range(n // 2 - 1, -1, -1)]
    first, second, rest = order[:n // 4], order[n // 4:n // 2], order[n // 2:]

    weight = jnp.swapaxes(conv_weight, 1, 2)
    if channels % 128 != 0:
        weight = lax.dynamic_slice_in_dim(weight, lax.axis_index("ch") * channels, channels, 2)
    (near,) = kernel_call(
        "near_source", near_source_kernel, [(inputs, False)], [((channels, halo), BF16, True)], [DMA]
    )
    near = swap(near, 0)
    pieces, cot_in = upstream(pw_weight, cotangent, inputs, first, first=True)
    ups = {k: exchange(p, k) for k, p in zip(first, pieces)}
    pieces, far = upstream(pw_weight, cot_in, inputs, second, with_far=True)
    far = swap(far, 1)
    ups.update({k: exchange(p, k) for k, p in zip(second, pieces)})
    (pieces,) = upstream(pw_weight, cot_in, inputs, rest)
    ups.update({k: exchange(p, k) for k, p in zip(rest, pieces)})

    active, slope, wide, plain, turned = interior(inputs, weight, n)
    active, slope, wide = one_end(True, near, plain, active, slope, wide, [ups[first[0]]])
    active, slope, wide = one_end(False, far, plain, active, slope, wide, [])
    ups.update(zip(second, arrived([ups[k] for k in second])))
    grad, near_grad, far_grad = grad_conv(slope, order, ups)
    active = {k: exchange(active[k], k) for k in order}
    near_grad, far_grad = swap(near_grad, 0), swap(far_grad, 1)

    grad_inputs, ends = kernel_call(
        "back_interior", back_interior_kernel, [(grad, True), (turned, True)],
        [((channels, length), BF16, False), ((channels, 2 * halo), F32, True)],
        [pltpu.VMEM((channels, length - 2 * halo), BF16), DMA],
    )
    partial = mix("early_mix", pw_weight, first, active, [])
    (partial,) = mix("half_mix", pw_weight, rest, active, partial)
    mixed, done = late_mix(pw_weight, second, partial, active)
    return mixed, back_ends(near_grad, far_grad, ends, turned, done, grad_inputs)


def solution(mesh):
    placed = (P("ch", "ctx"), P(), P(), P(None, ("ctx", "ch")))
    return jax.shard_map(
        body,
        mesh=mesh,
        in_specs=placed,
        out_specs=(P(None, ("ctx", "ch")), P("ch", "ctx")),
        check_vma=False,
    )
```

```python
import functools

import jax
import jax.numpy as jnp
from jax import lax
from jax.experimental import pallas as pl
from jax.experimental.pallas import tpu as pltpu
from jax.sharding import PartitionSpec as P

DILATION_STEP = 512
UPSTREAM_ROWS = 512
BF16, F32 = jnp.bfloat16, jnp.float32
ANY = pl.BlockSpec(memory_space=pl.ANY)
INSIDE = pl.BlockSpec(memory_space=pltpu.VMEM)
DMA = pltpu.SemaphoreType.DMA


def kernel_call(name, kernel, operands, outs, scratch=(), aliases=None):
    return pl.pallas_call(
        kernel,
        in_specs=[INSIDE if held else ANY for _, held in operands],
        out_specs=[INSIDE if held else ANY for _, _, held in outs],
        out_shape=[
            pltpu.VMEM(shape, kind) if held else jax.ShapeDtypeStruct(shape, kind)
            for shape, kind, held in outs
        ],
        scratch_shapes=list(scratch),
        input_output_aliases=aliases or {},
        compiler_params=pltpu.CompilerParams(vmem_limit_bytes=16 << 20),
        name=name,
    )(*[
        pltpu.with_memory_space_constraint(array, pltpu.VMEM if held else pltpu.HBM)
        for array, held in operands
    ])


def gelu_and_slope(v):
    square = v * v
    inner = v * (0.7978845608 + (0.7978845608 * 0.044715) * square)
    th = jnp.tanh(inner)
    half = 0.5 + 0.5 * th
    active = v * half
    inner_slope = 0.7978845608 + (3.0 * 0.7978845608 * 0.044715) * square
    slope = half + (0.5 * v) * (1.0 - th * th) * inner_slope
    return active, slope


def lanes(start, size):
    return pl.ds(pl.multiple_of(start, 128), size)


def dot(a, b):
    return jnp.dot(a, b, preferred_element_type=F32)


def turned_dot(a, b):
    return lax.dot_general(a, b, (((0,), (0,)), ((), ())), preferred_element_type=F32)


def odd_place():
    return lax.axis_index("ctx") % 2


def end_copy(x_ref, end_ref, at_end, sem):
    length, halo = x_ref.shape[1], end_ref.shape[1]
    return pltpu.make_async_copy(x_ref.at[:, lanes(at_end * (length - halo), halo)], end_ref, sem)


def near_source_kernel(x_ref, near_ref, sem):
    copy = end_copy(x_ref, near_ref, 1 - odd_place(), sem)
    copy.start()
    copy.wait()


def upstream_kernel(order, channels, first, with_far, pw_ref, cot_ref, x_ref, *rest):
    count = len(order)
    piece_refs, rest = rest[:count], rest[count:]
    columns_ref, total_ref, sems = rest[-3:]
    cot_in = rest[0] if first else cot_ref
    ch = lax.axis_index("ch")
    blocks = []
    for m in range(0, cot_in.shape[0], UPSTREAM_ROWS):
        rows = slice(m, m + UPSTREAM_ROWS)
        pairs = [(cot_ref.at[rows], cot_in.at[rows])] if first else []
        if channels % 128 == 0:
            for place, k in enumerate(order):
                columns = lanes((ch ^ k) * channels, channels)
                held = slice(place * channels, (place + 1) * channels)
                pairs.append((pw_ref.at[rows, columns], columns_ref.at[rows, held]))
        else:
            pairs.append((pw_ref.at[rows], columns_ref.at[rows]))
        copies = [
            pltpu.make_async_copy(source, place, sems.at[len(blocks), i])
            for i, (source, place) in enumerate(pairs)
        ]
        for copy in copies:
            copy.start()
        blocks.append((rows, copies))
    if with_far:
        end = end_copy(x_ref, rest[-4], odd_place(), sems.at[0, count + 1])
        end.start()
    for step, (rows, copies) in enumerate(blocks):
        for copy in copies:
            copy.wait()
        for place in range(count):
            held = slice(place * channels, (place + 1) * channels)
            part = turned_dot(columns_ref[rows, held], cot_in[rows, :])
            if step > 0:
                part = part + total_ref[held, :]
            if step < len(blocks) - 1:
                total_ref[held, :] = part
            else:
                piece_refs[place][...] = part.astype(BF16)
    if with_far:
        end.wait()


def columns_of(pw_weight, channels, order):
    if channels % 128 == 0:
        return pw_weight
    ch = lax.axis_index("ch")
    return jnp.concatenate(
        [lax.dynamic_slice_in_dim(pw_weight, (ch ^ k) * channels, channels, 1) for k in order], axis=1
    )


def upstream(pw_weight, cotangent, inputs, order, first=False, with_far=False):
    channels = inputs.shape[0]
    total, width = cotangent.shape
    count = len(order)
    outs = [((channels, width), BF16, True)] * count
    outs += [(cotangent.shape, BF16, True)] * first
    outs += [((channels, DILATION_STEP), BF16, True)] * with_far
    results = kernel_call(
        "upstream", functools.partial(upstream_kernel, order, channels, first, with_far),
        [(columns_of(pw_weight, channels, order), False), (cotangent, not first), (inputs, False)], outs,
        [
            pltpu.VMEM((total, count * channels), BF16), pltpu.VMEM((count * channels, width), F32),
            DMA((total // UPSTREAM_ROWS, count + 2)),
        ],
    )
    return results[:count], *results[count:]


def convolve(w_ref, rows, wide, start, halo, unit):
    return sum(dot(w_ref[t, rows, :], wide[rows, lanes(start + t * halo, unit)]) for t in range(3))


def interior_kernel(n, x_ref, w_ref, *rest):
    active_refs, (slope_ref, wide, plain_ref, turned_ref, own_ref, sem, own_sem) = rest[:n], rest[n:]
    ch = lax.axis_index("ch")
    channels, length = x_ref.shape
    group = w_ref.shape[1]
    own = w_ref.at[:, :, lanes(ch * channels, channels)] if w_ref.shape[2] > channels else w_ref
    own_copy = pltpu.make_async_copy(own, own_ref, own_sem)
    own_copy.start()
    halo = DILATION_STEP
    block = length // n
    unit = min(block, 256)
    copy = pltpu.make_async_copy(x_ref, wide.at[:, halo:halo + length], sem)
    copy.start()
    groups = [slice(g, g + group) for g in range(0, channels, group)]
    own_copy.wait()
    for t in range(3):
        for rows in groups:
            square = own_ref[t, :, rows]
            turned_ref[2 - t, rows, :] = square
            plain_ref[t, rows, :] = square.T
    copy.wait()
    for k in range(n):
        base = (ch ^ k) * block

        @pl.when((base >= halo) & (base < length - halo))
        def _(k=k, base=base):
            for s in range(0, block, unit):
                for rows in groups:
                    active, slope = gelu_and_slope(convolve(plain_ref, rows, wide, base + s, halo, unit))
                    active_refs[k][rows, s:s + unit] = active.astype(BF16)
                    slope_ref[rows, lanes(base + s, unit)] = slope


def interior(inputs, weight, n):
    channels, length = inputs.shape
    group = weight.shape[1]
    block = length // n
    outs = [((channels, block), BF16, True)] * n
    outs += [((channels, length), F32, True), ((channels, length + 2 * DILATION_STEP), BF16, True)]
    outs += [((3, channels, group), BF16, True)] * 2
    results = kernel_call(
        "interior", functools.partial(interior_kernel, n), [(inputs, False), (weight, False)], outs,
        [pltpu.VMEM((3, group, channels), BF16), DMA, DMA],
    )
    return results[:n], *results[n:]


def end_kernel(n, near, waits, *refs):
    halo_ref, plain_ref, rest = refs[waits], refs[waits + 1], refs[-(n + 2):]
    active_refs, (slope_ref, wide) = rest[:n], rest[n:]
    ch, odd = lax.axis_index("ch"), odd_place()
    channels, length = slope_ref.shape
    group = plain_ref.shape[2]
    halo = halo_ref.shape[1]
    block = length // n
    unit = min(block, 256)
    groups = [slice(g, g + group) for g in range(0, channels, group)]
    at_end = 1 - odd if near else odd
    wide[:, lanes(at_end * (halo + length), halo)] = halo_ref[...]
    first = at_end * (length - halo)
    for k in range(n):
        base = (ch ^ k) * block

        @pl.when((base >= first) & (base < first + halo))
        def _(k=k, base=base):
            for s in range(0, block, unit):
                for rows in groups:
                    active, slope = gelu_and_slope(convolve(plain_ref, rows, wide, base + s, halo, unit))
                    active_refs[k][rows, s:s + unit] = active.astype(BF16)
                    slope_ref[rows, lanes(base + s, unit)] = slope


def one_end(near, halo, plain, active, slope, wide, waited):
    n = len(active)
    operands = [(o, True) for o in (*waited, halo, plain, *active, slope, wide)]
    results = kernel_call(
        "near_end" if near else "far_end", functools.partial(end_kernel, n, near, len(waited)), operands,
        [(a.shape, a.dtype, True) for a in (*active, slope, wide)],
        aliases={len(waited) + 2 + i: i for i in range(n + 2)},
    )
    return results[:n], *results[n:]


def grad_kernel(order, slope_ref, *rest):
    up_refs, (grad_ref, near_out, far_out) = rest[:-3], rest[-3:]
    ch, odd = lax.axis_index("ch"), odd_place()
    length, halo = grad_ref.shape[1], near_out.shape[1]
    block = up_refs[0].shape[1]
    step = 32

    @pl.loop(0, grad_ref.shape[0] // step)
    def _(i):
        rows = pl.ds(pl.multiple_of(i * step, step), step)
        for k, up_ref in zip(order, up_refs):
            here = lanes((ch ^ k) * block, block)
            grad_ref[rows, here] = (up_ref[rows, :].astype(F32) * slope_ref[rows, here]).astype(BF16)
        near_out[rows, :] = grad_ref[rows, lanes((1 - odd) * (length - halo), halo)]
        far_out[rows, :] = grad_ref[rows, lanes(odd * (length - halo), halo)]


def grad_conv(slope, order, ups):
    channels = slope.shape[0]
    return kernel_call(
        "grad_conv", functools.partial(grad_kernel, order),
        [(o, True) for o in (slope, *[ups[k] for k in order])],
        [(slope.shape, BF16, True)] + [((channels, DILATION_STEP), BF16, True)] * 2,
    )


def columns_times(order, pw_ref, rows, pieces):
    channels = pieces.shape[0] // len(order)
    if channels % 128 != 0:
        return dot(pw_ref[rows, :], pieces)
    return sum(
        dot(
            pw_ref[rows, lanes((lax.axis_index("ch") ^ k) * channels, channels)],
            pieces[place * channels:(place + 1) * channels],
        )
        for place, k in enumerate(order)
    )


def mix_kernel(order, pw_ref, *rest):
    piece_refs, before, sum_ref = rest[:len(order)], rest[len(order):-1], rest[-1]
    pieces = jnp.concatenate([p[...] for p in piece_refs], axis=0)
    step = 512
    for m in range(0, sum_ref.shape[0], step):
        rows = slice(m, m + step)
        part = columns_times(order, pw_ref, rows, pieces)
        sum_ref[rows, :] = part + before[0][rows, :] if before else part


def mix(name, pw_weight, order, active, before):
    channels, width = active[order[0]].shape
    operands = [columns_of(pw_weight, channels, order), *[active[k] for k in order], *before]
    return kernel_call(
        name, functools.partial(mix_kernel, order), [(o, True) for o in operands],
        [((pw_weight.shape[0], width), F32, True)],
        aliases={len(operands) - 1: 0} if before else {},
    )


def back_interior_kernel(grad_ref, turned_ref, out_ref, ends_ref, held, sem):
    channels, length = grad_ref.shape
    group, halo, unit = turned_ref.shape[2], DILATION_STEP, 256

    def taps(rows, start, which):
        return sum(
            dot(turned_ref[t, rows, :], grad_ref[rows, start + (t - 1) * halo:start + (t - 1) * halo + unit])
            for t in which
        )

    groups = [slice(g, g + group) for g in range(0, channels, group)]
    for rows in groups:
        for s in range(0, length - 2 * halo, unit):
            held[rows, s:s + unit] = taps(rows, halo + s, (0, 1, 2)).astype(BF16)
    copy = pltpu.make_async_copy(held, out_ref.at[:, halo:length - halo], sem)
    copy.start()
    for rows in groups:
        for s in range(0, halo, unit):
            ends_ref[rows, s:s + unit] = taps(rows, s, (1, 2))
            ends_ref[rows, halo + s:halo + s + unit] = taps(rows, length - halo + s, (0, 1))
    copy.wait()


def back_end(halo_ref, ends_ref, turned_ref, at_end, held):
    channels, halo = halo_ref.shape
    group, unit = turned_ref.shape[2], 256

    @pl.loop(0, channels // group)
    def _(g):
        rows = pl.ds(pl.multiple_of(g * group, 16), group)
        for s in range(0, halo, unit):
            outer = dot(turned_ref[2 * at_end, rows, :], halo_ref[rows, s:s + unit])
            held[rows, s:s + unit] = (ends_ref[rows, lanes(at_end * halo + s, unit)] + outer).astype(BF16)


def end_of(out_ref, at_end):
    return out_ref.at[:, lanes(at_end * (out_ref.shape[1] - DILATION_STEP), DILATION_STEP)]


def late_mix_kernel(order, pw_ref, sum_ref, *rest):
    piece_refs, (out_ref, done_ref, held, sems) = rest[:len(order)], rest[len(order):]
    pieces = jnp.concatenate([p[...] for p in piece_refs], axis=0)
    step = 512
    copies = []
    for m in range(0, sum_ref.shape[0], step):
        rows = slice(m, m + step)
        held[rows, :] = (sum_ref[rows, :] + columns_times(order, pw_ref, rows, pieces)).astype(BF16)
        copies.append(pltpu.make_async_copy(held.at[rows, :], out_ref.at[rows, :], sems.at[len(copies)]))
        copies[-1].start()
    done_ref[...] = jnp.zeros_like(done_ref)
    for copy in copies:
        copy.wait()


def late_mix(pw_weight, order, partial, active):
    channels = active[order[0]].shape[0]
    operands = [columns_of(pw_weight, channels, order), partial, *[active[k] for k in order]]
    return kernel_call(
        "late_mix", functools.partial(late_mix_kernel, order), [(o, True) for o in operands],
        [(partial.shape, BF16, False), ((8, 128), F32, True)],
        [pltpu.VMEM(partial.shape, BF16), DMA((partial.shape[0] // 512,))],
    )


def back_ends_kernel(near_ref, far_ref, ends_ref, turned_ref, _, __, out_ref, both, sems):
    odd = odd_place()
    copies = []
    for place, (halo_ref, at_end) in enumerate(((near_ref, 1 - odd), (far_ref, odd))):
        back_end(halo_ref, ends_ref, turned_ref, at_end, both.at[place])
        copies.append(pltpu.make_async_copy(both.at[place], end_of(out_ref, at_end), sems.at[place]))
        copies[-1].start()
    for copy in copies:
        copy.wait()


def back_ends(near, far, ends, turned, done, grad_inputs):
    operands = [(o, True) for o in (near, far, ends, turned, done)] + [(grad_inputs, False)]
    (result,) = kernel_call(
        "back_ends", back_ends_kernel, operands, [(grad_inputs.shape, BF16, False)],
        [pltpu.VMEM((2, *near.shape), BF16), DMA((2,))], {5: 0},
    )
    return result


def arrived(arrays):
    return kernel_call(
        "arrived", lambda *refs: None, [(o, True) for o in arrays], [(o.shape, o.dtype, True) for o in arrays],
        aliases={i: i for i in range(len(arrays))},
    )


def exchange(piece, k):
    if k == 0:
        return piece
    return lax.ppermute(piece, "ch", [(i, i ^ k) for i in range(lax.axis_size("ch"))])


def swap(values, first):
    size = lax.axis_size("ctx")
    pairs = [(i, i + 1) for i in range(first, size - 1, 2)]
    return lax.ppermute(values, "ctx", pairs + [(b, a) for a, b in pairs])


def body(inputs, conv_weight, pw_weight, cotangent):
    n = lax.axis_size("ch")
    channels, length = inputs.shape
    halo = DILATION_STEP
    order = [*range(n // 2, n), *range(n // 2 - 1, -1, -1)]
    first, second, rest = order[:n // 4], order[n // 4:n // 2], order[n // 2:]

    weight = jnp.swapaxes(conv_weight, 1, 2)
    if channels % 128 != 0:
        weight = lax.dynamic_slice_in_dim(weight, lax.axis_index("ch") * channels, channels, 2)
    (near,) = kernel_call(
        "near_source", near_source_kernel, [(inputs, False)], [((channels, halo), BF16, True)], [DMA]
    )
    near = swap(near, 0)
    pieces, cot_in = upstream(pw_weight, cotangent, inputs, first, first=True)
    ups = {k: exchange(p, k) for k, p in zip(first, pieces)}
    pieces, far = upstream(pw_weight, cot_in, inputs, second, with_far=True)
    far = swap(far, 1)
    ups.update({k: exchange(p, k) for k, p in zip(second, pieces)})
    (pieces,) = upstream(pw_weight, cot_in, inputs, rest)
    ups.update({k: exchange(p, k) for k, p in zip(rest, pieces)})

    active, slope, wide, plain, turned = interior(inputs, weight, n)
    active, slope, wide = one_end(True, near, plain, active, slope, wide, [ups[first[0]]])
    active, slope, wide = one_end(False, far, plain, active, slope, wide, [])
    ups.update(zip(second, arrived([ups[k] for k in second])))
    grad, near_grad, far_grad = grad_conv(slope, order, ups)
    active = {k: exchange(active[k], k) for k in order}
    near_grad, far_grad = swap(near_grad, 0), swap(far_grad, 1)

    grad_inputs, ends = kernel_call(
        "back_interior", back_interior_kernel, [(grad, True), (turned, True)],
        [((channels, length), BF16, False), ((channels, 2 * halo), F32, True)],
        [pltpu.VMEM((channels, length - 2 * halo), BF16), DMA],
    )
    partial = mix("early_mix", pw_weight, first, active, [])
    (partial,) = mix("half_mix", pw_weight, rest, active, partial)
    mixed, done = late_mix(pw_weight, second, partial, active)
    return mixed, back_ends(near_grad, far_grad, ends, turned, done, grad_inputs)


def solution(mesh):
    placed = (P("ch", "ctx"), P(), P(), P(None, ("ctx", "ch")))
    return jax.shard_map(
        body,
        mesh=mesh,
        in_specs=placed,
        out_specs=(P(None, ("ctx", "ch")), P("ch", "ctx")),
        check_vma=False,
    )
```

```python
import functools

import jax
import jax.numpy as jnp
from jax import lax
from jax.experimental import pallas as pl
from jax.experimental.pallas import tpu as pltpu
from jax.sharding import PartitionSpec as P

DILATION_STEP = 512
UPSTREAM_ROWS = 512
BF16, F32 = jnp.bfloat16, jnp.float32
ANY = pl.BlockSpec(memory_space=pl.ANY)
INSIDE = pl.BlockSpec(memory_space=pltpu.VMEM)
DMA = pltpu.SemaphoreType.DMA


def kernel_call(name, kernel, operands, outs, scratch=(), aliases=None):
    return pl.pallas_call(
        kernel,
        in_specs=[INSIDE if held else ANY for _, held in operands],
        out_specs=[INSIDE if held else ANY for _, _, held in outs],
        out_shape=[
            pltpu.VMEM(shape, kind) if held else jax.ShapeDtypeStruct(shape, kind)
            for shape, kind, held in outs
        ],
        scratch_shapes=list(scratch),
        input_output_aliases=aliases or {},
        compiler_params=pltpu.CompilerParams(vmem_limit_bytes=16 << 20),
        name=name,
    )(*[
        pltpu.with_memory_space_constraint(array, pltpu.VMEM if held else pltpu.HBM)
        for array, held in operands
    ])


def gelu_and_slope(v):
    square = v * v
    inner = v * (0.7978845608 + (0.7978845608 * 0.044715) * square)
    th = jnp.tanh(inner)
    half = 0.5 + 0.5 * th
    active = v * half
    inner_slope = 0.7978845608 + (3.0 * 0.7978845608 * 0.044715) * square
    slope = half + (0.5 * v) * (1.0 - th * th) * inner_slope
    return active, slope


def lanes(start, size):
    return pl.ds(pl.multiple_of(start, 128), size)


def dot(a, b):
    return jnp.dot(a, b, preferred_element_type=F32)


def turned_dot(a, b):
    return lax.dot_general(a, b, (((0,), (0,)), ((), ())), preferred_element_type=F32)


def odd_place():
    return lax.axis_index("ctx") % 2


def end_copy(x_ref, end_ref, at_end, sem):
    length, halo = x_ref.shape[1], end_ref.shape[1]
    return pltpu.make_async_copy(x_ref.at[:, lanes(at_end * (length - halo), halo)], end_ref, sem)


def near_source_kernel(x_ref, near_ref, sem):
    copy = end_copy(x_ref, near_ref, 1 - odd_place(), sem)
    copy.start()
    copy.wait()


def upstream_kernel(order, channels, first, with_far, pw_ref, cot_ref, x_ref, *rest):
    count = len(order)
    piece_refs, rest = rest[:count], rest[count:]
    columns_ref, total_ref, sems = rest[-3:]
    cot_in = rest[0] if first else cot_ref
    ch = lax.axis_index("ch")
    blocks = []
    for m in range(0, cot_in.shape[0], UPSTREAM_ROWS):
        rows = slice(m, m + UPSTREAM_ROWS)
        pairs = [(cot_ref.at[rows], cot_in.at[rows])] if first else []
        if channels % 128 == 0:
            for place, k in enumerate(order):
                columns = lanes((ch ^ k) * channels, channels)
                held = slice(place * channels, (place + 1) * channels)
                pairs.append((pw_ref.at[rows, columns], columns_ref.at[rows, held]))
        else:
            pairs.append((pw_ref.at[rows], columns_ref.at[rows]))
        copies = [
            pltpu.make_async_copy(source, place, sems.at[len(blocks), i])
            for i, (source, place) in enumerate(pairs)
        ]
        for copy in copies:
            copy.start()
        blocks.append((rows, copies))
    if with_far:
        end = end_copy(x_ref, rest[-4], odd_place(), sems.at[0, count + 1])
        end.start()
    for step, (rows, copies) in enumerate(blocks):
        for copy in copies:
            copy.wait()
        for place in range(count):
            held = slice(place * channels, (place + 1) * channels)
            part = turned_dot(columns_ref[rows, held], cot_in[rows, :])
            if step > 0:
                part = part + total_ref[held, :]
            if step < len(blocks) - 1:
                total_ref[held, :] = part
            else:
                piece_refs[place][...] = part.astype(BF16)
    if with_far:
        end.wait()


def columns_of(pw_weight, channels, order):
    if channels % 128 == 0:
        return pw_weight
    ch = lax.axis_index("ch")
    return jnp.concatenate(
        [lax.dynamic_slice_in_dim(pw_weight, (ch ^ k) * channels, channels, 1) for k in order], axis=1
    )


def upstream(pw_weight, cotangent, inputs, order, first=False, with_far=False):
    channels = inputs.shape[0]
    total, width = cotangent.shape
    count = len(order)
    outs = [((channels, width), BF16, True)] * count
    outs += [(cotangent.shape, BF16, True)] * first
    outs += [((channels, DILATION_STEP), BF16, True)] * with_far
    results = kernel_call(
        "upstream", functools.partial(upstream_kernel, order, channels, first, with_far),
        [(columns_of(pw_weight, channels, order), False), (cotangent, not first), (inputs, False)], outs,
        [
            pltpu.VMEM((total, count * channels), BF16), pltpu.VMEM((count * channels, width), F32),
            DMA((total // UPSTREAM_ROWS, count + 2)),
        ],
    )
    return results[:count], *results[count:]


def convolve(w_ref, rows, wide, start, halo, unit):
    return sum(dot(w_ref[t, rows, :], wide[rows, lanes(start + t * halo, unit)]) for t in range(3))


def interior_kernel(n, x_ref, w_ref, *rest):
    active_refs, (slope_ref, wide, plain_ref, turned_ref, own_ref, sem, own_sem) = rest[:n], rest[n:]
    ch = lax.axis_index("ch")
    channels, length = x_ref.shape
    group = w_ref.shape[1]
    own = w_ref.at[:, :, lanes(ch * channels, channels)] if w_ref.shape[2] > channels else w_ref
    own_copy = pltpu.make_async_copy(own, own_ref, own_sem)
    own_copy.start()
    halo = DILATION_STEP
    block = length // n
    unit = min(block, 256)
    copy = pltpu.make_async_copy(x_ref, wide.at[:, halo:halo + length], sem)
    copy.start()
    groups = [slice(g, g + group) for g in range(0, channels, group)]
    own_copy.wait()
    for t in range(3):
        for rows in groups:
            square = own_ref[t, :, rows]
            turned_ref[2 - t, rows, :] = square
            plain_ref[t, rows, :] = square.T
    copy.wait()
    for k in range(n):
        base = (ch ^ k) * block

        @pl.when((base >= halo) & (base < length - halo))
        def _(k=k, base=base):
            for s in range(0, block, unit):
                for rows in groups:
                    active, slope = gelu_and_slope(convolve(plain_ref, rows, wide, base + s, halo, unit))
                    active_refs[k][rows, s:s + unit] = active.astype(BF16)
                    slope_ref[rows, lanes(base + s, unit)] = slope


def interior(inputs, weight, n):
    channels, length = inputs.shape
    group = weight.shape[1]
    block = length // n
    outs = [((channels, block), BF16, True)] * n
    outs += [((channels, length), F32, True), ((channels, length + 2 * DILATION_STEP), BF16, True)]
    outs += [((3, channels, group), BF16, True)] * 2
    results = kernel_call(
        "interior", functools.partial(interior_kernel, n), [(inputs, False), (weight, False)], outs,
        [pltpu.VMEM((3, group, channels), BF16), DMA, DMA],
    )
    return results[:n], *results[n:]


def end_kernel(n, near, waits, *refs):
    halo_ref, plain_ref, rest = refs[waits], refs[waits + 1], refs[-(n + 2):]
    active_refs, (slope_ref, wide) = rest[:n], rest[n:]
    ch, odd = lax.axis_index("ch"), odd_place()
    channels, length = slope_ref.shape
    group = plain_ref.shape[2]
    halo = halo_ref.shape[1]
    block = length // n
    unit = min(block, 256)
    groups = [slice(g, g + group) for g in range(0, channels, group)]
    at_end = 1 - odd if near else odd
    wide[:, lanes(at_end * (halo + length), halo)] = halo_ref[...]
    first = at_end * (length - halo)
    for k in range(n):
        base = (ch ^ k) * block

        @pl.when((base >= first) & (base < first + halo))
        def _(k=k, base=base):
            for s in range(0, block, unit):
                for rows in groups:
                    active, slope = gelu_and_slope(convolve(plain_ref, rows, wide, base + s, halo, unit))
                    active_refs[k][rows, s:s + unit] = active.astype(BF16)
                    slope_ref[rows, lanes(base + s, unit)] = slope


def one_end(near, halo, plain, active, slope, wide, waited):
    n = len(active)
    operands = [(o, True) for o in (*waited, halo, plain, *active, slope, wide)]
    results = kernel_call(
        "near_end" if near else "far_end", functools.partial(end_kernel, n, near, len(waited)), operands,
        [(a.shape, a.dtype, True) for a in (*active, slope, wide)],
        aliases={len(waited) + 2 + i: i for i in range(n + 2)},
    )
    return results[:n], *results[n:]


def grad_kernel(order, slope_ref, *rest):
    up_refs, (grad_ref, near_out, far_out) = rest[:-3], rest[-3:]
    ch, odd = lax.axis_index("ch"), odd_place()
    length, halo = grad_ref.shape[1], near_out.shape[1]
    block = up_refs[0].shape[1]
    step = 32

    @pl.loop(0, grad_ref.shape[0] // step)
    def _(i):
        rows = pl.ds(pl.multiple_of(i * step, step), step)
        for k, up_ref in zip(order, up_refs):
            here = lanes((ch ^ k) * block, block)
            grad_ref[rows, here] = (up_ref[rows, :].astype(F32) * slope_ref[rows, here]).astype(BF16)
        near_out[rows, :] = grad_ref[rows, lanes((1 - odd) * (length - halo), halo)]
        far_out[rows, :] = grad_ref[rows, lanes(odd * (length - halo), halo)]


def grad_conv(slope, order, ups):
    channels = slope.shape[0]
    return kernel_call(
        "grad_conv", functools.partial(grad_kernel, order),
        [(o, True) for o in (slope, *[ups[k] for k in order])],
        [(slope.shape, BF16, True)] + [((channels, DILATION_STEP), BF16, True)] * 2,
    )


def columns_times(order, pw_ref, rows, pieces):
    channels = pieces.shape[0] // len(order)
    if channels % 128 != 0:
        return dot(pw_ref[rows, :], pieces)
    return sum(
        dot(
            pw_ref[rows, lanes((lax.axis_index("ch") ^ k) * channels, channels)],
            pieces[place * channels:(place + 1) * channels],
        )
        for place, k in enumerate(order)
    )


def mix_kernel(order, pw_ref, *rest):
    piece_refs, before, sum_ref = rest[:len(order)], rest[len(order):-1], rest[-1]
    pieces = jnp.concatenate([p[...] for p in piece_refs], axis=0)
    step = 512
    for m in range(0, sum_ref.shape[0], step):
        rows = slice(m, m + step)
        part = columns_times(order, pw_ref, rows, pieces)
        sum_ref[rows, :] = part + before[0][rows, :] if before else part


def mix(name, pw_weight, order, active, before):
    channels, width = active[order[0]].shape
    operands = [columns_of(pw_weight, channels, order), *[active[k] for k in order], *before]
    return kernel_call(
        name, functools.partial(mix_kernel, order), [(o, True) for o in operands],
        [((pw_weight.shape[0], width), F32, True)],
        aliases={len(operands) - 1: 0} if before else {},
    )


def back_interior_kernel(grad_ref, turned_ref, out_ref, ends_ref, held, sem):
    channels, length = grad_ref.shape
    group, halo, unit = turned_ref.shape[2], DILATION_STEP, 256

    def taps(rows, start, which):
        return sum(
            dot(turned_ref[t, rows, :], grad_ref[rows, start + (t - 1) * halo:start + (t - 1) * halo + unit])
            for t in which
        )

    groups = [slice(g, g + group) for g in range(0, channels, group)]
    for rows in groups:
        for s in range(0, length - 2 * halo, unit):
            held[rows, s:s + unit] = taps(rows, halo + s, (0, 1, 2)).astype(BF16)
    copy = pltpu.make_async_copy(held, out_ref.at[:, halo:length - halo], sem)
    copy.start()
    for rows in groups:
        for s in range(0, halo, unit):
            ends_ref[rows, s:s + unit] = taps(rows, s, (1, 2))
            ends_ref[rows, halo + s:halo + s + unit] = taps(rows, length - halo + s, (0, 1))
    copy.wait()


def back_end(halo_ref, ends_ref, turned_ref, at_end, held):
    channels, halo = halo_ref.shape
    group, unit = turned_ref.shape[2], 256
    for g in range(0, channels, group):
        rows = slice(g, g + group)
        for s in range(0, halo, unit):
            outer = dot(turned_ref[2 * at_end, rows, :], halo_ref[rows, s:s + unit])
            held[rows, s:s + unit] = (ends_ref[rows, lanes(at_end * halo + s, unit)] + outer).astype(BF16)


def end_of(out_ref, at_end):
    return out_ref.at[:, lanes(at_end * (out_ref.shape[1] - DILATION_STEP), DILATION_STEP)]


def late_mix_kernel(order, pw_ref, sum_ref, *rest):
    piece_refs, (out_ref, done_ref, held, sems) = rest[:len(order)], rest[len(order):]
    pieces = jnp.concatenate([p[...] for p in piece_refs], axis=0)
    step = 512
    copies = []
    for m in range(0, sum_ref.shape[0], step):
        rows = slice(m, m + step)
        held[rows, :] = (sum_ref[rows, :] + columns_times(order, pw_ref, rows, pieces)).astype(BF16)
        copies.append(pltpu.make_async_copy(held.at[rows, :], out_ref.at[rows, :], sems.at[len(copies)]))
        copies[-1].start()
    done_ref[...] = jnp.zeros_like(done_ref)
    for copy in copies:
        copy.wait()


def late_mix(pw_weight, order, partial, active):
    channels = active[order[0]].shape[0]
    operands = [columns_of(pw_weight, channels, order), partial, *[active[k] for k in order]]
    return kernel_call(
        "late_mix", functools.partial(late_mix_kernel, order), [(o, True) for o in operands],
        [(partial.shape, BF16, False), ((8, 128), F32, True)],
        [pltpu.VMEM(partial.shape, BF16), DMA((partial.shape[0] // 512,))],
    )


def back_ends_kernel(near_ref, far_ref, ends_ref, turned_ref, _, __, out_ref, both, sems):
    odd = odd_place()
    copies = []
    for place, (halo_ref, at_end) in enumerate(((near_ref, 1 - odd), (far_ref, odd))):
        back_end(halo_ref, ends_ref, turned_ref, at_end, both.at[place])
        copies.append(pltpu.make_async_copy(both.at[place], end_of(out_ref, at_end), sems.at[place]))
        copies[-1].start()
    for copy in copies:
        copy.wait()


def back_ends(near, far, ends, turned, done, grad_inputs):
    operands = [(o, True) for o in (near, far, ends, turned, done)] + [(grad_inputs, False)]
    (result,) = kernel_call(
        "back_ends", back_ends_kernel, operands, [(grad_inputs.shape, BF16, False)],
        [pltpu.VMEM((2, *near.shape), BF16), DMA((2,))], {5: 0},
    )
    return result


def arrived(arrays):
    return kernel_call(
        "arrived", lambda *refs: None, [(o, True) for o in arrays], [(o.shape, o.dtype, True) for o in arrays],
        aliases={i: i for i in range(len(arrays))},
    )


def exchange(piece, k):
    if k == 0:
        return piece
    return lax.ppermute(piece, "ch", [(i, i ^ k) for i in range(lax.axis_size("ch"))])


def swap(values, first):
    size = lax.axis_size("ctx")
    pairs = [(i, i + 1) for i in range(first, size - 1, 2)]
    return lax.ppermute(values, "ctx", pairs + [(b, a) for a, b in pairs])


def body(inputs, conv_weight, pw_weight, cotangent):
    n = lax.axis_size("ch")
    channels, length = inputs.shape
    halo = DILATION_STEP
    order = [*range(n // 2, n), *range(n // 2 - 1, -1, -1)]
    first, second, rest = order[:n // 4], order[n // 4:n // 2], order[n // 2:]

    weight = jnp.swapaxes(conv_weight, 1, 2)
    if channels % 128 != 0:
        weight = lax.dynamic_slice_in_dim(weight, lax.axis_index("ch") * channels, channels, 2)
    (near,) = kernel_call(
        "near_source", near_source_kernel, [(inputs, False)], [((channels, halo), BF16, True)], [DMA]
    )
    near = swap(near, 0)
    pieces, cot_in = upstream(pw_weight, cotangent, inputs, first, first=True)
    ups = {k: exchange(p, k) for k, p in zip(first, pieces)}
    pieces, far = upstream(pw_weight, cot_in, inputs, second, with_far=True)
    far = swap(far, 1)
    ups.update({k: exchange(p, k) for k, p in zip(second, pieces)})
    (pieces,) = upstream(pw_weight, cot_in, inputs, rest)
    ups.update({k: exchange(p, k) for k, p in zip(rest, pieces)})

    active, slope, wide, plain, turned = interior(inputs, weight, n)
    active, slope, wide = one_end(True, near, plain, active, slope, wide, [ups[first[0]]])
    active, slope, wide = one_end(False, far, plain, active, slope, wide, [])
    ups.update(zip(second, arrived([ups[k] for k in second])))
    grad, near_grad, far_grad = grad_conv(slope, order, ups)
    active = {k: exchange(active[k], k) for k in order}
    near_grad, far_grad = swap(near_grad, 0), swap(far_grad, 1)

    grad_inputs, ends = kernel_call(
        "back_interior", back_interior_kernel, [(grad, True), (turned, True)],
        [((channels, length), BF16, False), ((channels, 2 * halo), F32, True)],
        [pltpu.VMEM((channels, length - 2 * halo), BF16), DMA],
    )
    partial = mix("early_mix", pw_weight, first, active, [])
    (partial,) = mix("half_mix", pw_weight, rest, active, partial)
    mixed, done = late_mix(pw_weight, second, partial, active)
    return mixed, back_ends(near_grad, far_grad, ends, turned, done, grad_inputs)


def solution(mesh):
    placed = (P("ch", "ctx"), P(), P(), P(None, ("ctx", "ch")))
    return jax.shard_map(
        body,
        mesh=mesh,
        in_specs=placed,
        out_specs=(P(None, ("ctx", "ch")), P("ch", "ctx")),
        check_vma=False,
    )
```

```python
import functools

import jax
import jax.numpy as jnp
from jax import lax
from jax.experimental import pallas as pl
from jax.experimental.pallas import tpu as pltpu
from jax.sharding import PartitionSpec as P

DILATION_STEP = 512
UPSTREAM_ROWS = 512
BF16, F32 = jnp.bfloat16, jnp.float32
ANY = pl.BlockSpec(memory_space=pl.ANY)
INSIDE = pl.BlockSpec(memory_space=pltpu.VMEM)
DMA = pltpu.SemaphoreType.DMA


def kernel_call(name, kernel, operands, outs, scratch=(), aliases=None):
    return pl.pallas_call(
        kernel,
        in_specs=[INSIDE if held else ANY for _, held in operands],
        out_specs=[INSIDE if held else ANY for _, _, held in outs],
        out_shape=[
            pltpu.VMEM(shape, kind) if held else jax.ShapeDtypeStruct(shape, kind)
            for shape, kind, held in outs
        ],
        scratch_shapes=list(scratch),
        input_output_aliases=aliases or {},
        compiler_params=pltpu.CompilerParams(vmem_limit_bytes=16 << 20),
        name=name,
    )(*[
        pltpu.with_memory_space_constraint(array, pltpu.VMEM if held else pltpu.HBM)
        for array, held in operands
    ])


def gelu_and_slope(v):
    square = v * v
    inner = v * (0.7978845608 + (0.7978845608 * 0.044715) * square)
    th = jnp.tanh(inner)
    half = 0.5 + 0.5 * th
    active = v * half
    inner_slope = 0.7978845608 + (3.0 * 0.7978845608 * 0.044715) * square
    slope = half + (0.5 * v) * (1.0 - th * th) * inner_slope
    return active, slope


def lanes(start, size):
    return pl.ds(pl.multiple_of(start, 128), size)


def dot(a, b):
    return jnp.dot(a, b, preferred_element_type=F32)


def turned_dot(a, b):
    return lax.dot_general(a, b, (((0,), (0,)), ((), ())), preferred_element_type=F32)


def odd_place():
    return lax.axis_index("ctx") % 2


def end_copy(x_ref, end_ref, at_end, sem):
    length, halo = x_ref.shape[1], end_ref.shape[1]
    return pltpu.make_async_copy(x_ref.at[:, lanes(at_end * (length - halo), halo)], end_ref, sem)


def upstream_kernel(order, channels, first, with_far, pw_ref, cot_ref, x_ref, *rest):
    count = len(order)
    piece_refs, rest = rest[:count], rest[count:]
    columns_ref, total_ref, sems = rest[-3:]
    cot_in = rest[0] if first else cot_ref
    ch = lax.axis_index("ch")
    blocks = []
    for m in range(0, cot_in.shape[0], UPSTREAM_ROWS):
        rows = slice(m, m + UPSTREAM_ROWS)
        pairs = [(cot_ref.at[rows], cot_in.at[rows])] if first else []
        if channels % 128 == 0:
            for place, k in enumerate(order):
                columns = lanes((ch ^ k) * channels, channels)
                held = slice(place * channels, (place + 1) * channels)
                pairs.append((pw_ref.at[rows, columns], columns_ref.at[rows, held]))
        else:
            pairs.append((pw_ref.at[rows], columns_ref.at[rows]))
        copies = [
            pltpu.make_async_copy(source, place, sems.at[len(blocks), i])
            for i, (source, place) in enumerate(pairs)
        ]
        for copy in copies:
            copy.start()
        blocks.append((rows, copies))
    if first or with_far:
        at_end = 1 - odd_place() if first else odd_place()
        end = end_copy(x_ref, rest[-4], at_end, sems.at[0, count + 1])
        end.start()
    for step, (rows, copies) in enumerate(blocks):
        for copy in copies:
            copy.wait()
        for place in range(count):
            held = slice(place * channels, (place + 1) * channels)
            part = turned_dot(columns_ref[rows, held], cot_in[rows, :])
            if step > 0:
                part = part + total_ref[held, :]
            if step < len(blocks) - 1:
                total_ref[held, :] = part
            else:
                piece_refs[place][...] = part.astype(BF16)
    if first or with_far:
        end.wait()


def columns_of(pw_weight, channels, order):
    if channels % 128 == 0:
        return pw_weight
    ch = lax.axis_index("ch")
    return jnp.concatenate(
        [lax.dynamic_slice_in_dim(pw_weight, (ch ^ k) * channels, channels, 1) for k in order], axis=1
    )


def upstream(pw_weight, cotangent, inputs, order, first=False, with_far=False):
    channels = inputs.shape[0]
    total, width = cotangent.shape
    count = len(order)
    outs = [((channels, width), BF16, True)] * count
    outs += [(cotangent.shape, BF16, True)] * first
    outs += [((channels, DILATION_STEP), BF16, True)] * (first or with_far)
    results = kernel_call(
        "upstream", functools.partial(upstream_kernel, order, channels, first, with_far),
        [(columns_of(pw_weight, channels, order), False), (cotangent, not first), (inputs, False)], outs,
        [
            pltpu.VMEM((total, count * channels), BF16), pltpu.VMEM((count * channels, width), F32),
            DMA((total // UPSTREAM_ROWS, count + 2)),
        ],
    )
    return results[:count], *results[count:]


def convolve(w_ref, rows, wide, start, halo, unit):
    return sum(dot(w_ref[t, rows, :], wide[rows, lanes(start + t * halo, unit)]) for t in range(3))


def interior_kernel(n, x_ref, w_ref, *rest):
    active_refs, (slope_ref, wide, plain_ref, turned_ref, own_ref, sem, own_sem) = rest[:n], rest[n:]
    ch = lax.axis_index("ch")
    channels, length = x_ref.shape
    group = w_ref.shape[1]
    own = w_ref.at[:, :, lanes(ch * channels, channels)] if w_ref.shape[2] > channels else w_ref
    own_copy = pltpu.make_async_copy(own, own_ref, own_sem)
    own_copy.start()
    halo = DILATION_STEP
    block = length // n
    unit = min(block, 256)
    copy = pltpu.make_async_copy(x_ref, wide.at[:, halo:halo + length], sem)
    copy.start()
    groups = [slice(g, g + group) for g in range(0, channels, group)]
    own_copy.wait()
    for t in range(3):
        for rows in groups:
            square = own_ref[t, :, rows]
            turned_ref[2 - t, rows, :] = square
            plain_ref[t, rows, :] = square.T
    copy.wait()
    for k in range(n):
        base = (ch ^ k) * block

        @pl.when((base >= halo) & (base < length - halo))
        def _(k=k, base=base):
            for s in range(0, block, unit):
                for rows in groups:
                    active, slope = gelu_and_slope(convolve(plain_ref, rows, wide, base + s, halo, unit))
                    active_refs[k][rows, s:s + unit] = active.astype(BF16)
                    slope_ref[rows, lanes(base + s, unit)] = slope


def interior(inputs, weight, n):
    channels, length = inputs.shape
    group = weight.shape[1]
    block = length // n
    outs = [((channels, block), BF16, True)] * n
    outs += [((channels, length), F32, True), ((channels, length + 2 * DILATION_STEP), BF16, True)]
    outs += [((3, channels, group), BF16, True)] * 2
    results = kernel_call(
        "interior", functools.partial(interior_kernel, n), [(inputs, False), (weight, False)], outs,
        [pltpu.VMEM((3, group, channels), BF16), DMA, DMA],
    )
    return results[:n], *results[n:]


def end_kernel(n, near, waits, *refs):
    halo_ref, plain_ref, rest = refs[waits], refs[waits + 1], refs[-(n + 2):]
    active_refs, (slope_ref, wide) = rest[:n], rest[n:]
    ch, odd = lax.axis_index("ch"), odd_place()
    channels, length = slope_ref.shape
    group = plain_ref.shape[2]
    halo = halo_ref.shape[1]
    block = length // n
    unit = min(block, 256)
    groups = [slice(g, g + group) for g in range(0, channels, group)]
    at_end = 1 - odd if near else odd
    wide[:, lanes(at_end * (halo + length), halo)] = halo_ref[...]
    first = at_end * (length - halo)
    for k in range(n):
        base = (ch ^ k) * block

        @pl.when((base >= first) & (base < first + halo))
        def _(k=k, base=base):
            for s in range(0, block, unit):
                for rows in groups:
                    active, slope = gelu_and_slope(convolve(plain_ref, rows, wide, base + s, halo, unit))
                    active_refs[k][rows, s:s + unit] = active.astype(BF16)
                    slope_ref[rows, lanes(base + s, unit)] = slope


def one_end(near, halo, plain, active, slope, wide, waited):
    n = len(active)
    operands = [(o, True) for o in (*waited, halo, plain, *active, slope, wide)]
    results = kernel_call(
        "near_end" if near else "far_end", functools.partial(end_kernel, n, near, len(waited)), operands,
        [(a.shape, a.dtype, True) for a in (*active, slope, wide)],
        aliases={len(waited) + 2 + i: i for i in range(n + 2)},
    )
    return results[:n], *results[n:]


def grad_kernel(order, slope_ref, *rest):
    up_refs, (grad_ref, near_out, far_out) = rest[:-3], rest[-3:]
    ch, odd = lax.axis_index("ch"), odd_place()
    length, halo = grad_ref.shape[1], near_out.shape[1]
    block = up_refs[0].shape[1]
    step = 32

    @pl.loop(0, grad_ref.shape[0] // step)
    def _(i):
        rows = pl.ds(pl.multiple_of(i * step, step), step)
        for k, up_ref in zip(order, up_refs):
            here = lanes((ch ^ k) * block, block)
            grad_ref[rows, here] = (up_ref[rows, :].astype(F32) * slope_ref[rows, here]).astype(BF16)
        near_out[rows, :] = grad_ref[rows, lanes((1 - odd) * (length - halo), halo)]
        far_out[rows, :] = grad_ref[rows, lanes(odd * (length - halo), halo)]


def grad_conv(slope, order, ups):
    channels = slope.shape[0]
    return kernel_call(
        "grad_conv", functools.partial(grad_kernel, order),
        [(o, True) for o in (slope, *[ups[k] for k in order])],
        [(slope.shape, BF16, True)] + [((channels, DILATION_STEP), BF16, True)] * 2,
    )


def columns_times(order, pw_ref, rows, pieces):
    channels = pieces.shape[0] // len(order)
    if channels % 128 != 0:
        return dot(pw_ref[rows, :], pieces)
    return sum(
        dot(
            pw_ref[rows, lanes((lax.axis_index("ch") ^ k) * channels, channels)],
            pieces[place * channels:(place + 1) * channels],
        )
        for place, k in enumerate(order)
    )


def mix_kernel(order, pw_ref, *rest):
    piece_refs, before, sum_ref = rest[:len(order)], rest[len(order):-1], rest[-1]
    pieces = jnp.concatenate([p[...] for p in piece_refs], axis=0)
    step = 512
    for m in range(0, sum_ref.shape[0], step):
        rows = slice(m, m + step)
        part = columns_times(order, pw_ref, rows, pieces)
        sum_ref[rows, :] = part + before[0][rows, :] if before else part


def mix(name, pw_weight, order, active, before):
    channels, width = active[order[0]].shape
    operands = [columns_of(pw_weight, channels, order), *[active[k] for k in order], *before]
    return kernel_call(
        name, functools.partial(mix_kernel, order), [(o, True) for o in operands],
        [((pw_weight.shape[0], width), F32, True)],
        aliases={len(operands) - 1: 0} if before else {},
    )


def back_interior_kernel(grad_ref, turned_ref, out_ref, ends_ref, held, sem):
    channels, length = grad_ref.shape
    group, halo, unit = turned_ref.shape[2], DILATION_STEP, 256

    def taps(rows, start, which):
        return sum(
            dot(turned_ref[t, rows, :], grad_ref[rows, start + (t - 1) * halo:start + (t - 1) * halo + unit])
            for t in which
        )

    groups = [slice(g, g + group) for g in range(0, channels, group)]
    for rows in groups:
        for s in range(0, length - 2 * halo, unit):
            held[rows, s:s + unit] = taps(rows, halo + s, (0, 1, 2)).astype(BF16)
    copy = pltpu.make_async_copy(held, out_ref.at[:, halo:length - halo], sem)
    copy.start()
    for rows in groups:
        for s in range(0, halo, unit):
            ends_ref[rows, s:s + unit] = taps(rows, s, (1, 2))
            ends_ref[rows, halo + s:halo + s + unit] = taps(rows, length - halo + s, (0, 1))
    copy.wait()


def back_end(halo_ref, ends_ref, turned_ref, at_end, held):
    channels, halo = halo_ref.shape
    group, unit = turned_ref.shape[2], 256
    for g in range(0, channels, group):
        rows = slice(g, g + group)
        for s in range(0, halo, unit):
            outer = dot(turned_ref[2 * at_end, rows, :], halo_ref[rows, s:s + unit])
            held[rows, s:s + unit] = (ends_ref[rows, lanes(at_end * halo + s, unit)] + outer).astype(BF16)


def end_of(out_ref, at_end):
    return out_ref.at[:, lanes(at_end * (out_ref.shape[1] - DILATION_STEP), DILATION_STEP)]


def late_mix_kernel(order, pw_ref, sum_ref, *rest):
    piece_refs, (out_ref, done_ref, held, sems) = rest[:len(order)], rest[len(order):]
    pieces = jnp.concatenate([p[...] for p in piece_refs], axis=0)
    step = 512
    copies = []
    for m in range(0, sum_ref.shape[0], step):
        rows = slice(m, m + step)
        held[rows, :] = (sum_ref[rows, :] + columns_times(order, pw_ref, rows, pieces)).astype(BF16)
        copies.append(pltpu.make_async_copy(held.at[rows, :], out_ref.at[rows, :], sems.at[len(copies)]))
        copies[-1].start()
    done_ref[...] = jnp.zeros_like(done_ref)
    for copy in copies:
        copy.wait()


def late_mix(pw_weight, order, partial, active):
    channels = active[order[0]].shape[0]
    operands = [columns_of(pw_weight, channels, order), partial, *[active[k] for k in order]]
    return kernel_call(
        "late_mix", functools.partial(late_mix_kernel, order), [(o, True) for o in operands],
        [(partial.shape, BF16, False), ((8, 128), F32, True)],
        [pltpu.VMEM(partial.shape, BF16), DMA((partial.shape[0] // 512,))],
    )


def back_ends_kernel(near_ref, far_ref, ends_ref, turned_ref, _, __, out_ref, both, sems):
    odd = odd_place()
    copies = []
    for place, (halo_ref, at_end) in enumerate(((near_ref, 1 - odd), (far_ref, odd))):
        back_end(halo_ref, ends_ref, turned_ref, at_end, both.at[place])
        copies.append(pltpu.make_async_copy(both.at[place], end_of(out_ref, at_end), sems.at[place]))
        copies[-1].start()
    for copy in copies:
        copy.wait()


def back_ends(near, far, ends, turned, done, grad_inputs):
    operands = [(o, True) for o in (near, far, ends, turned, done)] + [(grad_inputs, False)]
    (result,) = kernel_call(
        "back_ends", back_ends_kernel, operands, [(grad_inputs.shape, BF16, False)],
        [pltpu.VMEM((2, *near.shape), BF16), DMA((2,))], {5: 0},
    )
    return result


def arrived(arrays):
    return kernel_call(
        "arrived", lambda *refs: None, [(o, True) for o in arrays], [(o.shape, o.dtype, True) for o in arrays],
        aliases={i: i for i in range(len(arrays))},
    )


def exchange(piece, k):
    if k == 0:
        return piece
    return lax.ppermute(piece, "ch", [(i, i ^ k) for i in range(lax.axis_size("ch"))])


def swap(values, first):
    size = lax.axis_size("ctx")
    pairs = [(i, i + 1) for i in range(first, size - 1, 2)]
    return lax.ppermute(values, "ctx", pairs + [(b, a) for a, b in pairs])


def body(inputs, conv_weight, pw_weight, cotangent):
    n = lax.axis_size("ch")
    channels, length = inputs.shape
    halo = DILATION_STEP
    order = [*range(n // 2, n), *range(n // 2 - 1, -1, -1)]
    first, second, rest = order[:n // 4], order[n // 4:n // 2], order[n // 2:]

    weight = jnp.swapaxes(conv_weight, 1, 2)
    if channels % 128 != 0:
        weight = lax.dynamic_slice_in_dim(weight, lax.axis_index("ch") * channels, channels, 2)
    pieces, cot_in, near = upstream(pw_weight, cotangent, inputs, first, first=True)
    near = swap(near, 0)
    ups = {k: exchange(p, k) for k, p in zip(first, pieces)}
    pieces, far = upstream(pw_weight, cot_in, inputs, second, with_far=True)
    far = swap(far, 1)
    ups.update({k: exchange(p, k) for k, p in zip(second, pieces)})
    (pieces,) = upstream(pw_weight, cot_in, inputs, rest)
    ups.update({k: exchange(p, k) for k, p in zip(rest, pieces)})

    active, slope, wide, plain, turned = interior(inputs, weight, n)
    active, slope, wide = one_end(True, near, plain, active, slope, wide, [ups[first[0]]])
    active, slope, wide = one_end(False, far, plain, active, slope, wide, [])
    ups.update(zip(second, arrived([ups[k] for k in second])))
    grad, near_grad, far_grad = grad_conv(slope, order, ups)
    active = {k: exchange(active[k], k) for k in order}
    near_grad, far_grad = swap(near_grad, 0), swap(far_grad, 1)

    grad_inputs, ends = kernel_call(
        "back_interior", back_interior_kernel, [(grad, True), (turned, True)],
        [((channels, length), BF16, False), ((channels, 2 * halo), F32, True)],
        [pltpu.VMEM((channels, length - 2 * halo), BF16), DMA],
    )
    partial = mix("early_mix", pw_weight, first, active, [])
    (partial,) = mix("half_mix", pw_weight, rest, active, partial)
    mixed, done = late_mix(pw_weight, second, partial, active)
    return mixed, back_ends(near_grad, far_grad, ends, turned, done, grad_inputs)


def solution(mesh):
    placed = (P("ch", "ctx"), P(), P(), P(None, ("ctx", "ch")))
    return jax.shard_map(
        body,
        mesh=mesh,
        in_specs=placed,
        out_specs=(P(None, ("ctx", "ch")), P("ch", "ctx")),
        check_vma=False,
    )
```

```python
import functools

import jax
import jax.numpy as jnp
from jax import lax
from jax.experimental import pallas as pl
from jax.experimental.pallas import tpu as pltpu
from jax.sharding import PartitionSpec as P

DILATION_STEP = 512
UPSTREAM_ROWS = 512
BF16, F32 = jnp.bfloat16, jnp.float32
ANY = pl.BlockSpec(memory_space=pl.ANY)
INSIDE = pl.BlockSpec(memory_space=pltpu.VMEM)
DMA = pltpu.SemaphoreType.DMA


def kernel_call(name, kernel, operands, outs, scratch=(), aliases=None):
    return pl.pallas_call(
        kernel,
        in_specs=[INSIDE if held else ANY for _, held in operands],
        out_specs=[INSIDE if held else ANY for _, _, held in outs],
        out_shape=[
            pltpu.VMEM(shape, kind) if held else jax.ShapeDtypeStruct(shape, kind)
            for shape, kind, held in outs
        ],
        scratch_shapes=list(scratch),
        input_output_aliases=aliases or {},
        compiler_params=pltpu.CompilerParams(vmem_limit_bytes=16 << 20),
        name=name,
    )(*[
        pltpu.with_memory_space_constraint(array, pltpu.VMEM if held else pltpu.HBM)
        for array, held in operands
    ])


def gelu_and_slope(v):
    square = v * v
    inner = v * (0.7978845608 + (0.7978845608 * 0.044715) * square)
    th = jnp.tanh(inner)
    half = 0.5 + 0.5 * th
    active = v * half
    inner_slope = 0.7978845608 + (3.0 * 0.7978845608 * 0.044715) * square
    slope = half + (0.5 * v) * (1.0 - th * th) * inner_slope
    return active, slope


def lanes(start, size):
    return pl.ds(pl.multiple_of(start, 128), size)


def dot(a, b):
    return jnp.dot(a, b, preferred_element_type=F32)


def turned_dot(a, b):
    return lax.dot_general(a, b, (((0,), (0,)), ((), ())), preferred_element_type=F32)


def odd_place():
    return lax.axis_index("ctx") % 2


def end_copy(x_ref, end_ref, at_end, sem):
    length, halo = x_ref.shape[1], end_ref.shape[1]
    return pltpu.make_async_copy(x_ref.at[:, lanes(at_end * (length - halo), halo)], end_ref, sem)


def upstream_kernel(order, channels, first, with_far, pw_ref, cot_ref, x_ref, *rest):
    count = len(order)
    piece_refs, rest = rest[:count], rest[count:]
    columns_ref, total_ref, sems = rest[-3:]
    cot_in = rest[0] if first else cot_ref
    ch = lax.axis_index("ch")
    blocks = []
    for m in range(0, cot_in.shape[0], UPSTREAM_ROWS):
        rows = slice(m, m + UPSTREAM_ROWS)
        pairs = [(cot_ref.at[rows], cot_in.at[rows])] if first else []
        if channels % 128 == 0:
            for place, k in enumerate(order):
                columns = lanes((ch ^ k) * channels, channels)
                held = slice(place * channels, (place + 1) * channels)
                pairs.append((pw_ref.at[rows, columns], columns_ref.at[rows, held]))
        else:
            pairs.append((pw_ref.at[rows], columns_ref.at[rows]))
        copies = [
            pltpu.make_async_copy(source, place, sems.at[len(blocks), i])
            for i, (source, place) in enumerate(pairs)
        ]
        for copy in copies:
            copy.start()
        blocks.append((rows, copies))
    if first or with_far:
        at_end = 1 - odd_place() if first else odd_place()
        end = end_copy(x_ref, rest[-4], at_end, sems.at[0, count + 1])
        end.start()
    for step, (rows, copies) in enumerate(blocks):
        for copy in copies:
            copy.wait()
        for place in range(count):
            held = slice(place * channels, (place + 1) * channels)
            part = turned_dot(columns_ref[rows, held], cot_in[rows, :])
            if step > 0:
                part = part + total_ref[held, :]
            if step < len(blocks) - 1:
                total_ref[held, :] = part
            else:
                piece_refs[place][...] = part.astype(BF16)
    if first or with_far:
        end.wait()


def columns_of(pw_weight, channels, order):
    if channels % 128 == 0:
        return pw_weight
    ch = lax.axis_index("ch")
    return jnp.concatenate(
        [lax.dynamic_slice_in_dim(pw_weight, (ch ^ k) * channels, channels, 1) for k in order], axis=1
    )


def upstream(pw_weight, cotangent, inputs, order, first=False, with_far=False):
    channels = inputs.shape[0]
    total, width = cotangent.shape
    count = len(order)
    outs = [((channels, width), BF16, True)] * count
    outs += [(cotangent.shape, BF16, True)] * first
    outs += [((channels, DILATION_STEP), BF16, True)] * (first or with_far)
    results = kernel_call(
        "upstream", functools.partial(upstream_kernel, order, channels, first, with_far),
        [(columns_of(pw_weight, channels, order), False), (cotangent, not first), (inputs, False)], outs,
        [
            pltpu.VMEM((total, count * channels), BF16), pltpu.VMEM((count * channels, width), F32),
            DMA((total // UPSTREAM_ROWS, count + 2)),
        ],
    )
    return results[:count], *results[count:]


def convolve(w_ref, rows, wide, start, halo, unit):
    return sum(dot(w_ref[t, rows, :], wide[rows, lanes(start + t * halo, unit)]) for t in range(3))


def interior_kernel(n, x_ref, w_ref, *rest):
    active_refs, (slope_ref, wide, plain_ref, turned_ref, own_ref, sem, own_sem) = rest[:n], rest[n:]
    ch = lax.axis_index("ch")
    channels, length = x_ref.shape
    group = w_ref.shape[1]
    own = w_ref.at[:, :, lanes(ch * channels, channels)] if w_ref.shape[2] > channels else w_ref
    own_copy = pltpu.make_async_copy(own, own_ref, own_sem)
    own_copy.start()
    halo = DILATION_STEP
    block = length // n
    unit = min(block, 256)
    copy = pltpu.make_async_copy(x_ref, wide.at[:, halo:halo + length], sem)
    copy.start()
    groups = [slice(g, g + group) for g in range(0, channels, group)]
    own_copy.wait()
    for t in range(3):
        for rows in groups:
            square = own_ref[t, :, rows]
            turned_ref[2 - t, rows, :] = square
            plain_ref[t, rows, :] = square.T
    copy.wait()
    for k in range(n):
        base = (ch ^ k) * block

        @pl.when((base >= halo) & (base < length - halo))
        def _(k=k, base=base):
            for s in range(0, block, unit):
                for rows in groups:
                    active, slope = gelu_and_slope(convolve(plain_ref, rows, wide, base + s, halo, unit))
                    active_refs[k][rows, s:s + unit] = active.astype(BF16)
                    slope_ref[rows, lanes(base + s, unit)] = slope


def interior(inputs, weight, n):
    channels, length = inputs.shape
    group = weight.shape[1]
    block = length // n
    outs = [((channels, block), BF16, True)] * n
    outs += [((channels, length), F32, True), ((channels, length + 2 * DILATION_STEP), BF16, True)]
    outs += [((3, channels, group), BF16, True)] * 2
    results = kernel_call(
        "interior", functools.partial(interior_kernel, n), [(inputs, False), (weight, False)], outs,
        [pltpu.VMEM((3, group, channels), BF16), DMA, DMA],
    )
    return results[:n], *results[n:]


def end_kernel(n, near, waits, *refs):
    halo_ref, plain_ref, rest = refs[0], refs[waits + 1], refs[-(n + 2):]
    active_refs, (slope_ref, wide) = rest[:n], rest[n:]
    ch, odd = lax.axis_index("ch"), odd_place()
    channels, length = slope_ref.shape
    group = plain_ref.shape[2]
    halo = halo_ref.shape[1]
    block = length // n
    unit = min(block, 256)
    groups = [slice(g, g + group) for g in range(0, channels, group)]
    at_end = 1 - odd if near else odd
    wide[:, lanes(at_end * (halo + length), halo)] = halo_ref[...]
    first = at_end * (length - halo)
    for k in range(n):
        base = (ch ^ k) * block

        @pl.when((base >= first) & (base < first + halo))
        def _(k=k, base=base):
            for s in range(0, block, unit):
                for rows in groups:
                    active, slope = gelu_and_slope(convolve(plain_ref, rows, wide, base + s, halo, unit))
                    active_refs[k][rows, s:s + unit] = active.astype(BF16)
                    slope_ref[rows, lanes(base + s, unit)] = slope


def one_end(near, halo, plain, active, slope, wide, waited):
    n = len(active)
    operands = [(o, True) for o in (halo, *waited, plain, *active, slope, wide)]
    results = kernel_call(
        "near_end" if near else "far_end", functools.partial(end_kernel, n, near, len(waited)), operands,
        [(a.shape, a.dtype, True) for a in (*active, slope, wide)],
        aliases={len(waited) + 2 + i: i for i in range(n + 2)},
    )
    return results[:n], *results[n:]


def grad_kernel(order, slope_ref, *rest):
    up_refs, (grad_ref, near_out, far_out) = rest[:-3], rest[-3:]
    ch, odd = lax.axis_index("ch"), odd_place()
    length, halo = grad_ref.shape[1], near_out.shape[1]
    block = up_refs[0].shape[1]
    step = 32

    @pl.loop(0, grad_ref.shape[0] // step)
    def _(i):
        rows = pl.ds(pl.multiple_of(i * step, step), step)
        for k, up_ref in zip(order, up_refs):
            here = lanes((ch ^ k) * block, block)
            grad_ref[rows, here] = (up_ref[rows, :].astype(F32) * slope_ref[rows, here]).astype(BF16)
        near_out[rows, :] = grad_ref[rows, lanes((1 - odd) * (length - halo), halo)]
        far_out[rows, :] = grad_ref[rows, lanes(odd * (length - halo), halo)]


def grad_conv(slope, order, ups):
    channels = slope.shape[0]
    return kernel_call(
        "grad_conv", functools.partial(grad_kernel, order),
        [(o, True) for o in (slope, *[ups[k] for k in order])],
        [(slope.shape, BF16, True)] + [((channels, DILATION_STEP), BF16, True)] * 2,
    )


def columns_times(order, pw_ref, rows, pieces):
    channels = pieces.shape[0] // len(order)
    if channels % 128 != 0:
        return dot(pw_ref[rows, :], pieces)
    return sum(
        dot(
            pw_ref[rows, lanes((lax.axis_index("ch") ^ k) * channels, channels)],
            pieces[place * channels:(place + 1) * channels],
        )
        for place, k in enumerate(order)
    )


def mix_kernel(order, pw_ref, *rest):
    piece_refs, before, sum_ref = rest[:len(order)], rest[len(order):-1], rest[-1]
    pieces = jnp.concatenate([p[...] for p in piece_refs], axis=0)
    step = 512
    for m in range(0, sum_ref.shape[0], step):
        rows = slice(m, m + step)
        part = columns_times(order, pw_ref, rows, pieces)
        sum_ref[rows, :] = part + before[0][rows, :] if before else part


def mix(name, pw_weight, order, active, before):
    channels, width = active[order[0]].shape
    operands = [columns_of(pw_weight, channels, order), *[active[k] for k in order], *before]
    return kernel_call(
        name, functools.partial(mix_kernel, order), [(o, True) for o in operands],
        [((pw_weight.shape[0], width), F32, True)],
        aliases={len(operands) - 1: 0} if before else {},
    )


def back_interior_kernel(grad_ref, turned_ref, out_ref, ends_ref, held, sem):
    channels, length = grad_ref.shape
    group, halo, unit = turned_ref.shape[2], DILATION_STEP, 256

    def taps(rows, start, which):
        return sum(
            dot(turned_ref[t, rows, :], grad_ref[rows, start + (t - 1) * halo:start + (t - 1) * halo + unit])
            for t in which
        )

    groups = [slice(g, g + group) for g in range(0, channels, group)]
    for rows in groups:
        for s in range(0, length - 2 * halo, unit):
            held[rows, s:s + unit] = taps(rows, halo + s, (0, 1, 2)).astype(BF16)
    copy = pltpu.make_async_copy(held, out_ref.at[:, halo:length - halo], sem)
    copy.start()
    for rows in groups:
        for s in range(0, halo, unit):
            ends_ref[rows, s:s + unit] = taps(rows, s, (1, 2))
            ends_ref[rows, halo + s:halo + s + unit] = taps(rows, length - halo + s, (0, 1))
    copy.wait()


def back_end(halo_ref, ends_ref, turned_ref, at_end, held):
    channels, halo = halo_ref.shape
    group, unit = turned_ref.shape[2], 256
    for g in range(0, channels, group):
        rows = slice(g, g + group)
        for s in range(0, halo, unit):
            outer = dot(turned_ref[2 * at_end, rows, :], halo_ref[rows, s:s + unit])
            held[rows, s:s + unit] = (ends_ref[rows, lanes(at_end * halo + s, unit)] + outer).astype(BF16)


def end_of(out_ref, at_end):
    return out_ref.at[:, lanes(at_end * (out_ref.shape[1] - DILATION_STEP), DILATION_STEP)]


def late_mix_kernel(order, pw_ref, sum_ref, *rest):
    piece_refs, (out_ref, done_ref, held, sems) = rest[:len(order)], rest[len(order):]
    pieces = jnp.concatenate([p[...] for p in piece_refs], axis=0)
    step = 512
    copies = []
    for m in range(0, sum_ref.shape[0], step):
        rows = slice(m, m + step)
        held[rows, :] = (sum_ref[rows, :] + columns_times(order, pw_ref, rows, pieces)).astype(BF16)
        copies.append(pltpu.make_async_copy(held.at[rows, :], out_ref.at[rows, :], sems.at[len(copies)]))
        copies[-1].start()
    done_ref[...] = jnp.zeros_like(done_ref)
    for copy in copies:
        copy.wait()


def late_mix(pw_weight, order, partial, active):
    channels = active[order[0]].shape[0]
    operands = [columns_of(pw_weight, channels, order), partial, *[active[k] for k in order]]
    return kernel_call(
        "late_mix", functools.partial(late_mix_kernel, order), [(o, True) for o in operands],
        [(partial.shape, BF16, False), ((8, 128), F32, True)],
        [pltpu.VMEM(partial.shape, BF16), DMA((partial.shape[0] // 512,))],
    )


def back_ends_kernel(near_ref, far_ref, ends_ref, turned_ref, _, __, out_ref, both, sems):
    odd = odd_place()
    copies = []
    for place, (halo_ref, at_end) in enumerate(((near_ref, 1 - odd), (far_ref, odd))):
        back_end(halo_ref, ends_ref, turned_ref, at_end, both.at[place])
        copies.append(pltpu.make_async_copy(both.at[place], end_of(out_ref, at_end), sems.at[place]))
        copies[-1].start()
    for copy in copies:
        copy.wait()


def back_ends(near, far, ends, turned, done, grad_inputs):
    operands = [(o, True) for o in (near, far, ends, turned, done)] + [(grad_inputs, False)]
    (result,) = kernel_call(
        "back_ends", back_ends_kernel, operands, [(grad_inputs.shape, BF16, False)],
        [pltpu.VMEM((2, *near.shape), BF16), DMA((2,))], {5: 0},
    )
    return result


def arrived(arrays):
    return kernel_call(
        "arrived", lambda *refs: None, [(o, True) for o in arrays], [(o.shape, o.dtype, True) for o in arrays],
        aliases={i: i for i in range(len(arrays))},
    )


def exchange(piece, k):
    if k == 0:
        return piece
    return lax.ppermute(piece, "ch", [(i, i ^ k) for i in range(lax.axis_size("ch"))])


def swap(values, first):
    size = lax.axis_size("ctx")
    pairs = [(i, i + 1) for i in range(first, size - 1, 2)]
    return lax.ppermute(values, "ctx", pairs + [(b, a) for a, b in pairs])


def body(inputs, conv_weight, pw_weight, cotangent):
    n = lax.axis_size("ch")
    channels, length = inputs.shape
    halo = DILATION_STEP
    order = [*range(n // 2, n), *range(n // 2 - 1, -1, -1)]
    first, second, rest = order[:n // 4], order[n // 4:n // 2], order[n // 2:]

    weight = jnp.swapaxes(conv_weight, 1, 2)
    if channels % 128 != 0:
        weight = lax.dynamic_slice_in_dim(weight, lax.axis_index("ch") * channels, channels, 2)
    pieces, cot_in, near = upstream(pw_weight, cotangent, inputs, first, first=True)
    near = swap(near, 0)
    ups = {k: exchange(p, k) for k, p in zip(first, pieces)}
    pieces, far = upstream(pw_weight, cot_in, inputs, second, with_far=True)
    far = swap(far, 1)
    ups.update({k: exchange(p, k) for k, p in zip(second, pieces)})
    (pieces,) = upstream(pw_weight, cot_in, inputs, rest)
    ups.update({k: exchange(p, k) for k, p in zip(rest, pieces)})

    active, slope, wide, plain, turned = interior(inputs, weight, n)
    active, slope, wide = one_end(True, near, plain, active, slope, wide, [ups[first[0]]])
    active, slope, wide = one_end(False, far, plain, active, slope, wide, [])
    ups.update(zip(second, arrived([ups[k] for k in second])))
    grad, near_grad, far_grad = grad_conv(slope, order, ups)
    active = {k: exchange(active[k], k) for k in order}
    near_grad, far_grad = swap(near_grad, 0), swap(far_grad, 1)

    grad_inputs, ends = kernel_call(
        "back_interior", back_interior_kernel, [(grad, True), (turned, True)],
        [((channels, length), BF16, False), ((channels, 2 * halo), F32, True)],
        [pltpu.VMEM((channels, length - 2 * halo), BF16), DMA],
    )
    partial = mix("early_mix", pw_weight, first, active, [])
    (partial,) = mix("half_mix", pw_weight, rest, active, partial)
    mixed, done = late_mix(pw_weight, second, partial, active)
    return mixed, back_ends(near_grad, far_grad, ends, turned, done, grad_inputs)


def solution(mesh):
    placed = (P("ch", "ctx"), P(), P(), P(None, ("ctx", "ch")))
    return jax.shard_map(
        body,
        mesh=mesh,
        in_specs=placed,
        out_specs=(P(None, ("ctx", "ch")), P("ch", "ctx")),
        check_vma=False,
    )
```
